256 devices in a mesh: rows: 128 (over x_lo, z, y, core), img: 2 (over x_hi).
Axes of the slice: x: 4 (x_hi: 2, x_lo: 2; x = x_hi * 2 + x_lo), y: 4, z: 8, core: 2. Of those that a mesh axis runs over, the one named last changes fastest.
Arguments:
- local_maps: bfloat16 [2, 1024, 1024, 128], P('img', 'rows'), may hold values from -6 to 6
- global_maps: bfloat16 [2, 1024, 1024, 128], P('img', 'rows'), may hold values from -6 to 6
- conv_weight: bfloat16 [3, 3, 128, 128], replicated, may hold values from -0.1875 to 0.1875
- in_weight: bfloat16 [128, 64], replicated, may hold values from -0.5 to 0.5
- mix_weight: bfloat16 [128, 128], replicated, may hold values from -0.5 to 0.5
- out_weight: bfloat16 [64, 128], replicated, may hold values from -0.75 to 0.75
- out_cotangent: bfloat16 [2, 1024, 1024, 128], P('img', 'rows'), may hold values from -0.0234375 to 0.0234375
Outputs:
- local_out: bfloat16 [2, 1024, 1024, 128], P('img', 'rows')
- global_out: bfloat16 [2, 1024, 1024, 128], P('img', 'rows')
- mix_grad: float32 [128, 128], P(None, 'rows')
- out_grad: float32 [64, 128], P(None, 'rows')
The draws below stay inside these ranges and needn't reach their ends.
All inputs are finite; a program needn't handle non-finite values.
Results may differ from the reference program's by a relative error of at most 0.017.
Values may be sent and summed in bfloat16 or wider, within the bound.
No kernel may reach another device: no remote copies, remote signals or barrier semaphores. Data moves between devices by JAX's collectives and lax.ppermute only.
A program may use at most 128 MiB of HBM per device.

```python
import math
import jax
import jax.numpy as jnp
from jax import lax

HEIGHT = 1024
WIDTH = 1024
LOCAL_CH = 128
GLOBAL_CH = 128
SPEC_CH = 64
FREQS = 512
MONTAGES = 2


def strengthened(array, key, source, target, blocks, factor):
    def block_of(position):
        return (jnp.arange(array.shape[position]) // (array.shape[position] // blocks)).reshape((-1,) + (1,) * (array.ndim - 1 - position))

    near = jax.random.permutation(key, blocks)[block_of(target)]
    far = (block_of(target) + blocks // 2) % blocks
    return jnp.where((block_of(source) == near) | (block_of(source) == far), factor * array, array)


def block_scale(rng, dims, shards, smallest, largest):
    loudness, own = 1.0, jax.random.fold_in(rng, 6)
    for position, blocks in shards:
        steps = jnp.exp(jax.random.uniform(jax.random.fold_in(own, position), (blocks,), jnp.float32, smallest / len(shards), largest / len(shards)))
        loudness = loudness * jnp.repeat(steps, dims[position] // blocks).reshape([-1 if axis == position else 1 for axis in range(len(dims))])
    return loudness


def normal_values(key, shape, spread, bound, cuts=(), kind=jnp.bfloat16):
    factor_of = block_scale(key, shape, cuts, -0.22, 0.18) if cuts else 1.0
    drawn = jax.random.normal(key, shape, jnp.float32) * spread * factor_of
    return jnp.minimum(jnp.maximum(drawn, -bound), bound).astype(kind)


def heavy_noise(own_key, extent, spread, most, split, heavy, kind=jnp.bfloat16):
    values = spread * jax.random.normal(own_key, extent, jnp.float32)
    if split:
        values = values * block_scale(own_key, extent, split, -0.22, 0.18)
    return jnp.clip(strengthened(values, jax.random.fold_in(own_key, 3), *heavy), -most, most).astype(kind)


def setup_inputs(seed: int = 0) -> dict:
    arg_keys = jax.random.split(jax.random.key(seed), 8)
    local_maps = normal_values(arg_keys[0], (MONTAGES, HEIGHT, WIDTH, LOCAL_CH), 1.0, 6.0, ((0, 2), (1, 128)))
    global_maps = normal_values(arg_keys[1], (MONTAGES, HEIGHT, WIDTH, GLOBAL_CH), 1.0, 6.0, ((0, 2), (1, 128)))
    conv_weight = normal_values(arg_keys[2], (3, 3, LOCAL_CH, LOCAL_CH), (9 * LOCAL_CH) ** -0.5, 0.1875)
    in_weight = normal_values(arg_keys[3], (GLOBAL_CH, SPEC_CH), GLOBAL_CH ** -0.5, 0.5)
    mix_weight = normal_values(arg_keys[4], (2 * SPEC_CH, 2 * SPEC_CH), (2 * SPEC_CH) ** -0.5, 0.5)
    out_weight = normal_values(arg_keys[5], (SPEC_CH, GLOBAL_CH), SPEC_CH ** -0.5, 0.75)
    out_cotangent = heavy_noise(arg_keys[6], (MONTAGES, HEIGHT, WIDTH, GLOBAL_CH), 0.001, 0.0234375, ((0, 2), (1, 128)), (1, 3, 128, 5.5))
    return dict(local_maps=local_maps, global_maps=global_maps, conv_weight=conv_weight, in_weight=in_weight, mix_weight=mix_weight, out_weight=out_weight, out_cotangent=out_cotangent)


def row_tables():
    cols = jnp.arange(WIDTH, dtype=jnp.int32)
    freq = jnp.arange(FREQS, dtype=jnp.int32)
    phase = (cols[:, None] * freq[None, :] % WIDTH).astype(jnp.float32) * (2.0 * math.pi / WIDTH)
    cosine = jnp.cos(phase) / math.sqrt(WIDTH)
    sine = jnp.sin(phase) / math.sqrt(WIDTH)
    forward = jnp.stack([cosine, -sine], axis=2).reshape(WIDTH, 2 * FREQS)
    factor = jnp.where(freq == 0, 1.0, 2.0).astype(jnp.float32)
    inverse = jnp.stack([cosine * factor, -sine * factor], axis=2).reshape(WIDTH, 2 * FREQS).T
    return (forward.astype(jnp.bfloat16), inverse.astype(jnp.bfloat16))

def column_table():
    rows_idx = jnp.arange(HEIGHT, dtype=jnp.int32)
    phase = (rows_idx[:, None] * rows_idx[None, :] % HEIGHT).astype(jnp.float32) * (2.0 * math.pi / HEIGHT)
    both = jnp.concatenate([jnp.cos(phase), jnp.sin(phase)], axis=0) / math.sqrt(HEIGHT)
    return both.astype(jnp.bfloat16)

def forward_columns(block, column):
    prod = jnp.dot(column, block.reshape(block.shape[0], -1), preferred_element_type=jnp.float32)
    prod = prod.reshape((2,) + block.shape)
    half = block.shape[-1] // 2
    real = prod[0][..., :half] + prod[1][..., half:]
    imag = prod[0][..., half:] - prod[1][..., :half]
    return jnp.concatenate([real, imag], axis=-1)

def inverse_columns(block, column):
    prod = jnp.dot(column, block.reshape(block.shape[0], -1), preferred_element_type=jnp.float32)
    prod = prod.reshape((2,) + block.shape)
    half = block.shape[-1] // 2
    real = prod[0][..., :half] - prod[1][..., half:]
    imag = prod[0][..., half:] + prod[1][..., :half]
    return jnp.concatenate([real, imag], axis=-1)

def silu_slope(pre):
    sigma = jax.nn.sigmoid(pre)
    return sigma * (1.0 + pre * (1.0 - sigma))

def reference(local_maps, global_maps, conv_weight, in_weight, mix_weight, out_weight, out_cotangent):
    row_fwd, row_inv = row_tables()
    column = column_table()
    fwd32 = row_fwd.astype(jnp.float32)
    inv32 = row_inv.astype(jnp.float32)

    def one_image(operands):
        local_one, global_one, cot_one = operands
        local_res = lax.conv_general_dilated(local_one[None], conv_weight, (1, 1), ((1, 1), (1, 1)), dimension_numbers=('NHWC', 'HWIO', 'NHWC'), preferred_element_type=jnp.float32)[0].astype(jnp.bfloat16)
        inner = jax.nn.relu(jnp.dot(global_one.reshape(-1, GLOBAL_CH), in_weight, preferred_element_type=jnp.float32)).astype(jnp.bfloat16)
        inner = inner.reshape(HEIGHT, WIDTH, SPEC_CH)
        row_spec = jnp.einsum('wj,hwc->hjc', fwd32, inner.astype(jnp.float32)).astype(jnp.bfloat16)
        row_spec = row_spec.reshape(HEIGHT, FREQS, 2 * SPEC_CH)
        spectrum = forward_columns(row_spec, column).astype(jnp.bfloat16)
        pre = jnp.dot(spectrum.reshape(-1, 2 * SPEC_CH), mix_weight, preferred_element_type=jnp.float32)
        pre = pre.reshape(HEIGHT, FREQS, 2 * SPEC_CH)
        mixed = jax.nn.silu(pre).astype(jnp.bfloat16)
        back_spec = inverse_columns(mixed, column).astype(jnp.bfloat16).reshape(HEIGHT, 2 * FREQS, SPEC_CH)
        spatial = jnp.einsum('jw,hjc->hwc', inv32, back_spec.astype(jnp.float32))
        summed = (inner.astype(jnp.float32) + spatial).astype(jnp.bfloat16)
        global_res = jnp.dot(summed.reshape(-1, SPEC_CH), out_weight, preferred_element_type=jnp.float32).astype(jnp.bfloat16)
        cot_flat = cot_one.reshape(-1, GLOBAL_CH)
        inner_cot = jnp.dot(cot_flat, out_weight.T, preferred_element_type=jnp.float32).astype(jnp.bfloat16)
        inner_cot = inner_cot.reshape(HEIGHT, WIDTH, SPEC_CH)
        back_cot = jnp.einsum('jw,hwc->hjc', inv32, inner_cot.astype(jnp.float32)).astype(jnp.bfloat16)
        back_cot = back_cot.reshape(HEIGHT, FREQS, 2 * SPEC_CH)
        mixed_cot = forward_columns(back_cot, column)
        pre_cot = (mixed_cot * silu_slope(pre)).astype(jnp.bfloat16)
        mix_part = jnp.dot(spectrum.reshape(-1, 2 * SPEC_CH).T, pre_cot.reshape(-1, 2 * SPEC_CH), preferred_element_type=jnp.float32)
        out_part = jnp.dot(summed.reshape(-1, SPEC_CH).T, cot_flat, preferred_element_type=jnp.float32)
        return (local_res, global_res.reshape(HEIGHT, WIDTH, GLOBAL_CH), mix_part, out_part)
    local_out, global_out, mix_parts, out_parts = lax.map(one_image, (local_maps, global_maps, out_cotangent))
    return (local_out, global_out, lax.optimization_barrier(jnp.sum(mix_parts, axis=0)), lax.optimization_barrier(jnp.sum(out_parts, axis=0)))
```

```python
import math

import jax
import jax.numpy as jnp
import ml_dtypes
import numpy as np
from jax import lax
from jax.experimental import pallas as pl
from jax.experimental.pallas import tpu as pltpu
from jax.sharding import PartitionSpec as P

HEIGHT = 1024
WIDTH = 1024
SPEC_CH = 64
FREQS = 512
ROWS = 8
GROUPS = 128
PER_GROUP = 4
PAIR = 128
BF16 = jnp.bfloat16
F32 = jnp.float32
LIMIT = 56 * 1024 * 1024


def params():
    return pltpu.CompilerParams(vmem_limit_bytes=LIMIT)


def cost(flops, nbytes):
    return pl.CostEstimate(flops=flops, bytes_accessed=nbytes, transcendentals=0)


def row_tables():
    cols = np.arange(WIDTH)
    freq = np.arange(FREQS)
    phase = ((cols[:, None] * freq[None, :]) % WIDTH) * (2.0 * math.pi / WIDTH)
    forward = np.stack([np.cos(phase), -np.sin(phase)], axis=1) / math.sqrt(WIDTH)
    forward = forward.reshape(WIDTH, 2, GROUPS, PER_GROUP).transpose(0, 2, 1, 3)
    factor = np.where(freq == 0, 1.0, 2.0).reshape(1, GROUPS, 1, PER_GROUP)
    inverse = (forward * factor).reshape(WIDTH, 2 * FREQS)
    forward = np.ascontiguousarray(forward.reshape(WIDTH, 2 * FREQS).T)
    return forward.astype(ml_dtypes.bfloat16), inverse.astype(ml_dtypes.bfloat16)


def column_tables():
    idx = np.arange(GROUPS)
    phase = ((idx[:, None] * idx[None, :]) % GROUPS) * (2.0 * math.pi / GROUPS)
    cosine, sine = np.cos(phase) / math.sqrt(HEIGHT), np.sin(phase) / math.sqrt(HEIGHT)
    forward = np.block([[cosine, sine], [-sine, cosine]])
    backward = np.block([[cosine, -sine], [sine, cosine]])
    turn = (idx[:, None] * np.arange(ROWS)[None, :]) * (2.0 * math.pi / HEIGHT)
    twiddle = np.repeat(np.stack([np.cos(turn), np.sin(turn)]), SPEC_CH, axis=2)
    return (
        forward.astype(ml_dtypes.bfloat16),
        backward.astype(ml_dtypes.bfloat16),
        twiddle.astype(np.float32),
    )


def dot(a, b):
    return jnp.dot(a, b, preferred_element_type=F32)


def dot_t(a, b):
    return lax.dot_general(a, b, (((0,), (0,)), ((), ())), preferred_element_type=F32)


def iota(shape, dim):
    return lax.broadcasted_iota(jnp.int32, shape, dim)


def first_half():
    return jnp.where(iota((SPEC_CH, PAIR), 0) == iota((SPEC_CH, PAIR), 1), 1.0, 0.0).astype(BF16)


def second_half():
    hit = iota((SPEC_CH, PAIR), 0) + SPEC_CH == iota((SPEC_CH, PAIR), 1)
    return jnp.where(hit, 1.0, 0.0).astype(BF16)


def rows_kernel(maps, cot, in_w, out_w, table, spec_out, inner_out, both, in_pair, out_pair):
    step = pl.program_id(0)
    half = ROWS * SPEC_CH

    @pl.when(step == 0)
    def _():
        a, b = first_half(), second_half()
        in_pair[0:PAIR, :] = dot(in_w[...], a).astype(BF16)
        in_pair[PAIR:, :] = dot(in_w[...], b).astype(BF16)
        out_pair[0:PAIR, :] = dot_t(out_w[...], a).astype(BF16)
        out_pair[PAIR:, :] = dot_t(out_w[...], b).astype(BF16)

    @pl.when(step < 4)
    def _():
        start = pl.multiple_of(step * PAIR, PAIR)
        pair = jnp.concatenate([maps[0, 0], maps[0, 1]], axis=1)
        inner = jnp.maximum(dot(pair, in_pair[...]), 0.0).astype(BF16)
        both[:, pl.ds(start, PAIR)] = inner
        inner_out[:, pl.ds(start, PAIR)] = inner
        pair = jnp.concatenate([cot[0, 0], cot[0, 1]], axis=1)
        start = pl.multiple_of(half + step * PAIR, PAIR)
        both[:, pl.ds(start, PAIR)] = dot(pair, out_pair[...]).astype(BF16)

    @pl.when(step >= 4)
    def _():
        prod = dot(table[...], both[...])
        row = (step - 4) * 256 + iota((256, half), 0)
        factor = jnp.where((row == 0) | (row == PER_GROUP), 1.0, 2.0)
        spec_out[:, 0:half] = prod[:, 0:half].astype(BF16)
        spec_out[:, half:] = (prod[:, half:] * factor).astype(BF16)


def rows_forward(maps, cot, in_w, out_w, table):
    def block(i):
        return (0, jnp.minimum(i, 3), 0, 0)

    def late(i):
        return (jnp.maximum(i - 4, 0), 0)

    def whole(i):
        return (0, 0)

    return pl.pallas_call(
        rows_kernel,
        grid=(8,),
        in_specs=[
            pl.BlockSpec((1, 2, WIDTH, 128), block),
            pl.BlockSpec((1, 2, WIDTH, 128), block),
            pl.BlockSpec((128, SPEC_CH), whole),
            pl.BlockSpec((SPEC_CH, 128), whole),
            pl.BlockSpec((256, WIDTH), late),
        ],
        out_specs=[pl.BlockSpec((256, 1024), late), pl.BlockSpec((WIDTH, 512), whole)],
        out_shape=[
            jax.ShapeDtypeStruct((1024, 1024), BF16),
            jax.ShapeDtypeStruct((WIDTH, 512), BF16),
        ],
        scratch_shapes=[
            pltpu.VMEM((WIDTH, 1024), BF16),
            pltpu.VMEM((256, PAIR), BF16),
            pltpu.VMEM((256, PAIR), BF16),
        ],
        compiler_params=params(),
        cost_estimate=cost(5 * 10**9, 11 * 2**20),
    )(maps, cot, in_w, out_w, table)


ROOT = math.sqrt(0.5)


def lane_signs(shape):
    return jnp.where(iota(shape, 1) % PAIR < SPEC_CH, 1.0, -1.0).astype(F32)


def lane_butterfly(x, signs):
    return pltpu.roll(x, SPEC_CH, 1) + x * signs


def turn_second(re, im, first, real, imag):
    new_re = jnp.where(first, re, re * real - im * imag)
    new_im = jnp.where(first, im, re * imag + im * real)
    return new_re, new_im


EIGHTHS = ((1.0, 0.0), (ROOT, -ROOT), (0.0, -1.0), (-ROOT, -ROOT))


def spectrum_rows(prod, twiddle, rows, signs, first):
    re, im = [], []
    for m in range(4):
        lanes = slice(m * PAIR, (m + 1) * PAIR)
        a = prod[pl.ds(rows, RB), lanes]
        b = prod[pl.ds(GROUPS + rows, RB), lanes]
        c = twiddle[0, pl.ds(rows, RB), lanes]
        s = twiddle[1, pl.ds(rows, RB), lanes]
        re.append(a * c + b * s)
        im.append(b * c - a * s)
    s0r, s0i, d0r, d0i = re[0] + re[2], im[0] + im[2], re[0] - re[2], im[0] - im[2]
    s1r, s1i, d1r, d1i = re[1] + re[3], im[1] + im[3], re[1] - re[3], im[1] - im[3]
    four = (
        (s0r + s1r, s0i + s1i),
        (d0r + d1i, d0i - d1r),
        (s0r - s1r, s0i - s1i),
        (d0r - d1i, d0i + d1r),
    )
    out = []
    for q in range(4):
        zr, zi = four[q]
        if q:
            zr, zi = turn_second(zr, zi, first, *EIGHTHS[q])
        out.append((lane_butterfly(zr, signs), lane_butterfly(zi, signs)))
    return out


def inverse_rows(parts, twiddle, rows, signs, first):
    z = []
    for q in range(4):
        zr, zi = (lane_butterfly(x, signs) for x in parts[q])
        if q:
            zr, zi = turn_second(zr, zi, first, EIGHTHS[q][0], -EIGHTHS[q][1])
        z.append((zr, zi))
    s0r, s0i = z[0][0] + z[2][0], z[0][1] + z[2][1]
    d0r, d0i = z[0][0] - z[2][0], z[0][1] - z[2][1]
    s1r, s1i = z[1][0] + z[3][0], z[1][1] + z[3][1]
    d1r, d1i = z[1][0] - z[3][0], z[1][1] - z[3][1]
    four = (
        (s0r + s1r, s0i + s1i),
        (d0r - d1i, d0i + d1r),
        (s0r - s1r, s0i - s1i),
        (d0r + d1i, d0i - d1r),
    )
    out = []
    for m in range(4):
        lanes = slice(m * PAIR, (m + 1) * PAIR)
        c = twiddle[0, pl.ds(rows, RB), lanes]
        s = twiddle[1, pl.ds(rows, RB), lanes]
        a, b = four[m]
        out.append((a * c - b * s, b * c + a * s))
    return out


RB = 16


def fill_mix(mix_w, wide):
    total = jnp.zeros((256, 256), F32)
    for t in range(2):
        row, col = iota((256, 128), 0), iota((256, 128), 1)
        at = (row // PAIR) * SPEC_CH + row % SPEC_CH
        hit = (at == col) & (row // SPEC_CH % 2 == t)
        pick = jnp.where(hit, 1.0, 0.0).astype(BF16)
        left = dot(pick, mix_w[...]).astype(BF16)
        total = total + lax.dot_general(
            left, pick, (((1,), (1,)), ((), ())), preferred_element_type=F32
        )
    wide[...] = total.astype(BF16)


def sigmoid(x):
    return 1.0 / (1.0 + jnp.exp(-x))


def gather_parts(stage, kk):
    lanes = []
    for m in range(4):
        re = stage[m, pl.ds(kk, GROUPS, stride=ROWS), :]
        im = stage[m, pl.ds(PER_GROUP + kk, GROUPS, stride=ROWS), :]
        lanes.append(jnp.concatenate([re, im], axis=0).astype(BF16))
    return jnp.concatenate(lanes, axis=1)


def fill_stage(block, stage):
    for m in range(4):
        stage[m] = block[:, m * PAIR : (m + 1) * PAIR].astype(F32)


def columns_kernel(block, forward, backward, twiddle, mix_w, spec, back, stage, wide, prod, pre, inv):
    fill_mix(mix_w, wide)
    fill_stage(block, stage)
    signs = lane_signs((RB, PAIR))
    first = iota((RB, PAIR), 1) < SPEC_CH
    for kk in range(PER_GROUP):
        prod[...] = dot(forward[...], gather_parts(stage, kk))

        @pl.loop(0, GROUPS, step=RB)
        def _(rows):
            rows = pl.multiple_of(rows, RB)
            parts = spectrum_rows(prod, twiddle, rows, signs, first)
            for q in range(4):
                spec[kk * 4 + q, pl.ds(rows, RB), 0:PAIR] = parts[q][0].astype(BF16)
                spec[kk * 4 + q, pl.ds(rows, RB), PAIR:] = parts[q][1].astype(BF16)

        pre[...] = dot(spec[kk * 4 : kk * 4 + 4].reshape(512, 256), wide[...])

        @pl.loop(0, GROUPS, step=RB)
        def _(rows):
            rows = pl.multiple_of(rows, RB)
            parts = []
            for q in range(4):
                v = pre[pl.ds(q * GROUPS + rows, RB), :]
                v = v * sigmoid(v)
                parts.append((v[:, 0:PAIR], v[:, PAIR:]))
            pairs = inverse_rows(parts, twiddle, rows, signs, first)
            for m in range(4):
                lanes = slice(m * PAIR, (m + 1) * PAIR)
                inv[pl.ds(rows, RB), lanes] = pairs[m][0].astype(BF16)
                inv[pl.ds(GROUPS + rows, RB), lanes] = pairs[m][1].astype(BF16)

        result = dot(backward[...], inv[...])
        for m in range(4):
            lanes = slice(m * PAIR, (m + 1) * PAIR)
            stage[m, pl.ds(kk, GROUPS, stride=ROWS), :] = result[0:GROUPS, lanes]
            stage[m, pl.ds(PER_GROUP + kk, GROUPS, stride=ROWS), :] = result[GROUPS:, lanes]
    for m in range(4):
        back[:, m * PAIR : (m + 1) * PAIR] = stage[m].astype(BF16)


def whole_spec(shape):
    return pl.BlockSpec(shape, lambda *_: (0,) * len(shape))


def columns(block, forward, backward, twiddle, mix_w):
    return pl.pallas_call(
        columns_kernel,
        grid=(1,),
        in_specs=[
            pl.BlockSpec((1024, 512), lambda i: (0, 0)),
            whole_spec((256, 256)),
            whole_spec((256, 256)),
            whole_spec((2, GROUPS, 512)),
            whole_spec((128, 128)),
        ],
        out_specs=[whole_spec((16, GROUPS, 256)), whole_spec((1024, 512))],
        out_shape=[
            jax.ShapeDtypeStruct((16, GROUPS, 256), BF16),
            jax.ShapeDtypeStruct((1024, 512), BF16),
        ],
        scratch_shapes=[
            pltpu.VMEM((4, 1024, PAIR), F32),
            pltpu.VMEM((256, 256), BF16),
            pltpu.VMEM((256, 512), F32),
            pltpu.VMEM((512, 256), F32),
            pltpu.VMEM((256, 512), BF16),
        ],
        compiler_params=params(),
        cost_estimate=cost(8 * 10**9, 5 * 2**20),
    )(block, forward, backward, twiddle, mix_w)


def mix_kernel(block, spec, forward, twiddle, mix_w, grad, stage, wide, prod, pre, slope, acc):
    fill_mix(mix_w, wide)
    fill_stage(block, stage)
    signs = lane_signs((RB, PAIR))
    first = iota((RB, PAIR), 1) < SPEC_CH
    acc[...] = jnp.zeros_like(acc)
    for kk in range(PER_GROUP):
        prod[...] = dot(forward[...], gather_parts(stage, kk))
        pre[...] = dot(spec[kk * 4 : kk * 4 + 4].reshape(512, 256), wide[...])

        @pl.loop(0, GROUPS, step=RB)
        def _(rows):
            rows = pl.multiple_of(rows, RB)
            parts = spectrum_rows(prod, twiddle, rows, signs, first)
            for q in range(4):
                for part in range(2):
                    lanes = slice(part * PAIR, (part + 1) * PAIR)
                    v = pre[pl.ds(q * GROUPS + rows, RB), lanes]
                    s = sigmoid(v)
                    v = parts[q][part] * (s * (1.0 + v * (1.0 - s)))
                    slope[pl.ds(q * GROUPS + rows, RB), lanes] = v.astype(BF16)

        acc[...] += dot_t(slope[...], spec[kk * 4 : kk * 4 + 4].reshape(512, 256))
    lane = iota((SPEC_CH, PAIR), 1) < SPEC_CH
    for part in range(2):
        even = acc[part * PAIR : part * PAIR + SPEC_CH, :]
        odd = acc[part * PAIR + SPEC_CH : (part + 1) * PAIR, :]
        real = even[:, 0:PAIR] + pltpu.roll(odd[:, 0:PAIR], SPEC_CH, 1)
        imag = pltpu.roll(even[:, PAIR:], SPEC_CH, 1) + odd[:, PAIR:]
        grad[part * SPEC_CH : (part + 1) * SPEC_CH, :] = jnp.where(lane, real, imag)


def mix_terms(block, spec, forward, twiddle, mix_w):
    return pl.pallas_call(
        mix_kernel,
        grid=(1,),
        in_specs=[
            pl.BlockSpec((1024, 512), lambda i: (0, 1)),
            whole_spec((16, GROUPS, 256)),
            whole_spec((256, 256)),
            whole_spec((2, GROUPS, 512)),
            whole_spec((128, 128)),
        ],
        out_specs=whole_spec((128, 128)),
        out_shape=jax.ShapeDtypeStruct((128, 128), F32),
        scratch_shapes=[
            pltpu.VMEM((4, 1024, PAIR), F32),
            pltpu.VMEM((256, 256), BF16),
            pltpu.VMEM((256, 512), F32),
            pltpu.VMEM((512, 256), F32),
            pltpu.VMEM((512, 256), BF16),
            pltpu.VMEM((256, 256), F32),
        ],
        compiler_params=params(),
        cost_estimate=cost(6 * 10**9, 5 * 2**20),
    )(block, spec, forward, twiddle, mix_w)


def back_kernel(table, rows, inner, cot, mix_part, summed, terms, acc):
    step = pl.program_id(0)

    @pl.when(step == 0)
    def _():
        acc[...] = jnp.zeros_like(acc)

    total = (dot(table[...], rows[...]) + inner[...].astype(F32)).astype(BF16)
    summed[...] = total
    for p in range(4):
        pair = jnp.concatenate([cot[0, 2 * p], cot[0, 2 * p + 1]], axis=1)
        acc[...] += dot_t(pair, total[:, p * PAIR : (p + 1) * PAIR])

    @pl.when(step == 3)
    def _():
        lane = iota((128, PAIR), 1) < SPEC_CH
        out_part = acc[0:128, :] + pltpu.roll(acc[128:, :], SPEC_CH, 1)
        terms[:, 0:128] = mix_part[...]
        terms[:, 128:] = jnp.where(lane, out_part, 0.0)


def back_rows(table, rows, inner, cot, mix_part):
    return pl.pallas_call(
        back_kernel,
        grid=(4,),
        in_specs=[
            pl.BlockSpec((256, 1024), lambda i: (i, 0)),
            whole_spec((1024, 512)),
            pl.BlockSpec((256, 512), lambda i: (i, 0)),
            pl.BlockSpec((1, ROWS, 256, 128), lambda i: (0, 0, i, 0)),
            whole_spec((128, 128)),
        ],
        out_specs=[pl.BlockSpec((256, 512), lambda i: (i, 0)), whole_spec((128, 256))],
        out_shape=[
            jax.ShapeDtypeStruct((WIDTH, 512), BF16),
            jax.ShapeDtypeStruct((128, 256), F32),
        ],
        scratch_shapes=[pltpu.VMEM((256, 128), F32)],
        compiler_params=params(),
        cost_estimate=cost(2 * 10**9, 8 * 2**20),
    )(table, rows, inner, cot, mix_part)


def out_kernel(summed, out_w, out, wide):
    @pl.when(pl.program_id(0) == 0)
    def _():
        zero = jnp.zeros((SPEC_CH, 128), BF16)
        wide[0:SPEC_CH, :] = jnp.concatenate([out_w[...], zero], axis=1)
        wide[SPEC_CH:, :] = jnp.concatenate([zero, out_w[...]], axis=1)

    for p in range(4):
        prod = dot(summed[:, p * PAIR : (p + 1) * PAIR], wide[...]).astype(BF16)
        out[0, 2 * p] = prod[:, 0:128]
        out[0, 2 * p + 1] = prod[:, 128:]


def project_out(summed, out_w):
    return pl.pallas_call(
        out_kernel,
        grid=(4,),
        in_specs=[pl.BlockSpec((256, 512), lambda i: (i, 0)), whole_spec((SPEC_CH, 128))],
        out_specs=pl.BlockSpec((1, ROWS, 256, 128), lambda i: (0, 0, i, 0)),
        out_shape=jax.ShapeDtypeStruct((1, ROWS, WIDTH, 128), BF16),
        scratch_shapes=[pltpu.VMEM((128, 256), BF16)],
        compiler_params=params(),
        cost_estimate=cost(5 * 10**8, 3 * 2**20),
    )(summed, out_w)


def extended(cells):
    ends = GROUPS - 1
    head, tail = cells[:, 0:1], cells[:, ROWS - 1 :]
    above = lax.ppermute(tail, "rows", [(i, i + 1) for i in range(ends)])
    below = lax.ppermute(head, "rows", [(i + 1, i) for i in range(ends)])
    return jnp.concatenate([above, cells, below], axis=1)


def exchange(block):
    lanes = block.shape[1]
    moved = lax.all_to_all(
        block.reshape(GROUPS, ROWS, lanes), "rows", split_axis=0, concat_axis=0, tiled=True
    )
    return moved.reshape(GROUPS * ROWS, lanes)


def shards(local_maps, global_maps, conv_weight, in_weight, mix_weight, out_weight, out_cotangent):
    row_fwd, row_inv = row_tables()
    forward, backward, twiddle = column_tables()
    spec_rows, inner = rows_forward(global_maps, out_cotangent, in_weight, out_weight, row_fwd)
    spec_cols = exchange(spec_rows)
    padded = extended(local_maps)
    local_out = lax.conv_general_dilated(
        padded,
        conv_weight,
        (1, 1),
        ((0, 0), (1, 1)),
        dimension_numbers=("NHWC", "HWIO", "NHWC"),
        preferred_element_type=F32,
    ).astype(BF16)
    spectrum, back_cols = columns(spec_cols, forward, backward, twiddle, mix_weight)
    back = exchange(back_cols)
    mix_part = mix_terms(spec_cols, spectrum, forward, twiddle, mix_weight)
    summed, terms = back_rows(row_inv, back, inner, out_cotangent, mix_part)
    terms = jnp.broadcast_to(terms.reshape(128, 1, 2, 128), (128, 2, 2, 128)).reshape(256, 2, 128)
    terms = lax.all_to_all(terms, ("rows", "img"), split_axis=0, concat_axis=0, tiled=True)
    global_out = project_out(summed, out_weight)
    total = jnp.sum(terms, axis=0)
    mix_grad = total[0].reshape(128, 1)
    out_grad = total[1, 0:SPEC_CH].reshape(SPEC_CH, 1)
    return (local_out, global_out, mix_grad, out_grad)


def solution(mesh):
    maps = P("img", "rows", None, None)
    in_specs = (maps, maps, P(), P(), P(), P(), maps)
    out_specs = (maps, maps, P(None, "rows"), P(None, "rows"))
    return jax.shard_map(shards, mesh=mesh, in_specs=in_specs, out_specs=out_specs, check_vma=False)
```

```python
import math

import jax
import jax.numpy as jnp
import ml_dtypes
import numpy as np
from jax import lax
from jax.experimental import pallas as pl
from jax.experimental.pallas import tpu as pltpu
from jax.sharding import PartitionSpec as P

HEIGHT = 1024
WIDTH = 1024
SPEC_CH = 64
FREQS = 512
ROWS = 8
GROUPS = 128
PER_GROUP = 4
PAIR = 128
BF16 = jnp.bfloat16
F32 = jnp.float32
LIMIT = 56 * 1024 * 1024


def params():
    return pltpu.CompilerParams(vmem_limit_bytes=LIMIT)


def cost(flops, nbytes):
    return pl.CostEstimate(flops=flops, bytes_accessed=nbytes, transcendentals=0)


def row_tables():
    cols = np.arange(WIDTH)
    freq = np.arange(FREQS)
    phase = ((cols[:, None] * freq[None, :]) % WIDTH) * (2.0 * math.pi / WIDTH)
    forward = np.stack([np.cos(phase), -np.sin(phase)], axis=1) / math.sqrt(WIDTH)
    forward = forward.reshape(WIDTH, 2, GROUPS, PER_GROUP).transpose(0, 2, 1, 3)
    factor = np.where(freq == 0, 1.0, 2.0).reshape(1, GROUPS, 1, PER_GROUP)
    inverse = (forward * factor).reshape(WIDTH, 2 * FREQS)
    forward = np.ascontiguousarray(forward.reshape(WIDTH, 2 * FREQS).T)
    return forward.astype(ml_dtypes.bfloat16), inverse.astype(ml_dtypes.bfloat16)


def column_tables():
    idx = np.arange(GROUPS)
    phase = ((idx[:, None] * idx[None, :]) % GROUPS) * (2.0 * math.pi / GROUPS)
    cosine, sine = np.cos(phase) / math.sqrt(HEIGHT), np.sin(phase) / math.sqrt(HEIGHT)
    forward = np.block([[cosine, sine], [-sine, cosine]])
    backward = np.block([[cosine, -sine], [sine, cosine]])
    turn = (idx[:, None] * np.arange(ROWS)[None, :]) * (2.0 * math.pi / HEIGHT)
    twiddle = np.repeat(np.stack([np.cos(turn), np.sin(turn)]), SPEC_CH, axis=2)
    return (
        forward.astype(ml_dtypes.bfloat16),
        backward.astype(ml_dtypes.bfloat16),
        twiddle.astype(np.float32),
    )


def dot(a, b):
    return jnp.dot(a, b, preferred_element_type=F32)


def dot_t(a, b):
    return lax.dot_general(a, b, (((0,), (0,)), ((), ())), preferred_element_type=F32)


def iota(shape, dim):
    return lax.broadcasted_iota(jnp.int32, shape, dim)


def first_half():
    return jnp.where(iota((SPEC_CH, PAIR), 0) == iota((SPEC_CH, PAIR), 1), 1.0, 0.0).astype(BF16)


def second_half():
    hit = iota((SPEC_CH, PAIR), 0) + SPEC_CH == iota((SPEC_CH, PAIR), 1)
    return jnp.where(hit, 1.0, 0.0).astype(BF16)


def rows_kernel(maps, cot, in_w, out_w, table, spec_out, inner_out, both, in_pair, out_pair):
    step = pl.program_id(0)
    half = ROWS * SPEC_CH

    @pl.when(step == 0)
    def _():
        a, b = first_half(), second_half()
        in_pair[0:PAIR, :] = dot_t(in_w[...], a).astype(BF16)
        in_pair[PAIR:, :] = dot_t(in_w[...], b).astype(BF16)
        out_pair[0:PAIR, :] = dot_t(out_w[...], a).astype(BF16)
        out_pair[PAIR:, :] = dot_t(out_w[...], b).astype(BF16)

    @pl.when(step < 4)
    def _():
        start = pl.multiple_of(step * PAIR, PAIR)
        pair = jnp.concatenate([maps[0, 0], maps[0, 1]], axis=1)
        inner = jnp.maximum(dot(pair, in_pair[...]), 0.0).astype(BF16)
        both[:, pl.ds(start, PAIR)] = inner
        inner_out[:, pl.ds(start, PAIR)] = inner
        pair = jnp.concatenate([cot[0, 0], cot[0, 1]], axis=1)
        start = pl.multiple_of(half + step * PAIR, PAIR)
        both[:, pl.ds(start, PAIR)] = dot(pair, out_pair[...]).astype(BF16)

    @pl.when(step >= 4)
    def _():
        prod = dot(table[...], both[...])
        row = (step - 4) * 256 + iota((256, half), 0)
        factor = jnp.where((row == 0) | (row == PER_GROUP), 1.0, 2.0)
        spec_out[:, 0:half] = prod[:, 0:half].astype(BF16)
        spec_out[:, half:] = (prod[:, half:] * factor).astype(BF16)


def rows_forward(maps, cot, in_w, out_w, table):
    def block(i):
        return (0, jnp.minimum(i, 3), 0, 0)

    def late(i):
        return (jnp.maximum(i - 4, 0), 0)

    def whole(i):
        return (0, 0)

    return pl.pallas_call(
        rows_kernel,
        grid=(8,),
        in_specs=[
            pl.BlockSpec((1, 2, WIDTH, 128), block),
            pl.BlockSpec((1, 2, WIDTH, 128), block),
            pl.BlockSpec((SPEC_CH, 128), whole),
            pl.BlockSpec((SPEC_CH, 128), whole),
            pl.BlockSpec((256, WIDTH), late),
        ],
        out_specs=[pl.BlockSpec((256, 1024), late), pl.BlockSpec((WIDTH, 512), whole)],
        out_shape=[
            jax.ShapeDtypeStruct((1024, 1024), BF16),
            jax.ShapeDtypeStruct((WIDTH, 512), BF16),
        ],
        scratch_shapes=[
            pltpu.VMEM((WIDTH, 1024), BF16),
            pltpu.VMEM((256, PAIR), BF16),
            pltpu.VMEM((256, PAIR), BF16),
        ],
        compiler_params=params(),
        cost_estimate=cost(5 * 10**9, 11 * 2**20),
    )(maps, cot, in_w, out_w, table)


ROOT = math.sqrt(0.5)


def lane_signs(shape):
    return jnp.where(iota(shape, 1) % PAIR < SPEC_CH, 1.0, -1.0).astype(F32)


def lane_butterfly(x, signs):
    return pltpu.roll(x, SPEC_CH, 1) + x * signs


def turn_second(re, im, first, real, imag):
    new_re = jnp.where(first, re, re * real - im * imag)
    new_im = jnp.where(first, im, re * imag + im * real)
    return new_re, new_im


EIGHTHS = ((1.0, 0.0), (ROOT, -ROOT), (0.0, -1.0), (-ROOT, -ROOT))


def spectrum_rows(prod, twiddle, rows, signs, first):
    re, im = [], []
    for m in range(4):
        lanes = slice(m * PAIR, (m + 1) * PAIR)
        a = prod[pl.ds(rows, RB), lanes]
        b = prod[pl.ds(GROUPS + rows, RB), lanes]
        c = twiddle[0, pl.ds(rows, RB), lanes]
        s = twiddle[1, pl.ds(rows, RB), lanes]
        re.append(a * c + b * s)
        im.append(b * c - a * s)
    s0r, s0i, d0r, d0i = re[0] + re[2], im[0] + im[2], re[0] - re[2], im[0] - im[2]
    s1r, s1i, d1r, d1i = re[1] + re[3], im[1] + im[3], re[1] - re[3], im[1] - im[3]
    four = (
        (s0r + s1r, s0i + s1i),
        (d0r + d1i, d0i - d1r),
        (s0r - s1r, s0i - s1i),
        (d0r - d1i, d0i + d1r),
    )
    out = []
    for q in range(4):
        zr, zi = four[q]
        if q:
            zr, zi = turn_second(zr, zi, first, *EIGHTHS[q])
        out.append((lane_butterfly(zr, signs), lane_butterfly(zi, signs)))
    return out


def inverse_rows(parts, twiddle, rows, signs, first):
    z = []
    for q in range(4):
        zr, zi = (lane_butterfly(x, signs) for x in parts[q])
        if q:
            zr, zi = turn_second(zr, zi, first, EIGHTHS[q][0], -EIGHTHS[q][1])
        z.append((zr, zi))
    s0r, s0i = z[0][0] + z[2][0], z[0][1] + z[2][1]
    d0r, d0i = z[0][0] - z[2][0], z[0][1] - z[2][1]
    s1r, s1i = z[1][0] + z[3][0], z[1][1] + z[3][1]
    d1r, d1i = z[1][0] - z[3][0], z[1][1] - z[3][1]
    four = (
        (s0r + s1r, s0i + s1i),
        (d0r - d1i, d0i + d1r),
        (s0r - s1r, s0i - s1i),
        (d0r + d1i, d0i - d1r),
    )
    out = []
    for m in range(4):
        lanes = slice(m * PAIR, (m + 1) * PAIR)
        c = twiddle[0, pl.ds(rows, RB), lanes]
        s = twiddle[1, pl.ds(rows, RB), lanes]
        a, b = four[m]
        out.append((a * c - b * s, b * c + a * s))
    return out


RB = 16


def fill_mix(mix_w, wide):
    total = jnp.zeros((256, 256), F32)
    for t in range(2):
        row, col = iota((256, 128), 0), iota((256, 128), 1)
        at = (row // PAIR) * SPEC_CH + row % SPEC_CH
        hit = (at == col) & (row // SPEC_CH % 2 == t)
        pick = jnp.where(hit, 1.0, 0.0).astype(BF16)
        left = dot(pick, mix_w[...]).astype(BF16)
        total = total + lax.dot_general(
            left, pick, (((1,), (1,)), ((), ())), preferred_element_type=F32
        )
    wide[...] = total.astype(BF16)


def sigmoid(x):
    return 1.0 / (1.0 + jnp.exp(-x))


def gather_parts(stage, kk):
    lanes = []
    for m in range(4):
        re = stage[m, pl.ds(kk, GROUPS, stride=ROWS), :]
        im = stage[m, pl.ds(PER_GROUP + kk, GROUPS, stride=ROWS), :]
        lanes.append(jnp.concatenate([re, im], axis=0).astype(BF16))
    return jnp.concatenate(lanes, axis=1)


def fill_stage(block, stage):
    for m in range(4):
        stage[m] = block[:, m * PAIR : (m + 1) * PAIR].astype(F32)


def columns_kernel(block, forward, backward, twiddle, mix_w, ready, spec, back, stage, wide, prod, pre, inv):
    del ready
    fill_mix(mix_w, wide)
    fill_stage(block, stage)
    signs = lane_signs((RB, PAIR))
    first = iota((RB, PAIR), 1) < SPEC_CH
    for kk in range(PER_GROUP):
        prod[...] = dot(forward[...], gather_parts(stage, kk))

        @pl.loop(0, GROUPS, step=RB)
        def _(rows):
            rows = pl.multiple_of(rows, RB)
            parts = spectrum_rows(prod, twiddle, rows, signs, first)
            for q in range(4):
                spec[kk * 4 + q, pl.ds(rows, RB), 0:PAIR] = parts[q][0].astype(BF16)
                spec[kk * 4 + q, pl.ds(rows, RB), PAIR:] = parts[q][1].astype(BF16)

        pre[...] = dot(spec[kk * 4 : kk * 4 + 4].reshape(512, 256), wide[...])

        @pl.loop(0, GROUPS, step=RB)
        def _(rows):
            rows = pl.multiple_of(rows, RB)
            parts = []
            for q in range(4):
                v = pre[pl.ds(q * GROUPS + rows, RB), :]
                v = v * sigmoid(v)
                parts.append((v[:, 0:PAIR], v[:, PAIR:]))
            pairs = inverse_rows(parts, twiddle, rows, signs, first)
            for m in range(4):
                lanes = slice(m * PAIR, (m + 1) * PAIR)
                inv[pl.ds(rows, RB), lanes] = pairs[m][0].astype(BF16)
                inv[pl.ds(GROUPS + rows, RB), lanes] = pairs[m][1].astype(BF16)

        result = dot(backward[...], inv[...])
        for m in range(4):
            lanes = slice(m * PAIR, (m + 1) * PAIR)
            stage[m, pl.ds(kk, GROUPS, stride=ROWS), :] = result[0:GROUPS, lanes]
            stage[m, pl.ds(PER_GROUP + kk, GROUPS, stride=ROWS), :] = result[GROUPS:, lanes]
    for m in range(4):
        back[:, m * PAIR : (m + 1) * PAIR] = stage[m].astype(BF16)


def whole_spec(shape):
    return pl.BlockSpec(shape, lambda *_: (0,) * len(shape))


def columns(block, forward, backward, twiddle, mix_w, ready):
    return pl.pallas_call(
        columns_kernel,
        grid=(1,),
        in_specs=[
            pl.BlockSpec((1024, 512), lambda i: (0, 0)),
            whole_spec((256, 256)),
            whole_spec((256, 256)),
            whole_spec((2, GROUPS, 512)),
            whole_spec((128, 128)),
            pl.BlockSpec(memory_space=pl.ANY),
        ],
        out_specs=[whole_spec((16, GROUPS, 256)), whole_spec((1024, 512))],
        out_shape=[
            jax.ShapeDtypeStruct((16, GROUPS, 256), BF16),
            jax.ShapeDtypeStruct((1024, 512), BF16),
        ],
        scratch_shapes=[
            pltpu.VMEM((4, 1024, PAIR), F32),
            pltpu.VMEM((256, 256), BF16),
            pltpu.VMEM((256, 512), F32),
            pltpu.VMEM((512, 256), F32),
            pltpu.VMEM((256, 512), BF16),
        ],
        compiler_params=params(),
        cost_estimate=cost(8 * 10**9, 5 * 2**20),
    )(block, forward, backward, twiddle, mix_w, ready)


def mix_kernel(block, spec, forward, twiddle, mix_w, grad, stage, wide, prod, pre, slope, acc):
    fill_mix(mix_w, wide)
    fill_stage(block, stage)
    signs = lane_signs((RB, PAIR))
    first = iota((RB, PAIR), 1) < SPEC_CH
    acc[...] = jnp.zeros_like(acc)
    for kk in range(PER_GROUP):
        prod[...] = dot(forward[...], gather_parts(stage, kk))
        pre[...] = dot(spec[kk * 4 : kk * 4 + 4].reshape(512, 256), wide[...])

        @pl.loop(0, GROUPS, step=RB)
        def _(rows):
            rows = pl.multiple_of(rows, RB)
            parts = spectrum_rows(prod, twiddle, rows, signs, first)
            for q in range(4):
                for part in range(2):
                    lanes = slice(part * PAIR, (part + 1) * PAIR)
                    v = pre[pl.ds(q * GROUPS + rows, RB), lanes]
                    s = sigmoid(v)
                    v = parts[q][part] * (s * (1.0 + v * (1.0 - s)))
                    slope[pl.ds(q * GROUPS + rows, RB), lanes] = v.astype(BF16)

        acc[...] += dot_t(slope[...], spec[kk * 4 : kk * 4 + 4].reshape(512, 256))
    lane = iota((SPEC_CH, PAIR), 1) < SPEC_CH
    for part in range(2):
        even = acc[part * PAIR : part * PAIR + SPEC_CH, :]
        odd = acc[part * PAIR + SPEC_CH : (part + 1) * PAIR, :]
        real = even[:, 0:PAIR] + pltpu.roll(odd[:, 0:PAIR], SPEC_CH, 1)
        imag = pltpu.roll(even[:, PAIR:], SPEC_CH, 1) + odd[:, PAIR:]
        grad[part * SPEC_CH : (part + 1) * SPEC_CH, :] = jnp.where(lane, real, imag)


def mix_terms(block, spec, forward, twiddle, mix_w):
    return pl.pallas_call(
        mix_kernel,
        grid=(1,),
        in_specs=[
            pl.BlockSpec((1024, 512), lambda i: (0, 1)),
            whole_spec((16, GROUPS, 256)),
            whole_spec((256, 256)),
            whole_spec((2, GROUPS, 512)),
            whole_spec((128, 128)),
        ],
        out_specs=whole_spec((128, 128)),
        out_shape=jax.ShapeDtypeStruct((128, 128), F32),
        scratch_shapes=[
            pltpu.VMEM((4, 1024, PAIR), F32),
            pltpu.VMEM((256, 256), BF16),
            pltpu.VMEM((256, 512), F32),
            pltpu.VMEM((512, 256), F32),
            pltpu.VMEM((512, 256), BF16),
            pltpu.VMEM((256, 256), F32),
        ],
        compiler_params=params(),
        cost_estimate=cost(6 * 10**9, 5 * 2**20),
    )(block, spec, forward, twiddle, mix_w)


def back_kernel(table, rows, inner, cot, mix_part, above, below, summed, terms, acc):
    del above, below
    step = pl.program_id(0)

    @pl.when(step == 0)
    def _():
        acc[...] = jnp.zeros_like(acc)

    total = (dot(table[...], rows[...]) + inner[...].astype(F32)).astype(BF16)
    summed[...] = total
    for p in range(4):
        pair = jnp.concatenate([cot[0, 2 * p], cot[0, 2 * p + 1]], axis=1)
        acc[...] += dot_t(pair, total[:, p * PAIR : (p + 1) * PAIR])

    @pl.when(step == 3)
    def _():
        lane = iota((128, PAIR), 1) < SPEC_CH
        out_part = acc[0:128, :] + pltpu.roll(acc[128:, :], SPEC_CH, 1)
        out_part = jnp.where(lane, out_part, 0.0)
        for img in range(2):
            terms[pl.ds(2 * img, 128, stride=4), :] = mix_part[...]
            terms[pl.ds(2 * img + 1, 128, stride=4), :] = out_part


def back_rows(table, rows, inner, cot, mix_part, above, below):
    return pl.pallas_call(
        back_kernel,
        grid=(4,),
        in_specs=[
            pl.BlockSpec((256, 1024), lambda i: (i, 0)),
            whole_spec((1024, 512)),
            pl.BlockSpec((256, 512), lambda i: (i, 0)),
            pl.BlockSpec((1, ROWS, 256, 128), lambda i: (0, 0, i, 0)),
            whole_spec((128, 128)),
            pl.BlockSpec(memory_space=pl.ANY),
            pl.BlockSpec(memory_space=pl.ANY),
        ],
        out_specs=[pl.BlockSpec((256, 512), lambda i: (i, 0)), whole_spec((512, 128))],
        out_shape=[
            jax.ShapeDtypeStruct((WIDTH, 512), BF16),
            jax.ShapeDtypeStruct((512, 128), F32),
        ],
        scratch_shapes=[pltpu.VMEM((256, 128), F32)],
        compiler_params=params(),
        cost_estimate=cost(2 * 10**9, 8 * 2**20),
    )(table, rows, inner, cot, mix_part, above, below)


def out_kernel(summed, out_w, out, wide):
    @pl.when(pl.program_id(0) == 0)
    def _():
        zero = jnp.zeros((SPEC_CH, 128), BF16)
        wide[0:SPEC_CH, :] = jnp.concatenate([out_w[...], zero], axis=1)
        wide[SPEC_CH:, :] = jnp.concatenate([zero, out_w[...]], axis=1)

    for p in range(4):
        prod = dot(summed[:, p * PAIR : (p + 1) * PAIR], wide[...]).astype(BF16)
        out[0, 2 * p] = prod[:, 0:128]
        out[0, 2 * p + 1] = prod[:, 128:]


def project_out(summed, out_w):
    return pl.pallas_call(
        out_kernel,
        grid=(4,),
        in_specs=[pl.BlockSpec((256, 512), lambda i: (i, 0)), whole_spec((SPEC_CH, 128))],
        out_specs=pl.BlockSpec((1, ROWS, 256, 128), lambda i: (0, 0, i, 0)),
        out_shape=jax.ShapeDtypeStruct((1, ROWS, WIDTH, 128), BF16),
        scratch_shapes=[pltpu.VMEM((128, 256), BF16)],
        compiler_params=params(),
        cost_estimate=cost(5 * 10**8, 3 * 2**20),
    )(summed, out_w)


def conv_row(top, mid, bottom, weight, out, sums, wide):
    @pl.when(pl.program_id(0) == 0)
    def _():
        for a in range(3):
            for b in range(3):
                wide[a * 128 : (a + 1) * 128, b * 128 : (b + 1) * 128] = weight[a, b]
        sums[0, 0:8] = jnp.zeros((8, 128), F32)
        sums[2, WIDTH + 8 :] = jnp.zeros((8, 128), F32)

    prod = dot(jnp.concatenate([top, mid, bottom], axis=1), wide[...])
    for b in range(3):
        sums[b, 8 : WIDTH + 8] = prod[:, b * 128 : (b + 1) * 128]
    total = sums[0, 7 : WIDTH + 7] + sums[1, 8 : WIDTH + 8] + sums[2, 9 : WIDTH + 9]
    out[0, 0] = total.astype(BF16)


def inner_kernel(above, mid, below, weight, ready, out, sums, wide):
    del ready
    conv_row(above[0, 0], mid[0, 0], below[0, 0], weight, out, sums, wide)


def edge_kernel(mid, beside, edge_above, edge_below, weight, done, ready, out, sums, wide):
    del done, ready
    first = pl.program_id(0) == 0
    top = jnp.where(first, edge_above[0, 0], beside[0, 0])
    bottom = jnp.where(first, beside[0, 0], edge_below[0, 0])
    conv_row(top, mid[0, 0], bottom, weight, out, sums, wide)


def row_spec(index):
    return pl.BlockSpec((1, 1, WIDTH, 128), lambda i: (0, index(i), 0, 0))


def conv_call(kernel, rows, in_specs, out_index, aliases, args):
    return pl.pallas_call(
        kernel,
        grid=(rows,),
        in_specs=in_specs,
        out_specs=row_spec(out_index),
        out_shape=jax.ShapeDtypeStruct((1, ROWS, WIDTH, 128), BF16),
        scratch_shapes=[pltpu.VMEM((3, WIDTH + 16, 128), F32), pltpu.VMEM((384, 384), BF16)],
        input_output_aliases=aliases,
        compiler_params=params(),
        cost_estimate=cost(rows * 10**9, rows * 2**20),
    )(*args)


def inner_rows(cells, weight, ready):
    specs = [
        row_spec(lambda i: i),
        row_spec(lambda i: i + 1),
        row_spec(lambda i: i + 2),
        whole_spec((3, 3, 128, 128)),
        pl.BlockSpec(memory_space=pl.ANY),
    ]
    args = (cells, cells, cells, weight, ready)
    return conv_call(inner_kernel, ROWS - 2, specs, lambda i: i + 1, {}, args)


def neighbour_rows(cells):
    ends = GROUPS - 1
    head, tail = cells[:, 0:1], cells[:, ROWS - 1 :]
    above = lax.ppermute(tail, "rows", [(i, i + 1) for i in range(ends)])
    below = lax.ppermute(head, "rows", [(i + 1, i) for i in range(ends)])
    return above, below


def edge_rows(cells, above, below, weight, done, ready):
    specs = [
        row_spec(lambda i: i * (ROWS - 1)),
        row_spec(lambda i: 1 + i * (ROWS - 3)),
        whole_spec((1, 1, WIDTH, 128)),
        whole_spec((1, 1, WIDTH, 128)),
        whole_spec((3, 3, 128, 128)),
        pl.BlockSpec(memory_space=pl.ANY),
        pl.BlockSpec(memory_space=pl.ANY),
    ]
    args = (cells, cells, above, below, weight, done, ready)
    return conv_call(edge_kernel, 2, specs, lambda i: i * (ROWS - 1), {5: 0}, args)


def exchange(block):
    lanes = block.shape[1]
    moved = lax.all_to_all(
        block.reshape(GROUPS, ROWS, lanes), "rows", split_axis=0, concat_axis=0, tiled=True
    )
    return moved.reshape(GROUPS * ROWS, lanes)


def shards(local_maps, global_maps, conv_weight, in_weight, mix_weight, out_weight, out_cotangent):
    row_fwd, row_inv = row_tables()
    forward, backward, twiddle = column_tables()
    spec_rows, inner = rows_forward(global_maps, out_cotangent, in_weight.T, out_weight, row_fwd)
    spec_cols = exchange(spec_rows)
    local_inner = inner_rows(local_maps, conv_weight, spec_rows)
    spectrum, back_cols = columns(spec_cols, forward, backward, twiddle, mix_weight, local_inner)
    back = exchange(back_cols)
    mix_part = mix_terms(spec_cols, spectrum, forward, twiddle, mix_weight)
    above, below = neighbour_rows(local_maps)
    summed, terms = back_rows(row_inv, back, inner, out_cotangent, mix_part, above, below)
    local_out = edge_rows(local_maps, above, below, conv_weight, local_inner, terms)
    terms = terms.reshape(256, 2, 128)
    terms = lax.all_to_all(terms, ("rows", "img"), split_axis=0, concat_axis=0, tiled=True)
    global_out = project_out(summed, out_weight)
    total = jnp.sum(terms, axis=0)
    mix_grad = total[0].reshape(128, 1)
    out_grad = total[1, 0:SPEC_CH].reshape(SPEC_CH, 1)
    return (local_out, global_out, mix_grad, out_grad)


def solution(mesh):
    maps = P("img", "rows", None, None)
    in_specs = (maps, maps, P(), P(), P(), P(), maps)
    out_specs = (maps, maps, P(None, "rows"), P(None, "rows"))
    return jax.shard_map(shards, mesh=mesh, in_specs=in_specs, out_specs=out_specs, check_vma=False)
```

```python
import math

import jax
import jax.numpy as jnp
import ml_dtypes
import numpy as np
from jax import lax
from jax.experimental import pallas as pl
from jax.experimental.pallas import tpu as pltpu
from jax.sharding import PartitionSpec as P

HEIGHT = 1024
WIDTH = 1024
SPEC_CH = 64
FREQS = 512
ROWS = 8
GROUPS = 128
PER_GROUP = 4
PAIR = 128
BF16 = jnp.bfloat16
F32 = jnp.float32

LIMIT = 60 * 2**20
SMALL = 40 * 2**20


def params(limit=LIMIT):
    return pltpu.CompilerParams(vmem_limit_bytes=limit)


def in_hbm(x):
    return pltpu.with_memory_space_constraint(x, pltpu.HBM)


VMEM = pl.BlockSpec(memory_space=pltpu.VMEM)


ANY = pl.BlockSpec(memory_space=pl.ANY)


def cost(flops, nbytes):
    return pl.CostEstimate(flops=flops, bytes_accessed=nbytes, transcendentals=0)


def row_tables():
    cols = np.arange(WIDTH)
    freq = np.arange(FREQS)
    phase = ((cols[:, None] * freq[None, :]) % WIDTH) * (2.0 * math.pi / WIDTH)
    forward = np.stack([np.cos(phase), -np.sin(phase)], axis=1) / math.sqrt(WIDTH)
    forward = forward.reshape(WIDTH, 2, GROUPS, PER_GROUP).transpose(0, 2, 1, 3)
    factor = np.where(freq == 0, 1.0, 2.0).reshape(1, GROUPS, 1, PER_GROUP)
    inverse = (forward * factor).reshape(WIDTH, 2 * FREQS)
    forward = np.ascontiguousarray(forward.reshape(WIDTH, 2 * FREQS).T)
    return forward.astype(ml_dtypes.bfloat16), inverse.astype(ml_dtypes.bfloat16)


def column_tables():
    idx = np.arange(GROUPS)
    phase = ((idx[:, None] * idx[None, :]) % GROUPS) * (2.0 * math.pi / GROUPS)
    cosine, sine = np.cos(phase) / math.sqrt(HEIGHT), np.sin(phase) / math.sqrt(HEIGHT)
    forward = np.block([[cosine, sine], [-sine, cosine]])
    backward = np.block([[cosine, -sine], [sine, cosine]])
    turn = (idx[:, None] * np.arange(ROWS)[None, :]) * (2.0 * math.pi / HEIGHT)
    twiddle = np.repeat(np.stack([np.cos(turn), np.sin(turn)]), SPEC_CH, axis=2)
    return (
        forward.astype(ml_dtypes.bfloat16),
        backward.astype(ml_dtypes.bfloat16),
        twiddle.astype(np.float32),
    )


def dot(a, b):
    return jnp.dot(a, b, preferred_element_type=F32)


def dot_t(a, b):
    return lax.dot_general(a, b, (((0,), (0,)), ((), ())), preferred_element_type=F32)


def iota(shape, dim):
    return lax.broadcasted_iota(jnp.int32, shape, dim)


def first_half():
    return jnp.where(iota((SPEC_CH, PAIR), 0) == iota((SPEC_CH, PAIR), 1), 1.0, 0.0).astype(BF16)


def second_half():
    hit = iota((SPEC_CH, PAIR), 0) + SPEC_CH == iota((SPEC_CH, PAIR), 1)
    return jnp.where(hit, 1.0, 0.0).astype(BF16)


def rows_kernel(
    maps, cot, in_w, out_w, table, spec_out, inner_out,
    pairs, held, both, result, in_pair, out_pair, sems, table_sems, out_sems,
):
    half = ROWS * SPEC_CH
    loads = []
    for p in range(4):
        for n, source in enumerate((maps, cot)):
            rows = source.at[0, pl.ds(2 * p, 2)]
            loads.append(pltpu.make_async_copy(rows, pairs.at[p, n], sems.at[p, n]))
    tables = []
    for b in range(4):
        rows = pl.ds(b * 256, 256)
        tables.append(pltpu.make_async_copy(table.at[rows], held.at[rows], table_sems.at[b]))
    for copy in loads + tables:
        copy.start()
    a, b = first_half(), second_half()
    in_pair[0:PAIR, :] = dot_t(in_w[...], a).astype(BF16)
    in_pair[PAIR:, :] = dot_t(in_w[...], b).astype(BF16)
    out_pair[0:PAIR, :] = dot_t(out_w[...], a).astype(BF16)
    out_pair[PAIR:, :] = dot_t(out_w[...], b).astype(BF16)
    for p in range(4):
        lanes = slice(p * PAIR, (p + 1) * PAIR)
        loads[2 * p].wait()
        pair = jnp.concatenate([pairs[p, 0, 0], pairs[p, 0, 1]], axis=1)
        both[:, lanes] = jnp.maximum(dot(pair, in_pair[...]), 0.0).astype(BF16)
        lanes = slice(half + p * PAIR, half + (p + 1) * PAIR)
        loads[2 * p + 1].wait()
        pair = jnp.concatenate([pairs[p, 1, 0], pairs[p, 1, 1]], axis=1)
        both[:, lanes] = dot(pair, out_pair[...]).astype(BF16)
    stores = [pltpu.make_async_copy(both.at[:, pl.ds(0, half)], inner_out, out_sems.at[4])]
    stores[0].start()
    for b in range(4):
        rows = pl.ds(b * 256, 256)
        tables[b].wait()
        prod = dot(held[rows, :], both[...])
        result[rows, 0:half] = prod[:, 0:half].astype(BF16)
        row = b * 256 + iota((256, half), 0)
        factor = jnp.where((row == 0) | (row == PER_GROUP), 1.0, 2.0)
        result[rows, half:] = (prod[:, half:] * factor).astype(BF16)
        stores.append(pltpu.make_async_copy(result.at[rows], spec_out.at[rows], out_sems.at[b]))
        stores[-1].start()
    for copy in stores:
        copy.wait()


def rows_forward(maps, cot, in_w, out_w, table):
    return pl.pallas_call(
        rows_kernel,
        grid=(1,),
        in_specs=[ANY, ANY, whole_spec((SPEC_CH, 128)), whole_spec((SPEC_CH, 128)), ANY],
        out_specs=[ANY, ANY],
        out_shape=[
            pltpu.HBM((1024, 1024), BF16),
            pltpu.HBM((WIDTH, 512), BF16),
        ],
        scratch_shapes=[
            pltpu.VMEM((4, 2, 2, WIDTH, 128), BF16),
            pltpu.VMEM((1024, WIDTH), BF16),
            pltpu.VMEM((WIDTH, 1024), BF16),
            pltpu.VMEM((1024, 1024), BF16),
            pltpu.VMEM((256, PAIR), BF16),
            pltpu.VMEM((256, PAIR), BF16),
            pltpu.SemaphoreType.DMA((4, 2)),
            pltpu.SemaphoreType.DMA((4,)),
            pltpu.SemaphoreType.DMA((5,)),
        ],
        compiler_params=params(),
        cost_estimate=cost(5 * 10**9, 11 * 2**20),
    )(maps, cot, in_w, out_w, table)


ROOT = math.sqrt(0.5)


def lane_signs(shape):
    return jnp.where(iota(shape, 1) % PAIR < SPEC_CH, 1.0, -1.0).astype(F32)


def lane_butterfly(x, signs):
    return pltpu.roll(x, SPEC_CH, 1) + x * signs


def turn_second(re, im, first, real, imag):
    new_re = jnp.where(first, re, re * real - im * imag)
    new_im = jnp.where(first, im, re * imag + im * real)
    return new_re, new_im


EIGHTHS = ((1.0, 0.0), (ROOT, -ROOT), (0.0, -1.0), (-ROOT, -ROOT))


def spectrum_rows(prod, twiddle, rows, signs, first):
    re, im = [], []
    for m in range(4):
        lanes = slice(m * PAIR, (m + 1) * PAIR)
        a = prod[pl.ds(rows, RB), lanes]
        b = prod[pl.ds(GROUPS + rows, RB), lanes]
        c = twiddle[0, pl.ds(rows, RB), lanes]
        s = twiddle[1, pl.ds(rows, RB), lanes]
        re.append(a * c + b * s)
        im.append(b * c - a * s)
    s0r, s0i, d0r, d0i = re[0] + re[2], im[0] + im[2], re[0] - re[2], im[0] - im[2]
    s1r, s1i, d1r, d1i = re[1] + re[3], im[1] + im[3], re[1] - re[3], im[1] - im[3]
    four = (
        (s0r + s1r, s0i + s1i),
        (d0r + d1i, d0i - d1r),
        (s0r - s1r, s0i - s1i),
        (d0r - d1i, d0i + d1r),
    )
    out = []
    for q in range(4):
        zr, zi = four[q]
        if q:
            zr, zi = turn_second(zr, zi, first, *EIGHTHS[q])
        out.append((lane_butterfly(zr, signs), lane_butterfly(zi, signs)))
    return out


def inverse_rows(parts, twiddle, rows, signs, first):
    z = []
    for q in range(4):
        zr, zi = (lane_butterfly(x, signs) for x in parts[q])
        if q:
            zr, zi = turn_second(zr, zi, first, EIGHTHS[q][0], -EIGHTHS[q][1])
        z.append((zr, zi))
    s0r, s0i = z[0][0] + z[2][0], z[0][1] + z[2][1]
    d0r, d0i = z[0][0] - z[2][0], z[0][1] - z[2][1]
    s1r, s1i = z[1][0] + z[3][0], z[1][1] + z[3][1]
    d1r, d1i = z[1][0] - z[3][0], z[1][1] - z[3][1]
    four = (
        (s0r + s1r, s0i + s1i),
        (d0r - d1i, d0i + d1r),
        (s0r - s1r, s0i - s1i),
        (d0r + d1i, d0i - d1r),
    )
    out = []
    for m in range(4):
        lanes = slice(m * PAIR, (m + 1) * PAIR)
        c = twiddle[0, pl.ds(rows, RB), lanes]
        s = twiddle[1, pl.ds(rows, RB), lanes]
        a, b = four[m]
        out.append((a * c - b * s, b * c + a * s))
    return out


RB = 16


def fill_mix(mix_w, wide):
    total = jnp.zeros((256, 256), F32)
    for t in range(2):
        row, col = iota((256, 128), 0), iota((256, 128), 1)
        at = (row // PAIR) * SPEC_CH + row % SPEC_CH
        hit = (at == col) & (row // SPEC_CH % 2 == t)
        pick = jnp.where(hit, 1.0, 0.0).astype(BF16)
        left = dot(pick, mix_w[...]).astype(BF16)
        total = total + lax.dot_general(
            left, pick, (((1,), (1,)), ((), ())), preferred_element_type=F32
        )
    wide[...] = total.astype(BF16)


def sigmoid(x):
    return 0.5 * jnp.tanh(0.5 * x) + 0.5


def gather_parts(stage, kk):
    lanes = []
    for m in range(4):
        re = stage[m, pl.ds(kk, GROUPS, stride=ROWS), :]
        im = stage[m, pl.ds(PER_GROUP + kk, GROUPS, stride=ROWS), :]
        lanes.append(jnp.concatenate([re, im], axis=0).astype(BF16))
    return jnp.concatenate(lanes, axis=1)


def fill_stage(block, stage):
    for m in range(4):
        stage[m] = block[:, m * PAIR : (m + 1) * PAIR].astype(F32)


def columns_kernel(
    block, forward_in, backward_in, twiddle_in, mix_in, ready, above, below, spec_out, back_out,
    land, forward, backward, twiddle, mix_w, spec, stage, wide, prod, pre, inv, sems, out_sems,
):
    del ready, above, below
    mix_load = pltpu.make_async_copy(mix_in, mix_w, sems.at[4])
    forward_load = pltpu.make_async_copy(forward_in, forward, sems.at[5])
    twiddle_load = pltpu.make_async_copy(twiddle_in, twiddle, sems.at[6])
    backward_load = pltpu.make_async_copy(backward_in, backward, sems.at[7])
    for copy in (mix_load, forward_load, twiddle_load, backward_load):
        copy.start()
    for m in range(4):
        stage[m] = block[:, m * PAIR : (m + 1) * PAIR].astype(F32)
    mix_load.wait()
    fill_mix(mix_w, wide)
    forward_load.wait()
    twiddle_load.wait()
    backward_load.wait()
    stores = []
    signs = lane_signs((RB, PAIR))
    first = iota((RB, PAIR), 1) < SPEC_CH
    for kk in range(PER_GROUP):
        prod[...] = dot(forward[...], gather_parts(stage, kk))

        @pl.loop(0, GROUPS, step=RB, unroll=True)
        def _(rows):
            rows = pl.multiple_of(rows, RB)
            parts = spectrum_rows(prod, twiddle, rows, signs, first)
            for q in range(4):
                spec[kk * 4 + q, pl.ds(rows, RB), 0:PAIR] = parts[q][0].astype(BF16)
                spec[kk * 4 + q, pl.ds(rows, RB), PAIR:] = parts[q][1].astype(BF16)

        part = pl.ds(kk * 4, 4)
        stores.append(pltpu.make_async_copy(spec.at[part], spec_out.at[part], out_sems.at[kk]))
        stores[-1].start()
        pre[...] = dot(spec[kk * 4 : kk * 4 + 4].reshape(512, 256), wide[...])

        @pl.loop(0, GROUPS, step=RB, unroll=True)
        def _(rows):
            rows = pl.multiple_of(rows, RB)
            parts = []
            for q in range(4):
                v = pre[pl.ds(q * GROUPS + rows, RB), :]
                v = v * sigmoid(v)
                parts.append((v[:, 0:PAIR], v[:, PAIR:]))
            pairs = inverse_rows(parts, twiddle, rows, signs, first)
            for m in range(4):
                lanes = slice(m * PAIR, (m + 1) * PAIR)
                inv[pl.ds(rows, RB), lanes] = pairs[m][0].astype(BF16)
                inv[pl.ds(GROUPS + rows, RB), lanes] = pairs[m][1].astype(BF16)

        result = dot(backward[...], inv[...])
        for m in range(4):
            lanes = slice(m * PAIR, (m + 1) * PAIR)
            stage[m, pl.ds(kk, GROUPS, stride=ROWS), :] = result[0:GROUPS, lanes]
            stage[m, pl.ds(PER_GROUP + kk, GROUPS, stride=ROWS), :] = result[GROUPS:, lanes]
    for m in range(4):
        land[:, m * PAIR : (m + 1) * PAIR] = stage[m].astype(BF16)
        lanes = pl.ds(m * PAIR, PAIR)
        copy = pltpu.make_async_copy(land.at[:, lanes], back_out.at[:, lanes], out_sems.at[4 + m])
        copy.start()
        stores.append(copy)
    for copy in stores:
        copy.wait()


def whole_spec(shape):
    return pl.BlockSpec(shape, lambda *_: (0,) * len(shape))


def columns(block, forward, backward, twiddle, mix_w, ready, above, below):
    return pl.pallas_call(
        columns_kernel,
        in_specs=[VMEM] + [ANY] * 7,
        out_specs=[ANY, ANY],
        out_shape=[
            pltpu.HBM((16, GROUPS, 256), BF16),
            pltpu.HBM((1024, 512), BF16),
        ],
        scratch_shapes=[
            pltpu.VMEM((1024, 512), BF16),
            pltpu.VMEM((256, 256), BF16),
            pltpu.VMEM((256, 256), BF16),
            pltpu.VMEM((2, GROUPS, 512), F32),
            pltpu.VMEM((128, 128), BF16),
            pltpu.VMEM((16, GROUPS, 256), BF16),
            pltpu.VMEM((4, 1024, PAIR), F32),
            pltpu.VMEM((256, 256), BF16),
            pltpu.VMEM((256, 512), F32),
            pltpu.VMEM((512, 256), F32),
            pltpu.VMEM((256, 512), BF16),
            pltpu.SemaphoreType.DMA((8,)),
            pltpu.SemaphoreType.DMA((8,)),
        ],
        compiler_params=params(SMALL),
        cost_estimate=cost(8 * 10**9, 5 * 2**20),
    )(block, forward, backward, twiddle, mix_w, in_hbm(ready), above, below)


def mix_kernel(block, spec, forward, twiddle, mix_w, grad, stage, wide, prod, pre, slope, acc):
    fill_mix(mix_w, wide)
    fill_stage(block, stage)
    signs = lane_signs((RB, PAIR))
    first = iota((RB, PAIR), 1) < SPEC_CH
    acc[...] = jnp.zeros_like(acc)
    for kk in range(PER_GROUP):
        prod[...] = dot(forward[...], gather_parts(stage, kk))
        pre[...] = dot(spec[kk * 4 : kk * 4 + 4].reshape(512, 256), wide[...])

        @pl.loop(0, GROUPS, step=RB, unroll=True)
        def _(rows):
            rows = pl.multiple_of(rows, RB)
            parts = spectrum_rows(prod, twiddle, rows, signs, first)
            for q in range(4):
                for part in range(2):
                    lanes = slice(part * PAIR, (part + 1) * PAIR)
                    v = pre[pl.ds(q * GROUPS + rows, RB), lanes]
                    s = sigmoid(v)
                    v = parts[q][part] * (s * (1.0 + v * (1.0 - s)))
                    slope[pl.ds(q * GROUPS + rows, RB), lanes] = v.astype(BF16)

        acc[...] += dot_t(slope[...], spec[kk * 4 : kk * 4 + 4].reshape(512, 256))
    lane = iota((SPEC_CH, PAIR), 1) < SPEC_CH
    for part in range(2):
        even = acc[part * PAIR : part * PAIR + SPEC_CH, :]
        odd = acc[part * PAIR + SPEC_CH : (part + 1) * PAIR, :]
        real = even[:, 0:PAIR] + pltpu.roll(odd[:, 0:PAIR], SPEC_CH, 1)
        imag = pltpu.roll(even[:, PAIR:], SPEC_CH, 1) + odd[:, PAIR:]
        grad[part * SPEC_CH : (part + 1) * SPEC_CH, :] = jnp.where(lane, real, imag)


def mix_terms(block, spec, forward, twiddle, mix_w):
    return pl.pallas_call(
        mix_kernel,
        grid=(1,),
        in_specs=[
            pl.BlockSpec((1024, 512), lambda i: (0, 1)),
            whole_spec((16, GROUPS, 256)),
            whole_spec((256, 256)),
            whole_spec((2, GROUPS, 512)),
            whole_spec((128, 128)),
        ],
        out_specs=whole_spec((128, 128)),
        out_shape=jax.ShapeDtypeStruct((128, 128), F32),
        scratch_shapes=[
            pltpu.VMEM((4, 1024, PAIR), F32),
            pltpu.VMEM((256, 256), BF16),
            pltpu.VMEM((256, 512), F32),
            pltpu.VMEM((512, 256), F32),
            pltpu.VMEM((512, 256), BF16),
            pltpu.VMEM((256, 256), F32),
        ],
        compiler_params=params(),
        cost_estimate=cost(6 * 10**9, 5 * 2**20),
    )(block, spec, forward, twiddle, mix_w)


def back_kernel(
    table, block, inner, cot, mix_part, ready, summed_out, terms_out,
    held, inners, cots, mix, summed, terms, acc, sems, out_sems,
):
    def load(source, target, sem):
        copy = pltpu.make_async_copy(source, target, sems.at[sem])
        copy.start()
        return copy

    del ready
    loads = []
    for b in range(4):
        at = pl.ds(b * 256, 256)
        loads.append(
            (
                load(table.at[at], held.at[at], 4 * b + 1),
                load(inner.at[at], inners.at[at], 4 * b + 2),
                load(cot.at[0, :, at], cots.at[:, at], 4 * b + 3),
            )
        )
    last = load(mix_part, mix, 4)
    stores = []
    for b in range(4):
        for copy in loads[b]:
            copy.wait()
        at = slice(b * 256, (b + 1) * 256)
        total = (dot(held[at, :], block[...]) + inners[at, :].astype(F32)).astype(BF16)
        summed[at, :] = total
        rows_at = pl.ds(b * 256, 256)
        copy = pltpu.make_async_copy(summed.at[rows_at], summed_out.at[rows_at], out_sems.at[b])
        copy.start()
        stores.append(copy)
        for p in range(4):
            pair = jnp.concatenate([cots[2 * p, at, :], cots[2 * p + 1, at, :]], axis=1)
            part = dot_t(pair, total[:, p * PAIR : (p + 1) * PAIR])
            if b + p:
                acc[...] += part
            else:
                acc[...] = part
    last.wait()
    lane = iota((128, PAIR), 1) < SPEC_CH
    out_part = acc[0:128, :] + pltpu.roll(acc[128:, :], SPEC_CH, 1)
    out_part = jnp.where(lane, out_part, 0.0)
    for img in range(2):
        terms[pl.ds(2 * img, 128, stride=4), :] = mix[...]
        terms[pl.ds(2 * img + 1, 128, stride=4), :] = out_part
    copy = pltpu.make_async_copy(terms, terms_out, out_sems.at[4])
    copy.start()
    stores.append(copy)
    for copy in stores:
        copy.wait()


def back_rows(table, rows, inner, cot, mix_part, ready):
    return pl.pallas_call(
        back_kernel,
        in_specs=[ANY, VMEM, ANY, ANY, ANY, ANY],
        out_specs=[ANY, ANY],
        out_shape=[
            pltpu.HBM((WIDTH, 512), BF16),
            pltpu.HBM((512, 128), F32),
        ],
        scratch_shapes=[
            pltpu.VMEM((WIDTH, 1024), BF16),
            pltpu.VMEM((WIDTH, 512), BF16),
            pltpu.VMEM((ROWS, WIDTH, 128), BF16),
            pltpu.VMEM((128, 128), F32),
            pltpu.VMEM((WIDTH, 512), BF16),
            pltpu.VMEM((512, 128), F32),
            pltpu.VMEM((256, 128), F32),
            pltpu.SemaphoreType.DMA((17,)),
            pltpu.SemaphoreType.DMA((5,)),
        ],
        compiler_params=params(SMALL),
        cost_estimate=cost(2 * 10**9, 8 * 2**20),
    )(in_hbm(table), rows, in_hbm(inner), in_hbm(cot), in_hbm(mix_part), in_hbm(ready))


def out_kernel(summed, out_w, out, wide):
    @pl.when(pl.program_id(0) == 0)
    def _():
        zero = jnp.zeros((SPEC_CH, 128), BF16)
        wide[0:SPEC_CH, :] = jnp.concatenate([out_w[...], zero], axis=1)
        wide[SPEC_CH:, :] = jnp.concatenate([zero, out_w[...]], axis=1)

    for p in range(4):
        prod = dot(summed[:, p * PAIR : (p + 1) * PAIR], wide[...]).astype(BF16)
        out[0, 2 * p] = prod[:, 0:128]
        out[0, 2 * p + 1] = prod[:, 128:]


def project_out(summed, out_w):
    return pl.pallas_call(
        out_kernel,
        grid=(4,),
        in_specs=[pl.BlockSpec((256, 512), lambda i: (i, 0)), whole_spec((SPEC_CH, 128))],
        out_specs=pl.BlockSpec((1, ROWS, 256, 128), lambda i: (0, 0, i, 0)),
        out_shape=jax.ShapeDtypeStruct((1, ROWS, WIDTH, 128), BF16),
        scratch_shapes=[pltpu.VMEM((128, 256), BF16)],
        compiler_params=params(),
        cost_estimate=cost(5 * 10**8, 3 * 2**20),
    )(summed, out_w)


def conv_row(top, mid, bottom, weight, out, token, sums, wide):
    @pl.when(pl.program_id(0) == 0)
    def _():
        token[...] = jnp.zeros((8, 128), F32)
        for a in range(3):
            for b in range(3):
                wide[a * 128 : (a + 1) * 128, b * 128 : (b + 1) * 128] = weight[a, b]
        sums[0, 0:8] = jnp.zeros((8, 128), F32)
        sums[2, WIDTH + 8 :] = jnp.zeros((8, 128), F32)

    prod = dot(jnp.concatenate([top, mid, bottom], axis=1), wide[...])
    for b in range(3):
        sums[b, 8 : WIDTH + 8] = prod[:, b * 128 : (b + 1) * 128]
    total = sums[0, 7 : WIDTH + 7] + sums[1, 8 : WIDTH + 8] + sums[2, 9 : WIDTH + 9]
    out[0, 0] = total.astype(BF16)


def inner_kernel(above, mid, below, weight, ready, out, token, sums, wide):
    del ready
    conv_row(above[0, 0], mid[0, 0], below[0, 0], weight, out, token, sums, wide)


def edge_kernel(mid, beside, edge_above, edge_below, weight, done, ready, out, token, sums, wide):
    del done, ready
    first = pl.program_id(0) == 0
    top = jnp.where(first, edge_above[0, 0], beside[0, 0])
    bottom = jnp.where(first, beside[0, 0], edge_below[0, 0])
    conv_row(top, mid[0, 0], bottom, weight, out, token, sums, wide)


def row_spec(index):
    return pl.BlockSpec((1, 1, WIDTH, 128), lambda i: (0, index(i), 0, 0))


def conv_call(kernel, rows, in_specs, out_index, aliases, args):
    return pl.pallas_call(
        kernel,
        grid=(rows,),
        in_specs=in_specs,
        out_specs=[row_spec(out_index), whole_spec((8, 128))],
        out_shape=[
            pltpu.HBM((1, ROWS, WIDTH, 128), BF16),
            jax.ShapeDtypeStruct((8, 128), F32),
        ],
        scratch_shapes=[pltpu.VMEM((3, WIDTH + 16, 128), F32), pltpu.VMEM((384, 384), BF16)],
        input_output_aliases=aliases,
        compiler_params=params(),
        cost_estimate=cost(rows * 10**9, rows * 2**20),
    )(*args)


def inner_rows(cells, weight, ready):
    specs = [
        row_spec(lambda i: i),
        row_spec(lambda i: i + 1),
        row_spec(lambda i: i + 2),
        whole_spec((3, 3, 128, 128)),
        pl.BlockSpec(memory_space=pl.ANY),
    ]
    args = (cells, cells, cells, weight, ready)
    return conv_call(inner_kernel, ROWS - 2, specs, lambda i: i + 1, {}, args)


def neighbour_rows(cells):
    ends = GROUPS - 1
    head, tail = cells[:, 0:1], cells[:, ROWS - 1 :]
    above = lax.ppermute(tail, "rows", [(i, i + 1) for i in range(ends)])
    below = lax.ppermute(head, "rows", [(i + 1, i) for i in range(ends)])
    return above, below


def edge_rows(cells, above, below, weight, done, ready):
    specs = [
        row_spec(lambda i: i * (ROWS - 1)),
        row_spec(lambda i: 1 + i * (ROWS - 3)),
        whole_spec((1, 1, WIDTH, 128)),
        whole_spec((1, 1, WIDTH, 128)),
        whole_spec((3, 3, 128, 128)),
        pl.BlockSpec(memory_space=pl.ANY),
        pl.BlockSpec(memory_space=pl.ANY),
    ]
    args = (cells, cells, above, below, weight, done, ready)
    return conv_call(edge_kernel, 2, specs, lambda i: i * (ROWS - 1), {5: 0}, args)


def exchange(block):
    lanes = block.shape[1]
    moved = lax.all_to_all(
        block.reshape(GROUPS, ROWS, lanes), "rows", split_axis=0, concat_axis=0, tiled=True
    )
    return moved.reshape(GROUPS * ROWS, lanes)


def shards(local_maps, global_maps, conv_weight, in_weight, mix_weight, out_weight, out_cotangent):
    row_fwd, row_inv = row_tables()
    forward, backward, twiddle = column_tables()
    spec_rows, inner = rows_forward(global_maps, out_cotangent, in_weight.T, out_weight, row_fwd)
    spec_cols = exchange(spec_rows)
    local_inner, token = inner_rows(local_maps, conv_weight, spec_rows)
    above, below = neighbour_rows(local_maps)
    spectrum, back_cols = columns(
        spec_cols, forward, backward, twiddle, mix_weight, token, above, below
    )
    back = exchange(back_cols)
    mix_part = mix_terms(spec_cols, spectrum, forward, twiddle, mix_weight)
    local_out, token = edge_rows(local_maps, above, below, conv_weight, local_inner, back_cols)
    summed, terms = back_rows(row_inv, back, inner, out_cotangent, mix_part, token)
    terms = terms.reshape(256, 2, 128)
    terms = lax.all_to_all(terms, ("rows", "img"), split_axis=0, concat_axis=0, tiled=True)
    global_out = project_out(summed, out_weight)
    total = jnp.sum(terms, axis=0)
    mix_grad = total[0].reshape(128, 1)
    out_grad = total[1, 0:SPEC_CH].reshape(SPEC_CH, 1)
    return (local_out, global_out, mix_grad, out_grad)


def solution(mesh):
    maps = P("img", "rows", None, None)
    in_specs = (maps, maps, P(), P(), P(), P(), maps)
    out_specs = (maps, maps, P(None, "rows"), P(None, "rows"))
    return jax.shard_map(shards, mesh=mesh, in_specs=in_specs, out_specs=out_specs, check_vma=False)
```

```python
import math

import jax
import jax.numpy as jnp
import ml_dtypes
import numpy as np
from jax import lax
from jax.experimental import pallas as pl
from jax.experimental.pallas import tpu as pltpu
from jax.sharding import PartitionSpec as P

HEIGHT = 1024
WIDTH = 1024
SPEC_CH = 64
FREQS = 512
ROWS = 8
GROUPS = 128
PER_GROUP = 4
PAIR = 128
BF16 = jnp.bfloat16
F32 = jnp.float32

LIMIT = 60 * 2**20
SMALL = 40 * 2**20


def params(limit=LIMIT):
    return pltpu.CompilerParams(vmem_limit_bytes=limit)


def in_hbm(x):
    return pltpu.with_memory_space_constraint(x, pltpu.HBM)


VMEM = pl.BlockSpec(memory_space=pltpu.VMEM)


ANY = pl.BlockSpec(memory_space=pl.ANY)


def cost(flops, nbytes):
    return pl.CostEstimate(flops=flops, bytes_accessed=nbytes, transcendentals=0)


FIRSTS = ((0, 4), (1, 7), (2, 6), (3, 5))


def row_tables():
    s = np.arange(128)
    forward = np.zeros((4, 2, 16, 2, PER_GROUP, 2, 128))
    inverse = np.zeros((4, 2, 128, 2, 16, 2, PER_GROUP))
    for b, firsts in enumerate(FIRSTS):
        for half, k0 in enumerate(firsts):
            k = k0 + 8 * np.arange(64).reshape(16, PER_GROUP, 1)
            phase = (k * s % WIDTH) * (2.0 * math.pi / WIDTH)
            cosine, sine = np.cos(phase) / 32.0, np.sin(phase) / 32.0
            factor = np.where(k == 0, 1.0, 2.0)
            sign = 1.0 if half else -1.0
            if b == 0:
                forward[b, half, :, 0, :, half] = cosine
                forward[b, half, :, 1, :, half] = -sine
                inverse[b, half, :, half, :, 0] = (cosine * factor).transpose(2, 0, 1)
                inverse[b, half, :, half, :, 1] = (-sine * factor).transpose(2, 0, 1)
                continue
            forward[b, half, :, 0, :, 0] = cosine
            forward[b, half, :, 0, :, 1] = sign * sine
            forward[b, half, :, 1, :, 0] = -sine
            forward[b, half, :, 1, :, 1] = sign * cosine
            inverse[b, 0, :, half, :, 0] = (cosine * factor).transpose(2, 0, 1)
            inverse[b, 0, :, half, :, 1] = (-sine * factor).transpose(2, 0, 1)
            inverse[b, 1, :, half, :, 0] = (-sign * sine * factor).transpose(2, 0, 1)
            inverse[b, 1, :, half, :, 1] = (-sign * cosine * factor).transpose(2, 0, 1)
    forward = forward.reshape(4, 256, 256).astype(ml_dtypes.bfloat16)
    return forward, inverse.reshape(4, 256, 256).astype(ml_dtypes.bfloat16)


def column_tables():
    idx = np.arange(GROUPS)
    phase = ((idx[:, None] * idx[None, :]) % GROUPS) * (2.0 * math.pi / GROUPS)
    cosine, sine = np.cos(phase) / math.sqrt(HEIGHT), np.sin(phase) / math.sqrt(HEIGHT)
    forward = np.block([[cosine, sine], [-sine, cosine]])
    backward = np.block([[cosine, -sine], [sine, cosine]])
    turn = (idx[:, None] * np.arange(ROWS)[None, :]) * (2.0 * math.pi / HEIGHT)
    twiddle = np.repeat(np.stack([np.cos(turn), np.sin(turn)]), SPEC_CH, axis=2)
    return (
        forward.astype(ml_dtypes.bfloat16),
        backward.astype(ml_dtypes.bfloat16),
        twiddle.astype(np.float32),
    )


def dot(a, b):
    return jnp.dot(a, b, preferred_element_type=F32)


def dot_t(a, b):
    return lax.dot_general(a, b, (((0,), (0,)), ((), ())), preferred_element_type=F32)


def iota(shape, dim):
    return lax.broadcasted_iota(jnp.int32, shape, dim)


def first_half():
    return jnp.where(iota((SPEC_CH, PAIR), 0) == iota((SPEC_CH, PAIR), 1), 1.0, 0.0).astype(BF16)


def second_half():
    hit = iota((SPEC_CH, PAIR), 0) + SPEC_CH == iota((SPEC_CH, PAIR), 1)
    return jnp.where(hit, 1.0, 0.0).astype(BF16)


ROOT = math.sqrt(0.5)
RB = 16


def eight_points(x):
    a = [x[r] + x[r + 4] for r in range(4)]
    b = [x[r] - x[r + 4] for r in range(4)]
    even, odd = a[0] + a[2], a[1] + a[3]
    c, d = (b[1] - b[3]) * ROOT, (b[1] + b[3]) * ROOT
    return (
        (even + odd, even - odd),
        (b[0] + c, d + b[2]),
        (a[0] - a[2], a[1] - a[3]),
        (b[0] - c, d - b[2]),
    )


def eight_back(u):
    (u0, u4), (p1, q1), (p2, q2), (p3, q3) = u
    total, rest = u0 + u4, u0 - u4
    even = (total + p2, rest - q2, total - p2, rest + q2)
    c, d = (p1 - p3) * ROOT, (q1 + q3) * ROOT
    odd = (p1 + p3, c - d, q3 - q1, -c - d)
    return [even[r] + odd[r] for r in range(4)] + [even[r] - odd[r] for r in range(4)]


def rows_kernel(
    maps, cot, in_w, out_w, table, spec_out, inner_out,
    pairs, held, part, inner, eights, result, in_pair, out_pair, sems, table_sem, out_sems,
):
    half = ROWS * SPEC_CH
    loads = []
    for p in range(4):
        for n, source in enumerate((maps, cot)):
            rows = source.at[0, pl.ds(2 * p, 2)]
            loads.append(pltpu.make_async_copy(rows, pairs.at[p, n], sems.at[p, n]))
    table_load = pltpu.make_async_copy(table, held, table_sem)
    def start(i):
        p, n = (i % 4, i // 4)
        loads[2 * p + n].start()

    for i in range(8):
        start(i)
    table_load.start()
    a, b = first_half(), second_half()
    in_pair[0:PAIR, :] = dot_t(in_w[...], a).astype(BF16)
    in_pair[PAIR:, :] = dot_t(in_w[...], b).astype(BF16)
    out_pair[0:PAIR, :] = (2.0 * dot_t(out_w[...], a)).astype(BF16)
    out_pair[PAIR:, :] = (2.0 * dot_t(out_w[...], b)).astype(BF16)
    def project(i):
        p, n = (i % 4, i // 4)
        loads[2 * p + n].wait()
        if i + 8 < 8:
            start(i + 8)
        pair = jnp.concatenate([pairs[p, n, 0], pairs[p, n, 1]], axis=1)
        part[i % 2] = dot(pair, out_pair[...] if n else in_pair[...])

    project(0)
    for i in range(8):
        p, n = (i % 4, i // 4)
        if i < 7:
            project(i + 1)
        lanes = slice(n * half + p * PAIR, n * half + (p + 1) * PAIR)

        @pl.loop(0, 128, step=RB, unroll=True)
        def _(rows):
            rows = pl.multiple_of(rows, RB)
            x = [part[i % 2, pl.ds(128 * r + rows, RB), :] for r in range(8)]
            if n == 0:
                x = [jnp.maximum(v, 0.0) for v in x]
                for r in range(8):
                    inner[pl.ds(128 * r + rows, RB), lanes] = x[r].astype(BF16)
            for block, both in enumerate(eight_points(x)):
                for k in range(2):
                    eights[block, pl.ds(128 * k + rows, RB), lanes] = both[k].astype(BF16)

    stores = [pltpu.make_async_copy(inner, inner_out, out_sems.at[4])]
    stores[0].start()
    table_load.wait()
    for b in range(4):
        rows = pl.ds(b * 256, 256)
        prod = dot(held[b], eights[b])
        result[rows, 0:half] = prod[:, 0:half].astype(BF16)
        if b == 0:
            row = iota((256, half), 0)
            factor = jnp.where((row == 0) | (row == PER_GROUP), 0.5, 1.0)
            result[rows, half:] = (prod[:, half:] * factor).astype(BF16)
        else:
            result[rows, half:] = prod[:, half:].astype(BF16)
        stores.append(pltpu.make_async_copy(result.at[rows], spec_out.at[rows], out_sems.at[b]))
        stores[-1].start()
    for copy in stores:
        copy.wait()


def rows_forward(maps, cot, in_w, out_w, table):
    return pl.pallas_call(
        rows_kernel,
        grid=(1,),
        in_specs=[ANY, ANY, whole_spec((SPEC_CH, 128)), whole_spec((SPEC_CH, 128)), ANY],
        out_specs=[ANY, ANY],
        out_shape=[
            pltpu.HBM((1024, 1024), BF16),
            pltpu.HBM((WIDTH, 512), BF16),
        ],
        scratch_shapes=[
            pltpu.VMEM((4, 2, 2, WIDTH, 128), BF16),
            pltpu.VMEM((4, 256, 256), BF16),
            pltpu.VMEM((2, WIDTH, PAIR), F32),
            pltpu.VMEM((WIDTH, 512), BF16),
            pltpu.VMEM((4, 256, 1024), BF16),
            pltpu.VMEM((1024, 1024), BF16),
            pltpu.VMEM((256, PAIR), BF16),
            pltpu.VMEM((256, PAIR), BF16),
            pltpu.SemaphoreType.DMA((4, 2)),
            pltpu.SemaphoreType.DMA,
            pltpu.SemaphoreType.DMA((5,)),
        ],
        compiler_params=params(),
        cost_estimate=cost(5 * 10**9, 11 * 2**20),
    )(maps, cot, in_w, out_w, table)


def lane_signs(shape):
    return jnp.where(iota(shape, 1) % PAIR < SPEC_CH, 1.0, -1.0).astype(F32)


def lane_butterfly(x, signs):
    return pltpu.roll(x, SPEC_CH, 1) + x * signs


def turn_second(re, im, first, real, imag):
    new_re = jnp.where(first, re, re * real - im * imag)
    new_im = jnp.where(first, im, re * imag + im * real)
    return new_re, new_im


EIGHTHS = ((1.0, 0.0), (ROOT, -ROOT), (0.0, -1.0), (-ROOT, -ROOT))


def spectrum_rows(prod, twiddle, rows, signs, first):
    re, im = [], []
    for m in range(4):
        lanes = slice(m * PAIR, (m + 1) * PAIR)
        a = prod[pl.ds(rows, RB), lanes]
        b = prod[pl.ds(GROUPS + rows, RB), lanes]
        c = twiddle[0, pl.ds(rows, RB), lanes]
        s = twiddle[1, pl.ds(rows, RB), lanes]
        re.append(a * c + b * s)
        im.append(b * c - a * s)
    s0r, s0i, d0r, d0i = re[0] + re[2], im[0] + im[2], re[0] - re[2], im[0] - im[2]
    s1r, s1i, d1r, d1i = re[1] + re[3], im[1] + im[3], re[1] - re[3], im[1] - im[3]
    four = (
        (s0r + s1r, s0i + s1i),
        (d0r + d1i, d0i - d1r),
        (s0r - s1r, s0i - s1i),
        (d0r - d1i, d0i + d1r),
    )
    out = []
    for q in range(4):
        zr, zi = four[q]
        if q:
            zr, zi = turn_second(zr, zi, first, *EIGHTHS[q])
        out.append((lane_butterfly(zr, signs), lane_butterfly(zi, signs)))
    return out


def inverse_rows(parts, twiddle, rows, signs, first):
    z = []
    for q in range(4):
        zr, zi = (lane_butterfly(x, signs) for x in parts[q])
        if q:
            zr, zi = turn_second(zr, zi, first, EIGHTHS[q][0], -EIGHTHS[q][1])
        z.append((zr, zi))
    s0r, s0i = z[0][0] + z[2][0], z[0][1] + z[2][1]
    d0r, d0i = z[0][0] - z[2][0], z[0][1] - z[2][1]
    s1r, s1i = z[1][0] + z[3][0], z[1][1] + z[3][1]
    d1r, d1i = z[1][0] - z[3][0], z[1][1] - z[3][1]
    four = (
        (s0r + s1r, s0i + s1i),
        (d0r - d1i, d0i + d1r),
        (s0r - s1r, s0i - s1i),
        (d0r + d1i, d0i - d1r),
    )
    out = []
    for m in range(4):
        lanes = slice(m * PAIR, (m + 1) * PAIR)
        c = twiddle[0, pl.ds(rows, RB), lanes]
        s = twiddle[1, pl.ds(rows, RB), lanes]
        a, b = four[m]
        out.append((a * c - b * s, b * c + a * s))
    return out


def fill_mix(mix_w, wide):
    total = jnp.zeros((256, 256), F32)
    for t in range(2):
        row, col = iota((256, 128), 0), iota((256, 128), 1)
        at = (row // PAIR) * SPEC_CH + row % SPEC_CH
        hit = (at == col) & (row // SPEC_CH % 2 == t)
        pick = jnp.where(hit, 1.0, 0.0).astype(BF16)
        left = dot(pick, mix_w[...]).astype(BF16)
        total = total + lax.dot_general(
            left, pick, (((1,), (1,)), ((), ())), preferred_element_type=F32
        )
    wide[...] = total.astype(BF16)


def sigmoid(x):
    return 0.5 * jnp.tanh(0.5 * x) + 0.5


def gather_parts(stage, kk):
    lanes = []
    for m in range(4):
        re = stage[m, pl.ds(kk, GROUPS, stride=ROWS), :]
        im = stage[m, pl.ds(PER_GROUP + kk, GROUPS, stride=ROWS), :]
        lanes.append(jnp.concatenate([re, im], axis=0).astype(BF16))
    return jnp.concatenate(lanes, axis=1)


def fill_stage(block, stage):
    for m in range(4):
        stage[m] = block[:, m * PAIR : (m + 1) * PAIR].astype(F32)


def columns_kernel(
    block, forward_in, backward_in, twiddle_in, mix_in, ready, above, below, spec_out, back_out,
    land, forward, backward, twiddle, mix_w, spec, stage, back, wide, prod, pre, inv, sems, out_sems,
):
    del ready, above, below
    mix_load = pltpu.make_async_copy(mix_in, mix_w, sems.at[4])
    forward_load = pltpu.make_async_copy(forward_in, forward, sems.at[5])
    twiddle_load = pltpu.make_async_copy(twiddle_in, twiddle, sems.at[6])
    backward_load = pltpu.make_async_copy(backward_in, backward, sems.at[7])
    for copy in (mix_load, forward_load, twiddle_load, backward_load):
        copy.start()
    for m in range(4):
        stage[m] = block[:, m * PAIR : (m + 1) * PAIR].astype(F32)
    mix_load.wait()
    fill_mix(mix_w, wide)
    forward_load.wait()
    twiddle_load.wait()
    backward_load.wait()
    stores = []
    signs = lane_signs((RB, PAIR))
    first = iota((RB, PAIR), 1) < SPEC_CH
    def transform(kk):
        prod[kk % 2] = dot(forward[...], gather_parts(stage, kk))

    def spectrum(kk):
        @pl.loop(0, GROUPS, step=RB, unroll=True)
        def _(rows):
            rows = pl.multiple_of(rows, RB)
            parts = spectrum_rows(prod.at[kk % 2], twiddle, rows, signs, first)
            for q in range(4):
                spec[kk * 4 + q, pl.ds(rows, RB), 0:PAIR] = parts[q][0].astype(BF16)
                spec[kk * 4 + q, pl.ds(rows, RB), PAIR:] = parts[q][1].astype(BF16)

        part = pl.ds(kk * 4, 4)
        stores.append(pltpu.make_async_copy(spec.at[part], spec_out.at[part], out_sems.at[kk]))
        stores[-1].start()

    def mix(kk):
        pre[kk % 2] = dot(spec[kk * 4 : kk * 4 + 4].reshape(512, 256), wide[...])

    def activate(kk):
        @pl.loop(0, GROUPS, step=RB, unroll=True)
        def _(rows):
            rows = pl.multiple_of(rows, RB)
            parts = []
            for q in range(4):
                v = pre[kk % 2, pl.ds(q * GROUPS + rows, RB), :]
                v = v * sigmoid(v)
                parts.append((v[:, 0:PAIR], v[:, PAIR:]))
            pairs = inverse_rows(parts, twiddle, rows, signs, first)
            for m in range(4):
                lanes = slice(m * PAIR, (m + 1) * PAIR)
                inv[kk % 2, pl.ds(rows, RB), lanes] = pairs[m][0].astype(BF16)
                inv[kk % 2, pl.ds(GROUPS + rows, RB), lanes] = pairs[m][1].astype(BF16)

    def transform_back(kk):
        result = dot(backward[...], inv[kk % 2])
        for m in range(4):
            lanes = slice(m * PAIR, (m + 1) * PAIR)
            back[m, pl.ds(kk, GROUPS, stride=ROWS), :] = result[0:GROUPS, lanes]
            back[m, pl.ds(PER_GROUP + kk, GROUPS, stride=ROWS), :] = result[GROUPS:, lanes]

    transform(0)
    for kk in range(PER_GROUP + 2):
        if kk + 1 < PER_GROUP:
            transform(kk + 1)
        if kk < PER_GROUP:
            spectrum(kk)
        if 0 <= kk - 1 < PER_GROUP:
            activate(kk - 1)
        if kk < PER_GROUP:
            mix(kk)
        if 0 <= kk - 1 < PER_GROUP:
            transform_back(kk - 1)
    for m in range(4):
        land[:, m * PAIR : (m + 1) * PAIR] = back[m].astype(BF16)
        lanes = pl.ds(m * PAIR, PAIR)
        copy = pltpu.make_async_copy(land.at[:, lanes], back_out.at[:, lanes], out_sems.at[4 + m])
        copy.start()
        stores.append(copy)
    for copy in stores:
        copy.wait()


def whole_spec(shape):
    return pl.BlockSpec(shape, lambda *_: (0,) * len(shape))


def columns(block, forward, backward, twiddle, mix_w, ready, above, below):
    return pl.pallas_call(
        columns_kernel,
        in_specs=[VMEM] + [ANY] * 7,
        out_specs=[ANY, ANY],
        out_shape=[
            pltpu.HBM((16, GROUPS, 256), BF16),
            pltpu.HBM((1024, 512), BF16),
        ],
        scratch_shapes=[
            pltpu.VMEM((1024, 512), BF16),
            pltpu.VMEM((256, 256), BF16),
            pltpu.VMEM((256, 256), BF16),
            pltpu.VMEM((2, GROUPS, 512), F32),
            pltpu.VMEM((128, 128), BF16),
            pltpu.VMEM((16, GROUPS, 256), BF16),
            pltpu.VMEM((4, 1024, PAIR), F32),
            pltpu.VMEM((4, 1024, PAIR), F32),
            pltpu.VMEM((256, 256), BF16),
            pltpu.VMEM((2, 256, 512), F32),
            pltpu.VMEM((2, 512, 256), F32),
            pltpu.VMEM((2, 256, 512), BF16),
            pltpu.SemaphoreType.DMA((8,)),
            pltpu.SemaphoreType.DMA((8,)),
        ],
        compiler_params=params(SMALL),
        cost_estimate=cost(8 * 10**9, 5 * 2**20),
    )(block, forward, backward, twiddle, mix_w, in_hbm(ready), above, below)


def mix_kernel(block, spec, forward, twiddle, mix_w, grad, stage, wide, prod, pre, slope, acc):
    fill_mix(mix_w, wide)
    fill_stage(block, stage)
    signs = lane_signs((RB, PAIR))
    first = iota((RB, PAIR), 1) < SPEC_CH
    acc[...] = jnp.zeros_like(acc)
    for kk in range(PER_GROUP):
        prod[...] = dot(forward[...], gather_parts(stage, kk))
        pre[...] = dot(spec[kk * 4 : kk * 4 + 4].reshape(512, 256), wide[...])

        @pl.loop(0, GROUPS, step=RB, unroll=True)
        def _(rows):
            rows = pl.multiple_of(rows, RB)
            parts = spectrum_rows(prod, twiddle, rows, signs, first)
            for q in range(4):
                for part in range(2):
                    lanes = slice(part * PAIR, (part + 1) * PAIR)
                    v = pre[pl.ds(q * GROUPS + rows, RB), lanes]
                    s = sigmoid(v)
                    v = parts[q][part] * (s * (1.0 + v * (1.0 - s)))
                    slope[pl.ds(q * GROUPS + rows, RB), lanes] = v.astype(BF16)

        acc[...] += dot_t(slope[...], spec[kk * 4 : kk * 4 + 4].reshape(512, 256))
    lane = iota((SPEC_CH, PAIR), 1) < SPEC_CH
    for part in range(2):
        even = acc[part * PAIR : part * PAIR + SPEC_CH, :]
        odd = acc[part * PAIR + SPEC_CH : (part + 1) * PAIR, :]
        real = even[:, 0:PAIR] + pltpu.roll(odd[:, 0:PAIR], SPEC_CH, 1)
        imag = pltpu.roll(even[:, PAIR:], SPEC_CH, 1) + odd[:, PAIR:]
        grad[part * SPEC_CH : (part + 1) * SPEC_CH, :] = jnp.where(lane, real, imag)


def mix_terms(block, spec, forward, twiddle, mix_w):
    return pl.pallas_call(
        mix_kernel,
        grid=(1,),
        in_specs=[
            pl.BlockSpec((1024, 512), lambda i: (0, 1)),
            whole_spec((16, GROUPS, 256)),
            whole_spec((256, 256)),
            whole_spec((2, GROUPS, 512)),
            whole_spec((128, 128)),
        ],
        out_specs=whole_spec((128, 128)),
        out_shape=jax.ShapeDtypeStruct((128, 128), F32),
        scratch_shapes=[
            pltpu.VMEM((4, 1024, PAIR), F32),
            pltpu.VMEM((256, 256), BF16),
            pltpu.VMEM((256, 512), F32),
            pltpu.VMEM((512, 256), F32),
            pltpu.VMEM((512, 256), BF16),
            pltpu.VMEM((256, 256), F32),
        ],
        compiler_params=params(),
        cost_estimate=cost(6 * 10**9, 5 * 2**20),
    )(block, spec, forward, twiddle, mix_w)


def back_kernel(
    table, block, inner, cot, mix_part, ready, summed_out, terms_out,
    held, inners, cots, mix, summed, terms, packed, parts, sems, out_sems,
):
    del ready

    def load(source, target, sem):
        copy = pltpu.make_async_copy(source, target, sems.at[sem])
        copy.start()
        return copy

    first = load(table, held, 0)
    second = load(inner, inners, 1)
    pairs = [load(cot.at[0, pl.ds(2 * p, 2)], cots.at[p], 2 + p) for p in range(4)]
    last = load(mix_part, mix, 6)
    first.wait()
    for b in range(4):
        parts[b] = dot(held[b], block[b * 256 : (b + 1) * 256, :])
    second.wait()
    acc = jnp.zeros((PAIR, 256), F32)
    for p in range(4):
        lanes = slice(p * PAIR, (p + 1) * PAIR)

        @pl.loop(0, 128, step=RB, unroll=True)
        def _(rows):
            rows = pl.multiple_of(rows, RB)
            u = [
                [parts[b, pl.ds(128 * i + rows, RB), lanes] for i in range(2)] for b in range(4)
            ]
            for r, x in enumerate(eight_back(u)):
                at = pl.ds(128 * r + rows, RB)
                summed[at, lanes] = (x + inners[at, lanes].astype(F32)).astype(BF16)

        pairs[p].wait()
        pair = jnp.concatenate([cots[p, 0], cots[p, 1]], axis=1)
        acc = acc + dot_t(summed[:, lanes], pair)
    store = pltpu.make_async_copy(summed, summed_out, out_sems.at[0])
    store.start()
    last.wait()
    out_part = acc[0:SPEC_CH, 0:128] + acc[SPEC_CH:, 128:]
    out_part = jnp.concatenate([out_part, jnp.zeros((SPEC_CH, 128), F32)], axis=0).T
    for img in range(2):
        terms[pl.ds(2 * img, 128, stride=4), :] = mix[...]
        terms[pl.ds(2 * img + 1, 128, stride=4), :] = out_part
    packed[...] = terms[...].astype(BF16)
    copy = pltpu.make_async_copy(packed, terms_out, out_sems.at[1])
    copy.start()
    store.wait()
    copy.wait()


def back_rows(table, rows, inner, cot, mix_part, ready):
    return pl.pallas_call(
        back_kernel,
        in_specs=[ANY, VMEM, ANY, ANY, ANY, ANY],
        out_specs=[ANY, ANY],
        out_shape=[
            pltpu.HBM((WIDTH, 512), BF16),
            pltpu.HBM((512, 128), BF16),
        ],
        scratch_shapes=[
            pltpu.VMEM((4, 256, 256), BF16),
            pltpu.VMEM((WIDTH, 512), BF16),
            pltpu.VMEM((4, 2, WIDTH, 128), BF16),
            pltpu.VMEM((128, 128), F32),
            pltpu.VMEM((WIDTH, 512), BF16),
            pltpu.VMEM((512, 128), F32),
            pltpu.VMEM((512, 128), BF16),
            pltpu.VMEM((4, 256, 512), F32),
            pltpu.SemaphoreType.DMA((7,)),
            pltpu.SemaphoreType.DMA((2,)),
        ],
        compiler_params=params(SMALL),
        cost_estimate=cost(2 * 10**9, 8 * 2**20),
    )(in_hbm(table), rows, in_hbm(inner), in_hbm(cot), in_hbm(mix_part), in_hbm(ready))


def out_kernel(summed, out_w, out, wide):
    @pl.when(pl.program_id(0) == 0)
    def _():
        zero = jnp.zeros((SPEC_CH, 128), BF16)
        wide[0:SPEC_CH, :] = jnp.concatenate([out_w[...], zero], axis=1)
        wide[SPEC_CH:, :] = jnp.concatenate([zero, out_w[...]], axis=1)

    for p in range(4):
        prod = dot(summed[:, p * PAIR : (p + 1) * PAIR], wide[...]).astype(BF16)
        out[0, 2 * p] = prod[:, 0:128]
        out[0, 2 * p + 1] = prod[:, 128:]


def project_out(summed, out_w):
    return pl.pallas_call(
        out_kernel,
        grid=(4,),
        in_specs=[pl.BlockSpec((256, 512), lambda i: (i, 0)), whole_spec((SPEC_CH, 128))],
        out_specs=pl.BlockSpec((1, ROWS, 256, 128), lambda i: (0, 0, i, 0)),
        out_shape=jax.ShapeDtypeStruct((1, ROWS, WIDTH, 128), BF16),
        scratch_shapes=[pltpu.VMEM((128, 256), BF16)],
        compiler_params=params(),
        cost_estimate=cost(5 * 10**8, 3 * 2**20),
    )(summed, out_w)


def conv_row(top, mid, bottom, weight, out, token, sums, wide):
    @pl.when(pl.program_id(0) == 0)
    def _():
        token[...] = jnp.zeros((8, 128), F32)
        for a in range(3):
            for b in range(3):
                wide[a * 128 : (a + 1) * 128, b * 128 : (b + 1) * 128] = weight[a, b]
        sums[0, 0:8] = jnp.zeros((8, 128), F32)
        sums[2, WIDTH + 8 :] = jnp.zeros((8, 128), F32)

    prod = dot(jnp.concatenate([top, mid, bottom], axis=1), wide[...])
    for b in range(3):
        sums[b, 8 : WIDTH + 8] = prod[:, b * 128 : (b + 1) * 128]
    total = sums[0, 7 : WIDTH + 7] + sums[1, 8 : WIDTH + 8] + sums[2, 9 : WIDTH + 9]
    out[0, 0] = total.astype(BF16)


def inner_kernel(above, mid, below, weight, ready, out, token, sums, wide):
    del ready
    conv_row(above[0, 0], mid[0, 0], below[0, 0], weight, out, token, sums, wide)


def edge_kernel(mid, beside, edge_above, edge_below, weight, done, ready, out, token, sums, wide):
    del done, ready
    first = pl.program_id(0) == 0
    top = jnp.where(first, edge_above[0, 0], beside[0, 0])
    bottom = jnp.where(first, beside[0, 0], edge_below[0, 0])
    conv_row(top, mid[0, 0], bottom, weight, out, token, sums, wide)


def row_spec(index):
    return pl.BlockSpec((1, 1, WIDTH, 128), lambda i: (0, index(i), 0, 0))


def conv_call(kernel, rows, in_specs, out_index, aliases, args):
    return pl.pallas_call(
        kernel,
        grid=(rows,),
        in_specs=in_specs,
        out_specs=[row_spec(out_index), whole_spec((8, 128))],
        out_shape=[
            pltpu.HBM((1, ROWS, WIDTH, 128), BF16),
            jax.ShapeDtypeStruct((8, 128), F32),
        ],
        scratch_shapes=[pltpu.VMEM((3, WIDTH + 16, 128), F32), pltpu.VMEM((384, 384), BF16)],
        input_output_aliases=aliases,
        compiler_params=params(),
        cost_estimate=cost(rows * 10**9, rows * 2**20),
    )(*args)


def inner_rows(cells, weight, ready):
    specs = [
        row_spec(lambda i: i),
        row_spec(lambda i: i + 1),
        row_spec(lambda i: i + 2),
        whole_spec((3, 3, 128, 128)),
        pl.BlockSpec(memory_space=pl.ANY),
    ]
    args = (cells, cells, cells, weight, ready)
    return conv_call(inner_kernel, ROWS - 2, specs, lambda i: i + 1, {}, args)


def neighbour_rows(cells):
    ends = GROUPS - 1
    head, tail = cells[:, 0:1], cells[:, ROWS - 1 :]
    above = lax.ppermute(tail, "rows", [(i, i + 1) for i in range(ends)])
    below = lax.ppermute(head, "rows", [(i + 1, i) for i in range(ends)])
    return above, below


def edge_rows(cells, above, below, weight, done, ready):
    specs = [
        row_spec(lambda i: i * (ROWS - 1)),
        row_spec(lambda i: 1 + i * (ROWS - 3)),
        whole_spec((1, 1, WIDTH, 128)),
        whole_spec((1, 1, WIDTH, 128)),
        whole_spec((3, 3, 128, 128)),
        pl.BlockSpec(memory_space=pl.ANY),
        pl.BlockSpec(memory_space=pl.ANY),
    ]
    args = (cells, cells, above, below, weight, done, ready)
    return conv_call(edge_kernel, 2, specs, lambda i: i * (ROWS - 1), {5: 0}, args)


def exchange(block):
    lanes = block.shape[1]
    moved = lax.all_to_all(
        block.reshape(GROUPS, ROWS, lanes), "rows", split_axis=0, concat_axis=0, tiled=True
    )
    return moved.reshape(GROUPS * ROWS, lanes)


def shards(local_maps, global_maps, conv_weight, in_weight, mix_weight, out_weight, out_cotangent):
    row_fwd, row_inv = row_tables()
    forward, backward, twiddle = column_tables()
    spec_rows, inner = rows_forward(global_maps, out_cotangent, in_weight.T, out_weight, row_fwd)
    spec_cols = exchange(spec_rows)
    local_inner, token = inner_rows(local_maps, conv_weight, spec_rows)
    above, below = neighbour_rows(local_maps)
    spectrum, back_cols = columns(
        spec_cols, forward, backward, twiddle, mix_weight, token, above, below
    )
    back = exchange(back_cols)
    mix_part = mix_terms(spec_cols, spectrum, forward, twiddle, mix_weight)
    local_out, token = edge_rows(local_maps, above, below, conv_weight, local_inner, back_cols)
    summed, terms = back_rows(row_inv, back, inner, out_cotangent, mix_part, token)
    terms = terms.reshape(256, 2, 128)
    terms = lax.all_to_all(terms, ("rows", "img"), split_axis=0, concat_axis=0, tiled=True)
    global_out = project_out(summed, out_weight)
    total = jnp.sum(terms.astype(F32), axis=0)
    mix_grad = total[0].reshape(128, 1)
    out_grad = total[1, 0:SPEC_CH].reshape(SPEC_CH, 1)
    return (local_out, global_out, mix_grad, out_grad)


def solution(mesh):
    maps = P("img", "rows", None, None)
    in_specs = (maps, maps, P(), P(), P(), P(), maps)
    out_specs = (maps, maps, P(None, "rows"), P(None, "rows"))
    return jax.shard_map(shards, mesh=mesh, in_specs=in_specs, out_specs=out_specs, check_vma=False)
```

```python
import math

import jax
import jax.numpy as jnp
import ml_dtypes
import numpy as np
from jax import lax
from jax.experimental import pallas as pl
from jax.experimental.pallas import tpu as pltpu
from jax.sharding import PartitionSpec as P

HEIGHT = 1024
WIDTH = 1024
SPEC_CH = 64
FREQS = 512
ROWS = 8
GROUPS = 128
PER_GROUP = 4
PAIR = 128
BF16 = jnp.bfloat16
F32 = jnp.float32

LIMIT = 60 * 2**20
SMALL = 40 * 2**20


def params(limit=LIMIT):
    return pltpu.CompilerParams(vmem_limit_bytes=limit)


def in_hbm(x):
    return pltpu.with_memory_space_constraint(x, pltpu.HBM)


VMEM = pl.BlockSpec(memory_space=pltpu.VMEM)


ANY = pl.BlockSpec(memory_space=pl.ANY)


def cost(flops, nbytes):
    return pl.CostEstimate(flops=flops, bytes_accessed=nbytes, transcendentals=0)


FIRSTS = ((0, 4), (1, 7), (2, 6), (3, 5))


def row_tables():
    s = np.arange(128)
    forward = np.zeros((4, 2, 16, 2, PER_GROUP, 2, 128))
    inverse = np.zeros((4, 2, 128, 2, 16, 2, PER_GROUP))
    for b, firsts in enumerate(FIRSTS):
        for half, k0 in enumerate(firsts):
            k = k0 + 8 * np.arange(64).reshape(16, PER_GROUP, 1)
            phase = (k * s % WIDTH) * (2.0 * math.pi / WIDTH)
            cosine, sine = np.cos(phase) / 32.0, np.sin(phase) / 32.0
            factor = np.where(k == 0, 1.0, 2.0)
            sign = 1.0 if half else -1.0
            if b == 0:
                forward[b, half, :, 0, :, half] = cosine
                forward[b, half, :, 1, :, half] = -sine
                inverse[b, half, :, half, :, 0] = (cosine * factor).transpose(2, 0, 1)
                inverse[b, half, :, half, :, 1] = (-sine * factor).transpose(2, 0, 1)
                continue
            forward[b, half, :, 0, :, 0] = cosine
            forward[b, half, :, 0, :, 1] = sign * sine
            forward[b, half, :, 1, :, 0] = -sine
            forward[b, half, :, 1, :, 1] = sign * cosine
            inverse[b, 0, :, half, :, 0] = (cosine * factor).transpose(2, 0, 1)
            inverse[b, 0, :, half, :, 1] = (-sine * factor).transpose(2, 0, 1)
            inverse[b, 1, :, half, :, 0] = (-sign * sine * factor).transpose(2, 0, 1)
            inverse[b, 1, :, half, :, 1] = (-sign * cosine * factor).transpose(2, 0, 1)
    forward = forward.reshape(4, 256, 256).astype(ml_dtypes.bfloat16)
    return forward, inverse.reshape(4, 256, 256).astype(ml_dtypes.bfloat16)


def column_tables():
    idx = np.arange(GROUPS)
    phase = ((idx[:, None] * idx[None, :]) % GROUPS) * (2.0 * math.pi / GROUPS)
    cosine, sine = np.cos(phase) / math.sqrt(HEIGHT), np.sin(phase) / math.sqrt(HEIGHT)
    forward = np.block([[cosine, sine], [-sine, cosine]])
    backward = np.block([[cosine, -sine], [sine, cosine]])
    turn = (idx[:, None] * np.arange(ROWS)[None, :]) * (2.0 * math.pi / HEIGHT)
    twiddle = np.repeat(np.stack([np.cos(turn), np.sin(turn)]), SPEC_CH, axis=2)
    return (
        forward.astype(ml_dtypes.bfloat16),
        backward.astype(ml_dtypes.bfloat16),
        twiddle.astype(np.float32),
    )


def dot(a, b):
    return jnp.dot(a, b, preferred_element_type=F32)


def dot_t(a, b):
    return lax.dot_general(a, b, (((0,), (0,)), ((), ())), preferred_element_type=F32)


def iota(shape, dim):
    return lax.broadcasted_iota(jnp.int32, shape, dim)


def first_half():
    return jnp.where(iota((SPEC_CH, PAIR), 0) == iota((SPEC_CH, PAIR), 1), 1.0, 0.0).astype(BF16)


def second_half():
    hit = iota((SPEC_CH, PAIR), 0) + SPEC_CH == iota((SPEC_CH, PAIR), 1)
    return jnp.where(hit, 1.0, 0.0).astype(BF16)


ROOT = math.sqrt(0.5)
RB = 16


def eight_points(x):
    a = [x[r] + x[r + 4] for r in range(4)]
    b = [x[r] - x[r + 4] for r in range(4)]
    even, odd = a[0] + a[2], a[1] + a[3]
    c, d = (b[1] - b[3]) * ROOT, (b[1] + b[3]) * ROOT
    return (
        (even + odd, even - odd),
        (b[0] + c, d + b[2]),
        (a[0] - a[2], a[1] - a[3]),
        (b[0] - c, d - b[2]),
    )


def eight_back(u):
    (u0, u4), (p1, q1), (p2, q2), (p3, q3) = u
    total, rest = u0 + u4, u0 - u4
    even = (total + p2, rest - q2, total - p2, rest + q2)
    c, d = (p1 - p3) * ROOT, (q1 + q3) * ROOT
    odd = (p1 + p3, c - d, q3 - q1, -c - d)
    return [even[r] + odd[r] for r in range(4)] + [even[r] - odd[r] for r in range(4)]


def rows_kernel(
    maps, cot, in_w, out_w, table, spec_out, inner_out,
    pairs, held, part, inner, eights, result, in_pair, out_pair, sems, table_sem, out_sems,
):
    half = ROWS * SPEC_CH
    loads = []
    for p in range(4):
        for n, source in enumerate((maps, cot)):
            rows = source.at[0, pl.ds(2 * p, 2)]
            loads.append(pltpu.make_async_copy(rows, pairs.at[p, n], sems.at[p, n]))
    table_load = pltpu.make_async_copy(table, held, table_sem)
    def start(i):
        p, n = (i % 4, i // 4)
        loads[2 * p + n].start()

    for i in range(8):
        start(i)
    table_load.start()
    a, b = first_half(), second_half()
    in_pair[0:PAIR, :] = dot_t(in_w[...], a).astype(BF16)
    in_pair[PAIR:, :] = dot_t(in_w[...], b).astype(BF16)
    out_pair[0:PAIR, :] = (2.0 * dot_t(out_w[...], a)).astype(BF16)
    out_pair[PAIR:, :] = (2.0 * dot_t(out_w[...], b)).astype(BF16)
    def project(i):
        p, n = (i % 4, i // 4)
        loads[2 * p + n].wait()
        if i + 8 < 8:
            start(i + 8)
        pair = jnp.concatenate([pairs[p, n, 0], pairs[p, n, 1]], axis=1)
        part[i % 2] = dot(pair, out_pair[...] if n else in_pair[...])

    project(0)
    for i in range(8):
        p, n = (i % 4, i // 4)
        if i < 7:
            project(i + 1)
        lanes = slice(n * half + p * PAIR, n * half + (p + 1) * PAIR)

        @pl.loop(0, 128, step=RB, unroll=True)
        def _(rows):
            rows = pl.multiple_of(rows, RB)
            x = [part[i % 2, pl.ds(128 * r + rows, RB), :] for r in range(8)]
            if n == 0:
                x = [jnp.maximum(v, 0.0) for v in x]
                for r in range(8):
                    inner[pl.ds(128 * r + rows, RB), lanes] = x[r].astype(BF16)
            for block, both in enumerate(eight_points(x)):
                for k in range(2):
                    eights[block, pl.ds(128 * k + rows, RB), lanes] = both[k].astype(BF16)

    stores = [pltpu.make_async_copy(inner, inner_out, out_sems.at[4])]
    stores[0].start()
    table_load.wait()
    for b in range(4):
        rows = pl.ds(b * 256, 256)
        prod = dot(held[b], eights[b])
        result[rows, 0:half] = prod[:, 0:half].astype(BF16)
        if b == 0:
            row = iota((256, half), 0)
            factor = jnp.where((row == 0) | (row == PER_GROUP), 0.5, 1.0)
            result[rows, half:] = (prod[:, half:] * factor).astype(BF16)
        else:
            result[rows, half:] = prod[:, half:].astype(BF16)
        stores.append(pltpu.make_async_copy(result.at[rows], spec_out.at[rows], out_sems.at[b]))
        stores[-1].start()
    for copy in stores:
        copy.wait()


def rows_forward(maps, cot, in_w, out_w, table):
    return pl.pallas_call(
        rows_kernel,
        grid=(1,),
        in_specs=[ANY, ANY, whole_spec((SPEC_CH, 128)), whole_spec((SPEC_CH, 128)), ANY],
        out_specs=[ANY, ANY],
        out_shape=[
            pltpu.HBM((1024, 1024), BF16),
            pltpu.HBM((WIDTH, 512), BF16),
        ],
        scratch_shapes=[
            pltpu.VMEM((4, 2, 2, WIDTH, 128), BF16),
            pltpu.VMEM((4, 256, 256), BF16),
            pltpu.VMEM((2, WIDTH, PAIR), F32),
            pltpu.VMEM((WIDTH, 512), BF16),
            pltpu.VMEM((4, 256, 1024), BF16),
            pltpu.VMEM((1024, 1024), BF16),
            pltpu.VMEM((256, PAIR), BF16),
            pltpu.VMEM((256, PAIR), BF16),
            pltpu.SemaphoreType.DMA((4, 2)),
            pltpu.SemaphoreType.DMA,
            pltpu.SemaphoreType.DMA((5,)),
        ],
        compiler_params=params(),
        cost_estimate=cost(5 * 10**9, 11 * 2**20),
    )(maps, cot, in_w, out_w, table)


def lane_signs(shape):
    return jnp.where(iota(shape, 1) % PAIR < SPEC_CH, 1.0, -1.0).astype(F32)


def lane_butterfly(x, signs):
    return pltpu.roll(x, SPEC_CH, 1) + x * signs


def turn_second(re, im, first, real, imag):
    new_re = jnp.where(first, re, re * real - im * imag)
    new_im = jnp.where(first, im, re * imag + im * real)
    return new_re, new_im


EIGHTHS = ((1.0, 0.0), (ROOT, -ROOT), (0.0, -1.0), (-ROOT, -ROOT))


def spectrum_rows(prod, twiddle, rows, signs, first):
    re, im = [], []
    for m in range(4):
        lanes = slice(m * PAIR, (m + 1) * PAIR)
        a = prod[pl.ds(rows, RB), lanes]
        b = prod[pl.ds(GROUPS + rows, RB), lanes]
        c = twiddle[0, pl.ds(rows, RB), lanes]
        s = twiddle[1, pl.ds(rows, RB), lanes]
        re.append(a * c + b * s)
        im.append(b * c - a * s)
    s0r, s0i, d0r, d0i = re[0] + re[2], im[0] + im[2], re[0] - re[2], im[0] - im[2]
    s1r, s1i, d1r, d1i = re[1] + re[3], im[1] + im[3], re[1] - re[3], im[1] - im[3]
    four = (
        (s0r + s1r, s0i + s1i),
        (d0r + d1i, d0i - d1r),
        (s0r - s1r, s0i - s1i),
        (d0r - d1i, d0i + d1r),
    )
    out = []
    for q in range(4):
        zr, zi = four[q]
        if q:
            zr, zi = turn_second(zr, zi, first, *EIGHTHS[q])
        out.append((lane_butterfly(zr, signs), lane_butterfly(zi, signs)))
    return out


def inverse_rows(parts, twiddle, rows, signs, first):
    z = []
    for q in range(4):
        zr, zi = (lane_butterfly(x, signs) for x in parts[q])
        if q:
            zr, zi = turn_second(zr, zi, first, EIGHTHS[q][0], -EIGHTHS[q][1])
        z.append((zr, zi))
    s0r, s0i = z[0][0] + z[2][0], z[0][1] + z[2][1]
    d0r, d0i = z[0][0] - z[2][0], z[0][1] - z[2][1]
    s1r, s1i = z[1][0] + z[3][0], z[1][1] + z[3][1]
    d1r, d1i = z[1][0] - z[3][0], z[1][1] - z[3][1]
    four = (
        (s0r + s1r, s0i + s1i),
        (d0r - d1i, d0i + d1r),
        (s0r - s1r, s0i - s1i),
        (d0r + d1i, d0i - d1r),
    )
    out = []
    for m in range(4):
        lanes = slice(m * PAIR, (m + 1) * PAIR)
        c = twiddle[0, pl.ds(rows, RB), lanes]
        s = twiddle[1, pl.ds(rows, RB), lanes]
        a, b = four[m]
        out.append((a * c - b * s, b * c + a * s))
    return out


def fill_mix(mix_w, wide):
    total = jnp.zeros((256, 256), F32)
    for t in range(2):
        row, col = iota((256, 128), 0), iota((256, 128), 1)
        at = (row // PAIR) * SPEC_CH + row % SPEC_CH
        hit = (at == col) & (row // SPEC_CH % 2 == t)
        pick = jnp.where(hit, 1.0, 0.0).astype(BF16)
        left = dot(pick, mix_w[...]).astype(BF16)
        total = total + lax.dot_general(
            left, pick, (((1,), (1,)), ((), ())), preferred_element_type=F32
        )
    wide[...] = total.astype(BF16)


def sigmoid(x):
    return 0.5 * jnp.tanh(0.5 * x) + 0.5


def gather_parts(stage, kk):
    lanes = []
    for m in range(4):
        re = stage[m, pl.ds(kk, GROUPS, stride=ROWS), :]
        im = stage[m, pl.ds(PER_GROUP + kk, GROUPS, stride=ROWS), :]
        lanes.append(jnp.concatenate([re, im], axis=0).astype(BF16))
    return jnp.concatenate(lanes, axis=1)


def fill_stage(block, stage):
    for m in range(4):
        stage[m] = block[:, m * PAIR : (m + 1) * PAIR].astype(F32)


def columns_kernel(
    block, forward_in, backward_in, twiddle_in, mix_in, ready, above, below, spec_out, back_out,
    land, forward, backward, twiddle, mix_w, spec, stage, back, wide, prod, pre, inv, sems, out_sems,
):
    del ready, above, below
    mix_load = pltpu.make_async_copy(mix_in, mix_w, sems.at[4])
    forward_load = pltpu.make_async_copy(forward_in, forward, sems.at[5])
    twiddle_load = pltpu.make_async_copy(twiddle_in, twiddle, sems.at[6])
    backward_load = pltpu.make_async_copy(backward_in, backward, sems.at[7])
    for copy in (mix_load, forward_load, twiddle_load, backward_load):
        copy.start()
    for m in range(4):
        stage[m] = block[:, m * PAIR : (m + 1) * PAIR].astype(F32)
    mix_load.wait()
    fill_mix(mix_w, wide)
    forward_load.wait()
    twiddle_load.wait()
    backward_load.wait()
    stores = []
    signs = lane_signs((RB, PAIR))
    first = iota((RB, PAIR), 1) < SPEC_CH
    def transform(kk):
        prod[kk % 2] = dot(forward[...], gather_parts(stage, kk))

    def spectrum(kk):
        @pl.loop(0, GROUPS, step=RB, unroll=True)
        def _(rows):
            rows = pl.multiple_of(rows, RB)
            parts = spectrum_rows(prod.at[kk % 2], twiddle, rows, signs, first)
            for q in range(4):
                spec[kk * 4 + q, pl.ds(rows, RB), 0:PAIR] = parts[q][0].astype(BF16)
                spec[kk * 4 + q, pl.ds(rows, RB), PAIR:] = parts[q][1].astype(BF16)

        part = pl.ds(kk * 4, 4)
        stores.append(pltpu.make_async_copy(spec.at[part], spec_out.at[part], out_sems.at[kk]))
        stores[-1].start()

    def mix(kk):
        pre[kk % 2] = dot(spec[kk * 4 : kk * 4 + 4].reshape(512, 256), wide[...])

    def activate(kk):
        @pl.loop(0, GROUPS, step=RB, unroll=True)
        def _(rows):
            rows = pl.multiple_of(rows, RB)
            parts = []
            for q in range(4):
                v = pre[kk % 2, pl.ds(q * GROUPS + rows, RB), :]
                v = v * sigmoid(v)
                parts.append((v[:, 0:PAIR], v[:, PAIR:]))
            pairs = inverse_rows(parts, twiddle, rows, signs, first)
            for m in range(4):
                lanes = slice(m * PAIR, (m + 1) * PAIR)
                inv[kk % 2, pl.ds(rows, RB), lanes] = pairs[m][0].astype(BF16)
                inv[kk % 2, pl.ds(GROUPS + rows, RB), lanes] = pairs[m][1].astype(BF16)

    def transform_back(kk):
        result = dot(backward[...], inv[kk % 2])
        for m in range(4):
            lanes = slice(m * PAIR, (m + 1) * PAIR)
            back[m, pl.ds(kk, GROUPS, stride=ROWS), :] = result[0:GROUPS, lanes]
            back[m, pl.ds(PER_GROUP + kk, GROUPS, stride=ROWS), :] = result[GROUPS:, lanes]

    transform(0)
    for kk in range(PER_GROUP + 2):
        if kk + 1 < PER_GROUP:
            transform(kk + 1)
        if kk < PER_GROUP:
            spectrum(kk)
        if 0 <= kk - 1 < PER_GROUP:
            activate(kk - 1)
        if kk < PER_GROUP:
            mix(kk)
        if 0 <= kk - 1 < PER_GROUP:
            transform_back(kk - 1)
    for m in range(4):
        land[:, m * PAIR : (m + 1) * PAIR] = back[m].astype(BF16)
        lanes = pl.ds(m * PAIR, PAIR)
        copy = pltpu.make_async_copy(land.at[:, lanes], back_out.at[:, lanes], out_sems.at[4 + m])
        copy.start()
        stores.append(copy)
    for copy in stores:
        copy.wait()


def whole_spec(shape):
    return pl.BlockSpec(shape, lambda *_: (0,) * len(shape))


def columns(block, forward, backward, twiddle, mix_w, ready, above, below):
    return pl.pallas_call(
        columns_kernel,
        in_specs=[VMEM] + [ANY] * 7,
        out_specs=[ANY, ANY],
        out_shape=[
            pltpu.HBM((16, GROUPS, 256), BF16),
            pltpu.HBM((1024, 512), BF16),
        ],
        scratch_shapes=[
            pltpu.VMEM((1024, 512), BF16),
            pltpu.VMEM((256, 256), BF16),
            pltpu.VMEM((256, 256), BF16),
            pltpu.VMEM((2, GROUPS, 512), F32),
            pltpu.VMEM((128, 128), BF16),
            pltpu.VMEM((16, GROUPS, 256), BF16),
            pltpu.VMEM((4, 1024, PAIR), F32),
            pltpu.VMEM((4, 1024, PAIR), F32),
            pltpu.VMEM((256, 256), BF16),
            pltpu.VMEM((2, 256, 512), F32),
            pltpu.VMEM((2, 512, 256), F32),
            pltpu.VMEM((2, 256, 512), BF16),
            pltpu.SemaphoreType.DMA((8,)),
            pltpu.SemaphoreType.DMA((8,)),
        ],
        compiler_params=params(SMALL),
        cost_estimate=cost(8 * 10**9, 5 * 2**20),
    )(block, forward, backward, twiddle, mix_w, in_hbm(ready), above, below)


def mix_kernel(block, spec, forward, twiddle, mix_w, grad, stage, wide, prod, pre, slope, acc):
    fill_mix(mix_w, wide)
    fill_stage(block, stage)
    signs = lane_signs((RB, PAIR))
    first = iota((RB, PAIR), 1) < SPEC_CH
    acc[...] = jnp.zeros_like(acc)
    for kk in range(PER_GROUP):
        prod[...] = dot(forward[...], gather_parts(stage, kk))
        pre[...] = dot(spec[kk * 4 : kk * 4 + 4].reshape(512, 256), wide[...])

        @pl.loop(0, GROUPS, step=RB, unroll=True)
        def _(rows):
            rows = pl.multiple_of(rows, RB)
            parts = spectrum_rows(prod, twiddle, rows, signs, first)
            for q in range(4):
                for part in range(2):
                    lanes = slice(part * PAIR, (part + 1) * PAIR)
                    v = pre[pl.ds(q * GROUPS + rows, RB), lanes]
                    s = sigmoid(v)
                    v = parts[q][part] * (s * (1.0 + v * (1.0 - s)))
                    slope[pl.ds(q * GROUPS + rows, RB), lanes] = v.astype(BF16)

        acc[...] += dot_t(slope[...], spec[kk * 4 : kk * 4 + 4].reshape(512, 256))
    lane = iota((SPEC_CH, PAIR), 1) < SPEC_CH
    for part in range(2):
        even = acc[part * PAIR : part * PAIR + SPEC_CH, :]
        odd = acc[part * PAIR + SPEC_CH : (part + 1) * PAIR, :]
        real = even[:, 0:PAIR] + pltpu.roll(odd[:, 0:PAIR], SPEC_CH, 1)
        imag = pltpu.roll(even[:, PAIR:], SPEC_CH, 1) + odd[:, PAIR:]
        grad[part * SPEC_CH : (part + 1) * SPEC_CH, :] = jnp.where(lane, real, imag)


def mix_terms(block, spec, forward, twiddle, mix_w):
    return pl.pallas_call(
        mix_kernel,
        grid=(1,),
        in_specs=[
            pl.BlockSpec((1024, 512), lambda i: (0, 1)),
            whole_spec((16, GROUPS, 256)),
            whole_spec((256, 256)),
            whole_spec((2, GROUPS, 512)),
            whole_spec((128, 128)),
        ],
        out_specs=whole_spec((128, 128)),
        out_shape=jax.ShapeDtypeStruct((128, 128), F32),
        scratch_shapes=[
            pltpu.VMEM((4, 1024, PAIR), F32),
            pltpu.VMEM((256, 256), BF16),
            pltpu.VMEM((256, 512), F32),
            pltpu.VMEM((512, 256), F32),
            pltpu.VMEM((512, 256), BF16),
            pltpu.VMEM((256, 256), F32),
        ],
        compiler_params=params(),
        cost_estimate=cost(6 * 10**9, 5 * 2**20),
    )(block, spec, forward, twiddle, mix_w)


def back_kernel(
    table, block, inner, cot, mix_part, ready, summed_out, terms_out,
    held, inners, cots, mix, summed, terms, packed, parts, sems, out_sems,
):
    del ready

    def load(source, target, sem):
        copy = pltpu.make_async_copy(source, target, sems.at[sem])
        copy.start()
        return copy

    first = load(table, held, 0)
    second = load(inner, inners, 1)
    pairs = [load(cot.at[0, pl.ds(2 * p, 2)], cots.at[p], 2 + p) for p in range(4)]
    last = load(mix_part, mix, 6)
    first.wait()
    for b in range(4):
        parts[b] = dot(held[b], block[b * 256 : (b + 1) * 256, :])
    second.wait()
    acc = jnp.zeros((PAIR, 256), F32)
    for p in range(4):
        lanes = slice(p * PAIR, (p + 1) * PAIR)

        @pl.loop(0, 128, step=RB, unroll=True)
        def _(rows):
            rows = pl.multiple_of(rows, RB)
            u = [
                [parts[b, pl.ds(128 * i + rows, RB), lanes] for i in range(2)] for b in range(4)
            ]
            for r, x in enumerate(eight_back(u)):
                at = pl.ds(128 * r + rows, RB)
                summed[at, lanes] = (x + inners[at, lanes].astype(F32)).astype(BF16)

        pairs[p].wait()
        pair = jnp.concatenate([cots[p, 0], cots[p, 1]], axis=1)
        acc = acc + dot_t(summed[:, lanes], pair)
    store = pltpu.make_async_copy(summed, summed_out, out_sems.at[0])
    store.start()
    last.wait()
    out_part = acc[0:SPEC_CH, 0:128] + acc[SPEC_CH:, 128:]
    high = out_part.astype(BF16).astype(F32)
    out_both = jnp.concatenate([high, out_part - high], axis=0).T
    for img in range(2):
        terms[pl.ds(2 * img, 128, stride=4), :] = mix[...]
        terms[pl.ds(2 * img + 1, 128, stride=4), :] = out_both
    packed[...] = terms[...].astype(BF16)
    copy = pltpu.make_async_copy(packed, terms_out, out_sems.at[1])
    copy.start()
    store.wait()
    copy.wait()


def back_rows(table, rows, inner, cot, mix_part, ready):
    return pl.pallas_call(
        back_kernel,
        in_specs=[ANY, VMEM, ANY, ANY, ANY, ANY],
        out_specs=[ANY, ANY],
        out_shape=[
            pltpu.HBM((WIDTH, 512), BF16),
            pltpu.HBM((512, 128), BF16),
        ],
        scratch_shapes=[
            pltpu.VMEM((4, 256, 256), BF16),
            pltpu.VMEM((WIDTH, 512), BF16),
            pltpu.VMEM((4, 2, WIDTH, 128), BF16),
            pltpu.VMEM((128, 128), F32),
            pltpu.VMEM((WIDTH, 512), BF16),
            pltpu.VMEM((512, 128), F32),
            pltpu.VMEM((512, 128), BF16),
            pltpu.VMEM((4, 256, 512), F32),
            pltpu.SemaphoreType.DMA((7,)),
            pltpu.SemaphoreType.DMA((2,)),
        ],
        compiler_params=params(SMALL),
        cost_estimate=cost(2 * 10**9, 8 * 2**20),
    )(in_hbm(table), rows, in_hbm(inner), in_hbm(cot), in_hbm(mix_part), in_hbm(ready))


def out_kernel(summed, out_w, out, held, wide, result, sems, out_sems):
    loads = []
    for p in range(4):
        lanes = pl.ds(p * PAIR, PAIR)
        loads.append(pltpu.make_async_copy(summed.at[:, lanes], held.at[p], sems.at[p]))
        loads[p].start()
    zero = jnp.zeros((SPEC_CH, 128), BF16)
    wide[0:SPEC_CH, :] = jnp.concatenate([out_w[...], zero], axis=1)
    wide[SPEC_CH:, :] = jnp.concatenate([zero, out_w[...]], axis=1)
    stores = []
    for p in range(4):
        loads[p].wait()
        prod = dot(held[p], wide[...])
        result[2 * p] = prod[:, 0:128].astype(BF16)
        result[2 * p + 1] = prod[:, 128:].astype(BF16)
        rows = pl.ds(2 * p, 2)
        stores.append(pltpu.make_async_copy(result.at[rows], out.at[0, rows], out_sems.at[p]))
        stores[p].start()
    for copy in stores:
        copy.wait()


def project_out(summed, out_w):
    return pl.pallas_call(
        out_kernel,
        grid=(1,),
        in_specs=[ANY, whole_spec((SPEC_CH, 128))],
        out_specs=ANY,
        out_shape=pltpu.HBM((1, ROWS, WIDTH, 128), BF16),
        scratch_shapes=[
            pltpu.VMEM((4, WIDTH, PAIR), BF16),
            pltpu.VMEM((128, 256), BF16),
            pltpu.VMEM((ROWS, WIDTH, 128), BF16),
            pltpu.SemaphoreType.DMA((4,)),
            pltpu.SemaphoreType.DMA((4,)),
        ],
        compiler_params=params(),
        cost_estimate=cost(5 * 10**8, 3 * 2**20),
    )(summed, out_w)


def fill_wide(weight, wide, sums):
    for a in range(3):
        for b in range(3):
            wide[a * 128 : (a + 1) * 128, b * 128 : (b + 1) * 128] = weight[a, b]
    sums[0, 0:8] = jnp.zeros((8, 128), F32)
    sums[2, WIDTH + 8 :] = jnp.zeros((8, 128), F32)


def conv_sums(top, mid, bottom, sums, wide):
    prod = dot(jnp.concatenate([top, mid, bottom], axis=1), wide[...])
    for b in range(3):
        sums[b, 8 : WIDTH + 8] = prod[:, b * 128 : (b + 1) * 128]
    total = sums[0, 7 : WIDTH + 7] + sums[1, 8 : WIDTH + 8] + sums[2, 9 : WIDTH + 9]
    return total.astype(BF16)


def conv_row(top, mid, bottom, weight, out, token, sums, wide):
    @pl.when(pl.program_id(0) == 0)
    def _():
        token[...] = jnp.zeros((8, 128), F32)
        fill_wide(weight, wide, sums)

    out[0, 0] = conv_sums(top, mid, bottom, sums, wide)


def inner_kernel(above, mid, below, weight, ready, out, token, sums, wide):
    del ready
    conv_row(above[0, 0], mid[0, 0], below[0, 0], weight, out, token, sums, wide)


def edge_kernel(mid, beside, edge_above, edge_below, weight, done, ready, out, token, sums, wide):
    del done, ready
    first = pl.program_id(0) == 0
    top = jnp.where(first, edge_above[0, 0], beside[0, 0])
    bottom = jnp.where(first, beside[0, 0], edge_below[0, 0])
    conv_row(top, mid[0, 0], bottom, weight, out, token, sums, wide)


def sum_kernel(terms, mix, out):
    total = jnp.sum(terms[...].astype(F32).reshape(64, 8, 128), axis=0)
    even = iota((8, 128), 0) % 2 == 0
    mix[...] = jnp.sum(jnp.where(even, total, 0.0), axis=0, keepdims=True)
    odd = jnp.sum(jnp.where(even, 0.0, total), axis=0, keepdims=True)
    out[...] = odd[:, 0:SPEC_CH] + odd[:, SPEC_CH:]


def sum_terms(terms):
    return pl.pallas_call(
        sum_kernel,
        in_specs=[VMEM],
        out_specs=[VMEM, VMEM],
        out_shape=[
            jax.ShapeDtypeStruct((1, 128), F32),
            jax.ShapeDtypeStruct((1, SPEC_CH), F32),
        ],
        compiler_params=params(SMALL),
        cost_estimate=cost(10**6, 2**17),
    )(terms)


def row_spec(index):
    return pl.BlockSpec((1, 1, WIDTH, 128), lambda i: (0, index(i), 0, 0))


def conv_call(kernel, rows, in_specs, out_index, aliases, args):
    return pl.pallas_call(
        kernel,
        grid=(rows,),
        in_specs=in_specs,
        out_specs=[row_spec(out_index), whole_spec((8, 128))],
        out_shape=[
            pltpu.HBM((1, ROWS, WIDTH, 128), BF16),
            jax.ShapeDtypeStruct((8, 128), F32),
        ],
        scratch_shapes=[pltpu.VMEM((3, WIDTH + 16, 128), F32), pltpu.VMEM((384, 384), BF16)],
        input_output_aliases=aliases,
        compiler_params=params(),
        cost_estimate=cost(rows * 10**9, rows * 2**20),
    )(*args)


def inner_rows(cells, weight, ready):
    specs = [
        row_spec(lambda i: i),
        row_spec(lambda i: i + 1),
        row_spec(lambda i: i + 2),
        whole_spec((3, 3, 128, 128)),
        pl.BlockSpec(memory_space=pl.ANY),
    ]
    args = (cells, cells, cells, weight, ready)
    return conv_call(inner_kernel, ROWS - 2, specs, lambda i: i + 1, {}, args)


BLOCK = 8


def neighbour_rows(cells):
    head, tail = cells[:, 0:1], cells[:, ROWS - 1 :]
    near = [i for i in range(GROUPS - 1) if i % BLOCK != BLOCK - 1]
    above = lax.ppermute(tail, "rows", [(i, i + 1) for i in near])
    below = lax.ppermute(head, "rows", [(i + 1, i) for i in near])
    return above, below


def far_row(cells):
    last = lax.axis_index("rows") % BLOCK == BLOCK - 1
    row = lax.dynamic_slice_in_dim(cells, jnp.where(last, ROWS - 1, 0), 1, axis=1)
    far = range(BLOCK - 1, GROUPS - 1, BLOCK)
    return lax.ppermute(row, "rows", [(i, i + 1) for i in far] + [(i + 1, i) for i in far])


def edge_rows(cells, above, below, weight, done, ready):
    specs = [
        row_spec(lambda i: i * (ROWS - 1)),
        row_spec(lambda i: 1 + i * (ROWS - 3)),
        whole_spec((1, 1, WIDTH, 128)),
        whole_spec((1, 1, WIDTH, 128)),
        whole_spec((3, 3, 128, 128)),
        pl.BlockSpec(memory_space=pl.ANY),
        pl.BlockSpec(memory_space=pl.ANY),
    ]
    args = (cells, cells, above, below, weight, done, ready)
    return conv_call(edge_kernel, 2, specs, lambda i: i * (ROWS - 1), {5: 0}, args)


def far_kernel(cells, above, far, weight_in, done, ready, out, lines, weight, row_out, sums, wide, sems):
    del done, ready
    at = lax.axis_index("rows") % BLOCK
    last = at == BLOCK - 1
    row = jnp.where(last, ROWS - 1, 0)
    beside = jnp.where(last, ROWS - 2, 1)
    outer = jnp.where(last, 2, 0)
    weights = pltpu.make_async_copy(weight_in, weight, sems.at[0])
    weights.start()
    own = pltpu.make_async_copy(cells.at[0, row], lines.at[1], sems.at[1])
    own.start()
    inside = pltpu.make_async_copy(cells.at[0, beside], lines.at[2 - outer], sems.at[2])
    inside.start()

    @pl.when((at == 0) | last)
    def _():
        pltpu.make_async_copy(far.at[0, 0], lines.at[outer], sems.at[3]).start()

    @pl.when((at > 0) & (at < BLOCK - 1))
    def _():
        pltpu.make_async_copy(above.at[0, 0], lines.at[outer], sems.at[3]).start()

    weights.wait()
    fill_wide(weight, wide, sums)
    own.wait()
    inside.wait()
    pltpu.make_async_copy(above.at[0, 0], lines.at[outer], sems.at[3]).wait()
    row_out[...] = conv_sums(lines[0], lines[1], lines[2], sums, wide)
    copy = pltpu.make_async_copy(row_out, out.at[0, row], sems.at[4])
    copy.start()
    copy.wait()


def far_edge(cells, above, far, weight, done, ready):
    return pl.pallas_call(
        far_kernel,
        in_specs=[ANY] * 6,
        out_specs=ANY,
        out_shape=pltpu.HBM((1, ROWS, WIDTH, 128), BF16),
        scratch_shapes=[
            pltpu.VMEM((3, WIDTH, 128), BF16),
            pltpu.VMEM((3, 3, 128, 128), BF16),
            pltpu.VMEM((WIDTH, 128), BF16),
            pltpu.VMEM((3, WIDTH + 16, 128), F32),
            pltpu.VMEM((384, 384), BF16),
            pltpu.SemaphoreType.DMA((5,)),
        ],
        input_output_aliases={4: 0},
        compiler_params=params(SMALL),
        cost_estimate=cost(10**9, 2**20),
    )(in_hbm(cells), in_hbm(above), far, in_hbm(weight), in_hbm(done), in_hbm(ready))


def exchange(block):
    lanes = block.shape[1]
    moved = lax.all_to_all(
        block.reshape(GROUPS, ROWS, lanes), "rows", split_axis=0, concat_axis=0, tiled=True
    )
    return moved.reshape(GROUPS * ROWS, lanes)


def shards(local_maps, global_maps, conv_weight, in_weight, mix_weight, out_weight, out_cotangent):
    row_fwd, row_inv = row_tables()
    forward, backward, twiddle = column_tables()
    spec_rows, inner = rows_forward(global_maps, out_cotangent, in_weight.T, out_weight, row_fwd)
    spec_cols = exchange(spec_rows)
    local_inner, token = inner_rows(local_maps, conv_weight, spec_rows)
    above, below = neighbour_rows(local_maps)
    spectrum, back_cols = columns(
        spec_cols, forward, backward, twiddle, mix_weight, token, above, below
    )
    back = exchange(back_cols)
    mix_part = mix_terms(spec_cols, spectrum, forward, twiddle, mix_weight)
    local_out, token = edge_rows(local_maps, above, below, conv_weight, local_inner, back_cols)
    summed, terms = back_rows(row_inv, back, inner, out_cotangent, mix_part, token)
    local_out = far_edge(
        local_maps, above, far_row(local_maps), conv_weight, local_out, in_hbm(terms)
    )
    terms = terms.reshape(256, 2, 128)
    terms = lax.all_to_all(terms, ("rows", "img"), split_axis=0, concat_axis=0, tiled=True)
    global_out = project_out(summed, out_weight)
    mix_grad, out_grad = sum_terms(terms.reshape(512, 128))
    mix_grad, out_grad = mix_grad.reshape(128, 1), out_grad.reshape(SPEC_CH, 1)
    return (local_out, global_out, mix_grad, out_grad)


def solution(mesh):
    maps = P("img", "rows", None, None)
    in_specs = (maps, maps, P(), P(), P(), P(), maps)
    out_specs = (maps, maps, P(None, "rows"), P(None, "rows"))
    return jax.shard_map(shards, mesh=mesh, in_specs=in_specs, out_specs=out_specs, check_vma=False)
```

```python
import math

import jax
import jax.numpy as jnp
import ml_dtypes
import numpy as np
from jax import lax
from jax.experimental import pallas as pl
from jax.experimental.pallas import tpu as pltpu
from jax.sharding import PartitionSpec as P

HEIGHT = 1024
WIDTH = 1024
SPEC_CH = 64
FREQS = 512
ROWS = 8
GROUPS = 128
PER_GROUP = 4
PAIR = 128
BF16 = jnp.bfloat16
F32 = jnp.float32

LIMIT = 60 * 2**20
SMALL = 40 * 2**20


def params(limit=LIMIT):
    return pltpu.CompilerParams(vmem_limit_bytes=limit)


def in_hbm(x):
    return pltpu.with_memory_space_constraint(x, pltpu.HBM)


VMEM = pl.BlockSpec(memory_space=pltpu.VMEM)


ANY = pl.BlockSpec(memory_space=pl.ANY)


def cost(flops, nbytes):
    return pl.CostEstimate(flops=flops, bytes_accessed=nbytes, transcendentals=0)


FIRSTS = ((0, 4), (1, 7), (2, 6), (3, 5))


def row_tables():
    s = np.arange(128)
    forward = np.zeros((4, 2, 16, 2, PER_GROUP, 2, 128))
    inverse = np.zeros((4, 2, 128, 2, 16, 2, PER_GROUP))
    for b, firsts in enumerate(FIRSTS):
        for half, k0 in enumerate(firsts):
            k = k0 + 8 * np.arange(64).reshape(16, PER_GROUP, 1)
            phase = (k * s % WIDTH) * (2.0 * math.pi / WIDTH)
            cosine, sine = np.cos(phase) / 32.0, np.sin(phase) / 32.0
            factor = np.where(k == 0, 1.0, 2.0)
            sign = 1.0 if half else -1.0
            if b == 0:
                forward[b, half, :, 0, :, half] = cosine
                forward[b, half, :, 1, :, half] = -sine
                inverse[b, half, :, half, :, 0] = (cosine * factor).transpose(2, 0, 1)
                inverse[b, half, :, half, :, 1] = (-sine * factor).transpose(2, 0, 1)
                continue
            forward[b, half, :, 0, :, 0] = cosine
            forward[b, half, :, 0, :, 1] = sign * sine
            forward[b, half, :, 1, :, 0] = -sine
            forward[b, half, :, 1, :, 1] = sign * cosine
            inverse[b, 0, :, half, :, 0] = (cosine * factor).transpose(2, 0, 1)
            inverse[b, 0, :, half, :, 1] = (-sine * factor).transpose(2, 0, 1)
            inverse[b, 1, :, half, :, 0] = (-sign * sine * factor).transpose(2, 0, 1)
            inverse[b, 1, :, half, :, 1] = (-sign * cosine * factor).transpose(2, 0, 1)
    forward = forward.reshape(4, 256, 256).astype(ml_dtypes.bfloat16)
    return forward, inverse.reshape(4, 256, 256).astype(ml_dtypes.bfloat16)


def column_tables():
    idx = np.arange(GROUPS)
    phase = ((idx[:, None] * idx[None, :]) % GROUPS) * (2.0 * math.pi / GROUPS)
    cosine, sine = np.cos(phase) / math.sqrt(HEIGHT), np.sin(phase) / math.sqrt(HEIGHT)
    forward = np.block([[cosine, sine], [-sine, cosine]])
    backward = np.block([[cosine, -sine], [sine, cosine]])
    turn = (idx[:, None] * np.arange(ROWS)[None, :]) * (2.0 * math.pi / HEIGHT)
    twiddle = np.repeat(np.stack([np.cos(turn), np.sin(turn)]), SPEC_CH, axis=2)
    return (
        forward.astype(ml_dtypes.bfloat16),
        backward.astype(ml_dtypes.bfloat16),
        twiddle.astype(np.float32),
    )


def dot(a, b):
    return jnp.dot(a, b, preferred_element_type=F32)


def dot_t(a, b):
    return lax.dot_general(a, b, (((0,), (0,)), ((), ())), preferred_element_type=F32)


def iota(shape, dim):
    return lax.broadcasted_iota(jnp.int32, shape, dim)


def first_half():
    return jnp.where(iota((SPEC_CH, PAIR), 0) == iota((SPEC_CH, PAIR), 1), 1.0, 0.0).astype(BF16)


def second_half():
    hit = iota((SPEC_CH, PAIR), 0) + SPEC_CH == iota((SPEC_CH, PAIR), 1)
    return jnp.where(hit, 1.0, 0.0).astype(BF16)


ROOT = math.sqrt(0.5)
RB = 16


def eight_points(x):
    a = [x[r] + x[r + 4] for r in range(4)]
    b = [x[r] - x[r + 4] for r in range(4)]
    even, odd = a[0] + a[2], a[1] + a[3]
    c, d = (b[1] - b[3]) * ROOT, (b[1] + b[3]) * ROOT
    return (
        (even + odd, even - odd),
        (b[0] + c, d + b[2]),
        (a[0] - a[2], a[1] - a[3]),
        (b[0] - c, d - b[2]),
    )


def eight_back(u):
    (u0, u4), (p1, q1), (p2, q2), (p3, q3) = u
    total, rest = u0 + u4, u0 - u4
    even = (total + p2, rest - q2, total - p2, rest + q2)
    c, d = (p1 - p3) * ROOT, (q1 + q3) * ROOT
    odd = (p1 + p3, c - d, q3 - q1, -c - d)
    return [even[r] + odd[r] for r in range(4)] + [even[r] - odd[r] for r in range(4)]


def rows_kernel(
    maps, cot, in_w, out_w, table, spec_out, inner_out,
    pairs, held, part, inner, eights, result, in_pair, out_pair, sems, table_sem, out_sems,
):
    half = ROWS * SPEC_CH
    loads = []
    for p in range(4):
        for n, source in enumerate((maps, cot)):
            rows = source.at[0, pl.ds(2 * p, 2)]
            loads.append(pltpu.make_async_copy(rows, pairs.at[p, n], sems.at[p, n]))
    table_load = pltpu.make_async_copy(table, held, table_sem)
    def start(i):
        p, n = (i % 4, i // 4)
        loads[2 * p + n].start()

    for i in range(8):
        start(i)
    table_load.start()
    a, b = first_half(), second_half()
    in_pair[0:PAIR, :] = dot_t(in_w[...], a).astype(BF16)
    in_pair[PAIR:, :] = dot_t(in_w[...], b).astype(BF16)
    out_pair[0:PAIR, :] = (2.0 * dot_t(out_w[...], a)).astype(BF16)
    out_pair[PAIR:, :] = (2.0 * dot_t(out_w[...], b)).astype(BF16)
    def project(i):
        p, n = (i % 4, i // 4)
        pair = jnp.concatenate([pairs[p, n, 0], pairs[p, n, 1]], axis=1)
        part[i % 2] = dot(pair, out_pair[...] if n else in_pair[...])

    for copy in loads[0::2]:
        copy.wait()
    project(0)
    for i in range(8):
        p, n = (i % 4, i // 4)
        if i == 3:
            for copy in loads[1::2]:
                copy.wait()
        if i < 7:
            project(i + 1)
        lanes = slice(n * half + p * PAIR, n * half + (p + 1) * PAIR)

        @pl.loop(0, 128, step=RB, unroll=True)
        def _(rows):
            rows = pl.multiple_of(rows, RB)
            x = [part[i % 2, pl.ds(128 * r + rows, RB), :] for r in range(8)]
            if n == 0:
                x = [jnp.maximum(v, 0.0) for v in x]
                for r in range(8):
                    inner[pl.ds(128 * r + rows, RB), lanes] = x[r].astype(BF16)
            for block, both in enumerate(eight_points(x)):
                for k in range(2):
                    eights[block, pl.ds(128 * k + rows, RB), lanes] = both[k].astype(BF16)

    stores = [pltpu.make_async_copy(inner, inner_out, out_sems.at[4])]
    stores[0].start()
    table_load.wait()
    for b in range(4):
        rows = pl.ds(b * 256, 256)
        prod = dot(held[b], eights[b])
        result[rows, 0:half] = prod[:, 0:half].astype(BF16)
        if b == 0:
            row = iota((256, half), 0)
            factor = jnp.where((row == 0) | (row == PER_GROUP), 0.5, 1.0)
            result[rows, half:] = (prod[:, half:] * factor).astype(BF16)
        else:
            result[rows, half:] = prod[:, half:].astype(BF16)
        stores.append(pltpu.make_async_copy(result.at[rows], spec_out.at[rows], out_sems.at[b]))
        stores[-1].start()
    for copy in stores:
        copy.wait()


def rows_forward(maps, cot, in_w, out_w, table):
    return pl.pallas_call(
        rows_kernel,
        grid=(1,),
        in_specs=[ANY, ANY, whole_spec((SPEC_CH, 128)), whole_spec((SPEC_CH, 128)), ANY],
        out_specs=[ANY, ANY],
        out_shape=[
            pltpu.HBM((1024, 1024), BF16),
            pltpu.HBM((WIDTH, 512), BF16),
        ],
        scratch_shapes=[
            pltpu.VMEM((4, 2, 2, WIDTH, 128), BF16),
            pltpu.VMEM((4, 256, 256), BF16),
            pltpu.VMEM((2, WIDTH, PAIR), F32),
            pltpu.VMEM((WIDTH, 512), BF16),
            pltpu.VMEM((4, 256, 1024), BF16),
            pltpu.VMEM((1024, 1024), BF16),
            pltpu.VMEM((256, PAIR), BF16),
            pltpu.VMEM((256, PAIR), BF16),
            pltpu.SemaphoreType.DMA((4, 2)),
            pltpu.SemaphoreType.DMA,
            pltpu.SemaphoreType.DMA((5,)),
        ],
        compiler_params=params(),
        cost_estimate=cost(5 * 10**9, 11 * 2**20),
    )(maps, cot, in_w, out_w, table)


def lane_signs(shape):
    return jnp.where(iota(shape, 1) % PAIR < SPEC_CH, 1.0, -1.0).astype(F32)


def lane_butterfly(x, signs):
    return pltpu.roll(x, SPEC_CH, 1) + x * signs


def turn_second(re, im, first, real, imag):
    new_re = jnp.where(first, re, re * real - im * imag)
    new_im = jnp.where(first, im, re * imag + im * real)
    return new_re, new_im


EIGHTHS = ((1.0, 0.0), (ROOT, -ROOT), (0.0, -1.0), (-ROOT, -ROOT))


def spectrum_rows(prod, twiddle, rows, signs, first):
    re, im = [], []
    for m in range(4):
        lanes = slice(m * PAIR, (m + 1) * PAIR)
        a = prod[pl.ds(rows, RB), lanes]
        b = prod[pl.ds(GROUPS + rows, RB), lanes]
        c = twiddle[0, pl.ds(rows, RB), lanes]
        s = twiddle[1, pl.ds(rows, RB), lanes]
        re.append(a * c + b * s)
        im.append(b * c - a * s)
    s0r, s0i, d0r, d0i = re[0] + re[2], im[0] + im[2], re[0] - re[2], im[0] - im[2]
    s1r, s1i, d1r, d1i = re[1] + re[3], im[1] + im[3], re[1] - re[3], im[1] - im[3]
    four = (
        (s0r + s1r, s0i + s1i),
        (d0r + d1i, d0i - d1r),
        (s0r - s1r, s0i - s1i),
        (d0r - d1i, d0i + d1r),
    )
    out = []
    for q in range(4):
        zr, zi = four[q]
        if q:
            zr, zi = turn_second(zr, zi, first, *EIGHTHS[q])
        out.append((lane_butterfly(zr, signs), lane_butterfly(zi, signs)))
    return out


def inverse_rows(parts, twiddle, rows, signs, first):
    z = []
    for q in range(4):
        zr, zi = (lane_butterfly(x, signs) for x in parts[q])
        if q:
            zr, zi = turn_second(zr, zi, first, EIGHTHS[q][0], -EIGHTHS[q][1])
        z.append((zr, zi))
    s0r, s0i = z[0][0] + z[2][0], z[0][1] + z[2][1]
    d0r, d0i = z[0][0] - z[2][0], z[0][1] - z[2][1]
    s1r, s1i = z[1][0] + z[3][0], z[1][1] + z[3][1]
    d1r, d1i = z[1][0] - z[3][0], z[1][1] - z[3][1]
    four = (
        (s0r + s1r, s0i + s1i),
        (d0r - d1i, d0i + d1r),
        (s0r - s1r, s0i - s1i),
        (d0r + d1i, d0i - d1r),
    )
    out = []
    for m in range(4):
        lanes = slice(m * PAIR, (m + 1) * PAIR)
        c = twiddle[0, pl.ds(rows, RB), lanes]
        s = twiddle[1, pl.ds(rows, RB), lanes]
        a, b = four[m]
        out.append((a * c - b * s, b * c + a * s))
    return out


def fill_mix(mix_w, wide):
    total = jnp.zeros((256, 256), F32)
    for t in range(2):
        row, col = iota((256, 128), 0), iota((256, 128), 1)
        at = (row // PAIR) * SPEC_CH + row % SPEC_CH
        hit = (at == col) & (row // SPEC_CH % 2 == t)
        pick = jnp.where(hit, 1.0, 0.0).astype(BF16)
        left = dot(pick, mix_w[...]).astype(BF16)
        total = total + lax.dot_general(
            left, pick, (((1,), (1,)), ((), ())), preferred_element_type=F32
        )
    wide[...] = total.astype(BF16)


def sigmoid(x):
    return 0.5 * jnp.tanh(0.5 * x) + 0.5


def gather_parts(stage, kk):
    lanes = []
    for m in range(4):
        re = stage[m, pl.ds(kk, GROUPS, stride=ROWS), :]
        im = stage[m, pl.ds(PER_GROUP + kk, GROUPS, stride=ROWS), :]
        lanes.append(jnp.concatenate([re, im], axis=0).astype(BF16))
    return jnp.concatenate(lanes, axis=1)


def fill_stage(block, stage):
    for m in range(4):
        stage[m] = block[:, m * PAIR : (m + 1) * PAIR].astype(F32)


def columns_kernel(
    block, forward_in, backward_in, twiddle_in, mix_in, above, below, spec_out, back_out,
    land, forward, backward, twiddle, wide, spec, stage, back, prod, pre, inv, sems, out_sems,
):
    del above, below
    mix_load = pltpu.make_async_copy(mix_in, wide, sems.at[4])
    forward_load = pltpu.make_async_copy(forward_in, forward, sems.at[5])
    twiddle_load = pltpu.make_async_copy(twiddle_in, twiddle, sems.at[6])
    backward_load = pltpu.make_async_copy(backward_in, backward, sems.at[7])
    for copy in (mix_load, forward_load, twiddle_load, backward_load):
        copy.start()
    for m in range(4):
        stage[m] = block[:, m * PAIR : (m + 1) * PAIR].astype(F32)
    mix_load.wait()
    forward_load.wait()
    twiddle_load.wait()
    backward_load.wait()
    stores = []
    signs = lane_signs((RB, PAIR))
    first = iota((RB, PAIR), 1) < SPEC_CH
    def transform(kk):
        prod[kk % 2] = dot(forward[...], gather_parts(stage, kk))

    def spectrum(kk):
        @pl.loop(0, GROUPS, step=RB, unroll=True)
        def _(rows):
            rows = pl.multiple_of(rows, RB)
            parts = spectrum_rows(prod.at[kk % 2], twiddle, rows, signs, first)
            for q in range(4):
                spec[kk * 4 + q, pl.ds(rows, RB), 0:PAIR] = parts[q][0].astype(BF16)
                spec[kk * 4 + q, pl.ds(rows, RB), PAIR:] = parts[q][1].astype(BF16)

        part = pl.ds(kk * 4, 4)
        stores.append(pltpu.make_async_copy(spec.at[part], spec_out.at[part], out_sems.at[kk]))
        stores[-1].start()

    def mix(kk):
        pre[kk % 2] = dot(spec[kk * 4 : kk * 4 + 4].reshape(512, 256), wide[...])

    def activate(kk):
        @pl.loop(0, GROUPS, step=RB, unroll=True)
        def _(rows):
            rows = pl.multiple_of(rows, RB)
            parts = []
            for q in range(4):
                v = pre[kk % 2, pl.ds(q * GROUPS + rows, RB), :]
                v = v * sigmoid(v)
                parts.append((v[:, 0:PAIR], v[:, PAIR:]))
            pairs = inverse_rows(parts, twiddle, rows, signs, first)
            for m in range(4):
                lanes = slice(m * PAIR, (m + 1) * PAIR)
                inv[kk % 2, pl.ds(rows, RB), lanes] = pairs[m][0].astype(BF16)
                inv[kk % 2, pl.ds(GROUPS + rows, RB), lanes] = pairs[m][1].astype(BF16)

    def transform_back(kk):
        result = dot(backward[...], inv[kk % 2])
        for m in range(4):
            lanes = slice(m * PAIR, (m + 1) * PAIR)
            back[m, pl.ds(kk, GROUPS, stride=ROWS), :] = result[0:GROUPS, lanes]
            back[m, pl.ds(PER_GROUP + kk, GROUPS, stride=ROWS), :] = result[GROUPS:, lanes]

    transform(0)
    for kk in range(PER_GROUP + 2):
        if kk + 1 < PER_GROUP:
            transform(kk + 1)
        if kk < PER_GROUP:
            spectrum(kk)
        if 0 <= kk - 1 < PER_GROUP:
            activate(kk - 1)
        if kk < PER_GROUP:
            mix(kk)
        if 0 <= kk - 1 < PER_GROUP:
            transform_back(kk - 1)
    for m in range(4):
        land[:, m * PAIR : (m + 1) * PAIR] = back[m].astype(BF16)
        lanes = pl.ds(m * PAIR, PAIR)
        copy = pltpu.make_async_copy(land.at[:, lanes], back_out.at[:, lanes], out_sems.at[4 + m])
        copy.start()
        stores.append(copy)
    for copy in stores:
        copy.wait()


def whole_spec(shape):
    return pl.BlockSpec(shape, lambda *_: (0,) * len(shape))


def columns(block, forward, backward, twiddle, wide, above, below):
    return pl.pallas_call(
        columns_kernel,
        in_specs=[VMEM] + [ANY] * 6,
        out_specs=[ANY, ANY],
        out_shape=[
            pltpu.HBM((16, GROUPS, 256), BF16),
            pltpu.HBM((1024, 512), BF16),
        ],
        scratch_shapes=[
            pltpu.VMEM((1024, 512), BF16),
            pltpu.VMEM((256, 256), BF16),
            pltpu.VMEM((256, 256), BF16),
            pltpu.VMEM((2, GROUPS, 512), F32),
            pltpu.VMEM((256, 256), BF16),
            pltpu.VMEM((16, GROUPS, 256), BF16),
            pltpu.VMEM((4, 1024, PAIR), F32),
            pltpu.VMEM((4, 1024, PAIR), F32),
            pltpu.VMEM((2, 256, 512), F32),
            pltpu.VMEM((2, 512, 256), F32),
            pltpu.VMEM((2, 256, 512), BF16),
            pltpu.SemaphoreType.DMA((8,)),
            pltpu.SemaphoreType.DMA((8,)),
        ],
        compiler_params=params(SMALL),
        cost_estimate=cost(8 * 10**9, 5 * 2**20),
    )(block, forward, backward, twiddle, wide, above, below)


def mix_kernel(block, spec, forward, twiddle, wide, grad, stage, prod, pre, slope, acc):
    fill_stage(block, stage)
    signs = lane_signs((RB, PAIR))
    first = iota((RB, PAIR), 1) < SPEC_CH
    acc[...] = jnp.zeros_like(acc)
    for kk in range(PER_GROUP):
        prod[...] = dot(forward[...], gather_parts(stage, kk))
        pre[...] = dot(spec[kk * 4 : kk * 4 + 4].reshape(512, 256), wide[...])

        @pl.loop(0, GROUPS, step=RB, unroll=True)
        def _(rows):
            rows = pl.multiple_of(rows, RB)
            parts = spectrum_rows(prod, twiddle, rows, signs, first)
            for q in range(4):
                for part in range(2):
                    lanes = slice(part * PAIR, (part + 1) * PAIR)
                    v = pre[pl.ds(q * GROUPS + rows, RB), lanes]
                    s = sigmoid(v)
                    v = parts[q][part] * (s * (1.0 + v * (1.0 - s)))
                    slope[pl.ds(q * GROUPS + rows, RB), lanes] = v.astype(BF16)

        acc[...] += dot_t(slope[...], spec[kk * 4 : kk * 4 + 4].reshape(512, 256))
    lane = iota((SPEC_CH, PAIR), 1) < SPEC_CH
    for part in range(2):
        even = acc[part * PAIR : part * PAIR + SPEC_CH, :]
        odd = acc[part * PAIR + SPEC_CH : (part + 1) * PAIR, :]
        real = even[:, 0:PAIR] + pltpu.roll(odd[:, 0:PAIR], SPEC_CH, 1)
        imag = pltpu.roll(even[:, PAIR:], SPEC_CH, 1) + odd[:, PAIR:]
        grad[part * SPEC_CH : (part + 1) * SPEC_CH, :] = jnp.where(lane, real, imag)


def mix_terms(block, spec, forward, twiddle, wide):
    return pl.pallas_call(
        mix_kernel,
        grid=(1,),
        in_specs=[
            pl.BlockSpec((1024, 512), lambda i: (0, 1)),
            whole_spec((16, GROUPS, 256)),
            whole_spec((256, 256)),
            whole_spec((2, GROUPS, 512)),
            whole_spec((256, 256)),
        ],
        out_specs=whole_spec((128, 128)),
        out_shape=jax.ShapeDtypeStruct((128, 128), F32),
        scratch_shapes=[
            pltpu.VMEM((4, 1024, PAIR), F32),
            pltpu.VMEM((256, 512), F32),
            pltpu.VMEM((512, 256), F32),
            pltpu.VMEM((512, 256), BF16),
            pltpu.VMEM((256, 256), F32),
        ],
        compiler_params=params(),
        cost_estimate=cost(6 * 10**9, 5 * 2**20),
    )(block, spec, forward, twiddle, wide)


def back_kernel(
    table, block, inner, cot, mix_part, ready, summed_out, terms_out,
    held, inners, cots, mix, summed, terms, packed, parts, sems, out_sems,
):
    del ready

    def load(source, target, sem):
        copy = pltpu.make_async_copy(source, target, sems.at[sem])
        copy.start()
        return copy

    first = load(table, held, 0)
    second = load(inner, inners, 1)
    pairs = [load(cot.at[0, pl.ds(2 * p, 2)], cots.at[p], 2 + p) for p in range(4)]
    last = load(mix_part, mix, 6)
    first.wait()
    for b in range(4):
        parts[b] = dot(held[b], block[b * 256 : (b + 1) * 256, :])
    second.wait()
    acc = jnp.zeros((PAIR, 256), F32)
    for p in range(4):
        lanes = slice(p * PAIR, (p + 1) * PAIR)

        @pl.loop(0, 128, step=RB, unroll=True)
        def _(rows):
            rows = pl.multiple_of(rows, RB)
            u = [
                [parts[b, pl.ds(128 * i + rows, RB), lanes] for i in range(2)] for b in range(4)
            ]
            for r, x in enumerate(eight_back(u)):
                at = pl.ds(128 * r + rows, RB)
                summed[at, lanes] = (x + inners[at, lanes].astype(F32)).astype(BF16)

        pairs[p].wait()
        pair = jnp.concatenate([cots[p, 0], cots[p, 1]], axis=1)
        acc = acc + dot_t(summed[:, lanes], pair)
    store = pltpu.make_async_copy(summed, summed_out, out_sems.at[0])
    store.start()
    last.wait()
    out_part = acc[0:SPEC_CH, 0:128] + acc[SPEC_CH:, 128:]
    high = out_part.astype(BF16).astype(F32)
    out_both = jnp.concatenate([high, out_part - high], axis=0).T
    for img in range(2):
        terms[pl.ds(2 * img, 128, stride=4), :] = mix[...]
        terms[pl.ds(2 * img + 1, 128, stride=4), :] = out_both
    packed[...] = terms[...].astype(BF16)
    copy = pltpu.make_async_copy(packed, terms_out, out_sems.at[1])
    copy.start()
    store.wait()
    copy.wait()


def back_rows(table, rows, inner, cot, mix_part, ready):
    return pl.pallas_call(
        back_kernel,
        in_specs=[ANY, VMEM, ANY, ANY, ANY, ANY],
        out_specs=[ANY, ANY],
        out_shape=[
            pltpu.HBM((WIDTH, 512), BF16),
            pltpu.HBM((512, 128), BF16),
        ],
        scratch_shapes=[
            pltpu.VMEM((4, 256, 256), BF16),
            pltpu.VMEM((WIDTH, 512), BF16),
            pltpu.VMEM((4, 2, WIDTH, 128), BF16),
            pltpu.VMEM((128, 128), F32),
            pltpu.VMEM((WIDTH, 512), BF16),
            pltpu.VMEM((512, 128), F32),
            pltpu.VMEM((512, 128), BF16),
            pltpu.VMEM((4, 256, 512), F32),
            pltpu.SemaphoreType.DMA((7,)),
            pltpu.SemaphoreType.DMA((2,)),
        ],
        compiler_params=params(SMALL),
        cost_estimate=cost(2 * 10**9, 8 * 2**20),
    )(in_hbm(table), rows, in_hbm(inner), in_hbm(cot), in_hbm(mix_part), in_hbm(ready))


def out_kernel(summed, out_w, out, held, wide, result, sems, out_sems):
    loads = []
    for p in range(4):
        lanes = pl.ds(p * PAIR, PAIR)
        loads.append(pltpu.make_async_copy(summed.at[:, lanes], held.at[p], sems.at[p]))
        loads[p].start()
    zero = jnp.zeros((SPEC_CH, 128), BF16)
    wide[0:SPEC_CH, :] = jnp.concatenate([out_w[...], zero], axis=1)
    wide[SPEC_CH:, :] = jnp.concatenate([zero, out_w[...]], axis=1)
    stores = []
    for p in range(4):
        loads[p].wait()
        prod = dot(held[p], wide[...])
        result[2 * p] = prod[:, 0:128].astype(BF16)
        result[2 * p + 1] = prod[:, 128:].astype(BF16)
        rows = pl.ds(2 * p, 2)
        stores.append(pltpu.make_async_copy(result.at[rows], out.at[0, rows], out_sems.at[p]))
        stores[p].start()
    for copy in stores:
        copy.wait()


def project_out(summed, out_w):
    return pl.pallas_call(
        out_kernel,
        grid=(1,),
        in_specs=[ANY, whole_spec((SPEC_CH, 128))],
        out_specs=ANY,
        out_shape=pltpu.HBM((1, ROWS, WIDTH, 128), BF16),
        scratch_shapes=[
            pltpu.VMEM((4, WIDTH, PAIR), BF16),
            pltpu.VMEM((128, 256), BF16),
            pltpu.VMEM((ROWS, WIDTH, 128), BF16),
            pltpu.SemaphoreType.DMA((4,)),
            pltpu.SemaphoreType.DMA((4,)),
        ],
        compiler_params=params(),
        cost_estimate=cost(5 * 10**8, 3 * 2**20),
    )(summed, out_w)


def fill_wide(weight, wide, sums):
    for a in range(3):
        for b in range(3):
            wide[a * 128 : (a + 1) * 128, b * 128 : (b + 1) * 128] = weight[a, b]
    sums[0, 0:8] = jnp.zeros((8, 128), F32)
    sums[2, WIDTH + 8 :] = jnp.zeros((8, 128), F32)


def conv_sums(top, mid, bottom, sums, wide):
    prod = dot(jnp.concatenate([top, mid, bottom], axis=1), wide[...])
    for b in range(3):
        sums[b, 8 : WIDTH + 8] = prod[:, b * 128 : (b + 1) * 128]
    total = sums[0, 7 : WIDTH + 7] + sums[1, 8 : WIDTH + 8] + sums[2, 9 : WIDTH + 9]
    return total.astype(BF16)


def conv_row(top, mid, bottom, weight, out, sums, wide):
    @pl.when(pl.program_id(0) == 0)
    def _():
        fill_wide(weight, wide, sums)

    out[0, 0] = conv_sums(top, mid, bottom, sums, wide)


def inner_kernel(above, mid, below, weight, mix_w, ready, out, mix, sums, wide):
    del ready
    conv_row(above[0, 0], mid[0, 0], below[0, 0], weight, out, sums, wide)

    @pl.when(pl.program_id(0) == 0)
    def _():
        fill_mix(mix_w, mix)


def edge_kernel(
    mid, beside, edge_above, edge_below, weight, done, ready, out, token, sums, wide
):
    del done, ready
    token[...] = jnp.zeros((8, 128), F32)
    first = pl.program_id(0) == 0
    top = jnp.where(first, edge_above[0, 0], beside[0, 0])
    bottom = jnp.where(first, beside[0, 0], edge_below[0, 0])
    conv_row(top, mid[0, 0], bottom, weight, out, sums, wide)


def sum_kernel(terms, mix, out):
    total = jnp.sum(terms[...].astype(F32).reshape(64, 8, 128), axis=0)
    even = iota((8, 128), 0) % 2 == 0
    mix[...] = jnp.sum(jnp.where(even, total, 0.0), axis=0, keepdims=True)
    odd = jnp.sum(jnp.where(even, 0.0, total), axis=0, keepdims=True)
    out[...] = odd[:, 0:SPEC_CH] + odd[:, SPEC_CH:]


def sum_terms(terms):
    return pl.pallas_call(
        sum_kernel,
        in_specs=[VMEM],
        out_specs=[VMEM, VMEM],
        out_shape=[
            jax.ShapeDtypeStruct((1, 128), F32),
            jax.ShapeDtypeStruct((1, SPEC_CH), F32),
        ],
        compiler_params=params(SMALL),
        cost_estimate=cost(10**6, 2**17),
    )(terms)


def row_spec(index):
    return pl.BlockSpec((1, 1, WIDTH, 128), lambda i: (0, index(i), 0, 0))


def conv_call(kernel, rows, in_specs, out_index, second, aliases, args):
    return pl.pallas_call(
        kernel,
        grid=(rows,),
        in_specs=in_specs,
        out_specs=[row_spec(out_index), whole_spec(second.shape)],
        out_shape=[
            pltpu.HBM((1, ROWS, WIDTH, 128), BF16),
            second,
        ],
        scratch_shapes=[pltpu.VMEM((3, WIDTH + 16, 128), F32), pltpu.VMEM((384, 384), BF16)],
        input_output_aliases=aliases,
        compiler_params=params(),
        cost_estimate=cost(rows * 10**9, rows * 2**20),
    )(*args)


def inner_rows(cells, weight, mix_w, ready):
    specs = [
        row_spec(lambda i: i),
        row_spec(lambda i: i + 1),
        row_spec(lambda i: i + 2),
        whole_spec((3, 3, 128, 128)),
        whole_spec((128, 128)),
        pl.BlockSpec(memory_space=pl.ANY),
    ]
    args = (cells, cells, cells, weight, mix_w, ready)
    second = jax.ShapeDtypeStruct((256, 256), BF16)
    return conv_call(inner_kernel, ROWS - 2, specs, lambda i: i + 1, second, {}, args)


BLOCK = 8


def neighbour_rows(cells):
    head, tail = cells[:, 0:1], cells[:, ROWS - 1 :]
    near = [i for i in range(GROUPS - 1) if i % BLOCK != BLOCK - 1]
    above = lax.ppermute(tail, "rows", [(i, i + 1) for i in near])
    below = lax.ppermute(head, "rows", [(i + 1, i) for i in near])
    return above, below


def far_row(cells):
    last = lax.axis_index("rows") % BLOCK == BLOCK - 1
    row = lax.dynamic_slice_in_dim(cells, jnp.where(last, ROWS - 1, 0), 1, axis=1)
    far = range(BLOCK - 1, GROUPS - 1, BLOCK)
    return lax.ppermute(row, "rows", [(i, i + 1) for i in far] + [(i + 1, i) for i in far])


def edge_rows(cells, above, below, weight, done, ready):
    specs = [
        row_spec(lambda i: i * (ROWS - 1)),
        row_spec(lambda i: 1 + i * (ROWS - 3)),
        whole_spec((1, 1, WIDTH, 128)),
        whole_spec((1, 1, WIDTH, 128)),
        whole_spec((3, 3, 128, 128)),
        pl.BlockSpec(memory_space=pl.ANY),
        pl.BlockSpec(memory_space=pl.ANY),
    ]
    args = (cells, cells, above, below, weight, done, ready)
    second = jax.ShapeDtypeStruct((8, 128), F32)
    return conv_call(edge_kernel, 2, specs, lambda i: i * (ROWS - 1), second, {5: 0}, args)


def far_kernel(cells, above, far, weight_in, done, ready, out, lines, weight, row_out, sums, wide, sems):
    del done, ready
    at = lax.axis_index("rows") % BLOCK
    last = at == BLOCK - 1
    row = jnp.where(last, ROWS - 1, 0)
    beside = jnp.where(last, ROWS - 2, 1)
    outer = jnp.where(last, 2, 0)
    weights = pltpu.make_async_copy(weight_in, weight, sems.at[0])
    weights.start()
    own = pltpu.make_async_copy(cells.at[0, row], lines.at[1], sems.at[1])
    own.start()
    inside = pltpu.make_async_copy(cells.at[0, beside], lines.at[2 - outer], sems.at[2])
    inside.start()

    @pl.when((at == 0) | last)
    def _():
        pltpu.make_async_copy(far.at[0, 0], lines.at[outer], sems.at[3]).start()

    @pl.when((at > 0) & (at < BLOCK - 1))
    def _():
        pltpu.make_async_copy(above.at[0, 0], lines.at[outer], sems.at[3]).start()

    weights.wait()
    fill_wide(weight, wide, sums)
    own.wait()
    inside.wait()
    pltpu.make_async_copy(above.at[0, 0], lines.at[outer], sems.at[3]).wait()
    row_out[...] = conv_sums(lines[0], lines[1], lines[2], sums, wide)
    copy = pltpu.make_async_copy(row_out, out.at[0, row], sems.at[4])
    copy.start()
    copy.wait()


def far_edge(cells, above, far, weight, done, ready):
    return pl.pallas_call(
        far_kernel,
        in_specs=[ANY] * 6,
        out_specs=ANY,
        out_shape=pltpu.HBM((1, ROWS, WIDTH, 128), BF16),
        scratch_shapes=[
            pltpu.VMEM((3, WIDTH, 128), BF16),
            pltpu.VMEM((3, 3, 128, 128), BF16),
            pltpu.VMEM((WIDTH, 128), BF16),
            pltpu.VMEM((3, WIDTH + 16, 128), F32),
            pltpu.VMEM((384, 384), BF16),
            pltpu.SemaphoreType.DMA((5,)),
        ],
        input_output_aliases={4: 0},
        compiler_params=params(SMALL),
        cost_estimate=cost(10**9, 2**20),
    )(in_hbm(cells), in_hbm(above), far, in_hbm(weight), in_hbm(done), in_hbm(ready))


def exchange(block):
    lanes = block.shape[1]
    moved = lax.all_to_all(
        block.reshape(GROUPS, ROWS, lanes), "rows", split_axis=0, concat_axis=0, tiled=True
    )
    return moved.reshape(GROUPS * ROWS, lanes)


def shards(local_maps, global_maps, conv_weight, in_weight, mix_weight, out_weight, out_cotangent):
    row_fwd, row_inv = row_tables()
    forward, backward, twiddle = column_tables()
    spec_rows, inner = rows_forward(global_maps, out_cotangent, in_weight.T, out_weight, row_fwd)
    spec_cols = exchange(spec_rows)
    local_inner, wide = inner_rows(local_maps, conv_weight, mix_weight, spec_rows)
    above, below = neighbour_rows(local_maps)
    spectrum, back_cols = columns(
        spec_cols, forward, backward, twiddle, wide, above, below
    )
    back = exchange(back_cols)
    mix_part = mix_terms(spec_cols, spectrum, forward, twiddle, wide)
    local_out, token = edge_rows(local_maps, above, below, conv_weight, local_inner, back_cols)
    summed, terms = back_rows(row_inv, back, inner, out_cotangent, mix_part, token)
    local_out = far_edge(
        local_maps, above, far_row(local_maps), conv_weight, local_out, in_hbm(terms)
    )
    terms = terms.reshape(256, 2, 128)
    terms = lax.all_to_all(terms, ("rows", "img"), split_axis=0, concat_axis=0, tiled=True)
    global_out = project_out(summed, out_weight)
    mix_grad, out_grad = sum_terms(terms.reshape(512, 128))
    mix_grad, out_grad = mix_grad.reshape(128, 1), out_grad.reshape(SPEC_CH, 1)
    return (local_out, global_out, mix_grad, out_grad)


def solution(mesh):
    maps = P("img", "rows", None, None)
    in_specs = (maps, maps, P(), P(), P(), P(), maps)
    out_specs = (maps, maps, P(None, "rows"), P(None, "rows"))
    return jax.shard_map(shards, mesh=mesh, in_specs=in_specs, out_specs=out_specs, check_vma=False)
```

```python
import math

import jax
import jax.numpy as jnp
import ml_dtypes
import numpy as np
from jax import lax
from jax.experimental import pallas as pl
from jax.experimental.pallas import tpu as pltpu
from jax.sharding import PartitionSpec as P

HEIGHT = 1024
WIDTH = 1024
SPEC_CH = 64
FREQS = 512
ROWS = 8
GROUPS = 128
PER_GROUP = 4
PAIR = 128
BF16 = jnp.bfloat16
F32 = jnp.float32

LIMIT = 60 * 2**20
SMALL = 40 * 2**20


def params(limit=LIMIT):
    return pltpu.CompilerParams(vmem_limit_bytes=limit)


def in_hbm(x):
    return pltpu.with_memory_space_constraint(x, pltpu.HBM)


VMEM = pl.BlockSpec(memory_space=pltpu.VMEM)


ANY = pl.BlockSpec(memory_space=pl.ANY)


def cost(flops, nbytes):
    return pl.CostEstimate(flops=flops, bytes_accessed=nbytes, transcendentals=0)


FIRSTS = ((0, 4), (1, 7), (2, 6), (3, 5))


def row_tables():
    s = np.arange(128)
    forward = np.zeros((4, 2, 16, 2, PER_GROUP, 2, 128))
    inverse = np.zeros((4, 2, 128, 2, 16, 2, PER_GROUP))
    for b, firsts in enumerate(FIRSTS):
        for half, k0 in enumerate(firsts):
            k = k0 + 8 * np.arange(64).reshape(16, PER_GROUP, 1)
            phase = (k * s % WIDTH) * (2.0 * math.pi / WIDTH)
            cosine, sine = np.cos(phase) / 32.0, np.sin(phase) / 32.0
            factor = np.where(k == 0, 1.0, 2.0)
            sign = 1.0 if half else -1.0
            if b == 0:
                forward[b, half, :, 0, :, half] = cosine
                forward[b, half, :, 1, :, half] = -sine
                inverse[b, half, :, half, :, 0] = (cosine * factor).transpose(2, 0, 1)
                inverse[b, half, :, half, :, 1] = (-sine * factor).transpose(2, 0, 1)
                continue
            forward[b, half, :, 0, :, 0] = cosine
            forward[b, half, :, 0, :, 1] = sign * sine
            forward[b, half, :, 1, :, 0] = -sine
            forward[b, half, :, 1, :, 1] = sign * cosine
            inverse[b, 0, :, half, :, 0] = (cosine * factor).transpose(2, 0, 1)
            inverse[b, 0, :, half, :, 1] = (-sine * factor).transpose(2, 0, 1)
            inverse[b, 1, :, half, :, 0] = (-sign * sine * factor).transpose(2, 0, 1)
            inverse[b, 1, :, half, :, 1] = (-sign * cosine * factor).transpose(2, 0, 1)
    forward = forward.reshape(4, 256, 256).astype(ml_dtypes.bfloat16)
    return forward, inverse.reshape(4, 256, 256).astype(ml_dtypes.bfloat16)


def column_tables():
    idx = np.arange(GROUPS)
    phase = ((idx[:, None] * idx[None, :]) % GROUPS) * (2.0 * math.pi / GROUPS)
    cosine, sine = np.cos(phase) / math.sqrt(HEIGHT), np.sin(phase) / math.sqrt(HEIGHT)
    forward = np.block([[cosine, sine], [-sine, cosine]])
    backward = np.block([[cosine, -sine], [sine, cosine]])
    turn = (idx[:, None] * np.arange(ROWS)[None, :]) * (2.0 * math.pi / HEIGHT)
    twiddle = np.repeat(np.stack([np.cos(turn), np.sin(turn)]), SPEC_CH, axis=2)
    return (
        forward.astype(ml_dtypes.bfloat16),
        backward.astype(ml_dtypes.bfloat16),
        twiddle.astype(np.float32),
    )


def dot(a, b):
    return jnp.dot(a, b, preferred_element_type=F32)


def dot_t(a, b):
    return lax.dot_general(a, b, (((0,), (0,)), ((), ())), preferred_element_type=F32)


def iota(shape, dim):
    return lax.broadcasted_iota(jnp.int32, shape, dim)


def first_half():
    return jnp.where(iota((SPEC_CH, PAIR), 0) == iota((SPEC_CH, PAIR), 1), 1.0, 0.0).astype(BF16)


def second_half():
    hit = iota((SPEC_CH, PAIR), 0) + SPEC_CH == iota((SPEC_CH, PAIR), 1)
    return jnp.where(hit, 1.0, 0.0).astype(BF16)


ROOT = math.sqrt(0.5)
RB = 16


def eight_points(x):
    a = [x[r] + x[r + 4] for r in range(4)]
    b = [x[r] - x[r + 4] for r in range(4)]
    even, odd = a[0] + a[2], a[1] + a[3]
    c, d = (b[1] - b[3]) * ROOT, (b[1] + b[3]) * ROOT
    return (
        (even + odd, even - odd),
        (b[0] + c, d + b[2]),
        (a[0] - a[2], a[1] - a[3]),
        (b[0] - c, d - b[2]),
    )


def eight_back(u):
    (u0, u4), (p1, q1), (p2, q2), (p3, q3) = u
    total, rest = u0 + u4, u0 - u4
    even = (total + p2, rest - q2, total - p2, rest + q2)
    c, d = (p1 - p3) * ROOT, (q1 + q3) * ROOT
    odd = (p1 + p3, c - d, q3 - q1, -c - d)
    return [even[r] + odd[r] for r in range(4)] + [even[r] - odd[r] for r in range(4)]


def rows_kernel(
    maps, cot, in_w, out_w, table, spec_out, inner_out,
    pairs, held, part, inner, eights, result, in_pair, out_pair, sems, table_sem, out_sems,
):
    half = ROWS * SPEC_CH
    loads = []
    for p in range(4):
        for n, source in enumerate((maps, cot)):
            rows = source.at[0, pl.ds(2 * p, 2)]
            loads.append(pltpu.make_async_copy(rows, pairs.at[p, n], sems.at[p, n]))
    table_load = pltpu.make_async_copy(table, held, table_sem)
    def start(i):
        p, n = (i % 4, i // 4)
        loads[2 * p + n].start()

    for i in range(8):
        start(i)
    table_load.start()
    a, b = first_half(), second_half()
    in_pair[0:PAIR, :] = dot_t(in_w[...], a).astype(BF16)
    in_pair[PAIR:, :] = dot_t(in_w[...], b).astype(BF16)
    out_pair[0:PAIR, :] = (2.0 * dot_t(out_w[...], a)).astype(BF16)
    out_pair[PAIR:, :] = (2.0 * dot_t(out_w[...], b)).astype(BF16)
    def project(i):
        p, n = (i % 4, i // 4)
        pair = jnp.concatenate([pairs[p, n, 0], pairs[p, n, 1]], axis=1)
        part[i % 2] = dot(pair, out_pair[...] if n else in_pair[...])

    for copy in loads[0::2]:
        copy.wait()
    project(0)
    for i in range(8):
        p, n = (i % 4, i // 4)
        if i == 3:
            for copy in loads[1::2] + [table_load]:
                copy.wait()
        if i < 7:
            project(i + 1)
        lanes = slice(n * half + p * PAIR, n * half + (p + 1) * PAIR)

        @pl.loop(0, 128, step=RB, unroll=True)
        def _(rows):
            rows = pl.multiple_of(rows, RB)
            x = [part[i % 2, pl.ds(128 * r + rows, RB), :] for r in range(8)]
            if n == 0:
                x = [jnp.maximum(v, 0.0) for v in x]
                for r in range(8):
                    inner[pl.ds(128 * r + rows, RB), lanes] = x[r].astype(BF16)
            for block, both in enumerate(eight_points(x)):
                for k in range(2):
                    eights[block, pl.ds(128 * k + rows, RB), lanes] = both[k].astype(BF16)

    stores = [pltpu.make_async_copy(inner, inner_out, out_sems.at[4])]
    stores[0].start()
    for b in range(4):
        rows = pl.ds(b * 256, 256)
        prod = dot(held[b], eights[b])
        result[rows, 0:half] = prod[:, 0:half].astype(BF16)
        if b == 0:
            row = iota((256, half), 0)
            factor = jnp.where((row == 0) | (row == PER_GROUP), 0.5, 1.0)
            result[rows, half:] = (prod[:, half:] * factor).astype(BF16)
        else:
            result[rows, half:] = prod[:, half:].astype(BF16)
        stores.append(pltpu.make_async_copy(result.at[rows], spec_out.at[rows], out_sems.at[b]))
        stores[-1].start()
    for copy in stores:
        copy.wait()


def rows_forward(maps, cot, in_w, out_w, table):
    return pl.pallas_call(
        rows_kernel,
        grid=(1,),
        in_specs=[ANY, ANY, whole_spec((SPEC_CH, 128)), whole_spec((SPEC_CH, 128)), ANY],
        out_specs=[ANY, ANY],
        out_shape=[
            pltpu.HBM((1024, 1024), BF16),
            pltpu.HBM((WIDTH, 512), BF16),
        ],
        scratch_shapes=[
            pltpu.VMEM((4, 2, 2, WIDTH, 128), BF16),
            pltpu.VMEM((4, 256, 256), BF16),
            pltpu.VMEM((2, WIDTH, PAIR), F32),
            pltpu.VMEM((WIDTH, 512), BF16),
            pltpu.VMEM((4, 256, 1024), BF16),
            pltpu.VMEM((1024, 1024), BF16),
            pltpu.VMEM((256, PAIR), BF16),
            pltpu.VMEM((256, PAIR), BF16),
            pltpu.SemaphoreType.DMA((4, 2)),
            pltpu.SemaphoreType.DMA,
            pltpu.SemaphoreType.DMA((5,)),
        ],
        compiler_params=params(),
        cost_estimate=cost(5 * 10**9, 11 * 2**20),
    )(maps, cot, in_w, out_w, table)


def lane_signs(shape):
    return jnp.where(iota(shape, 1) % PAIR < SPEC_CH, 1.0, -1.0).astype(F32)


def lane_butterfly(x, signs):
    return pltpu.roll(x, SPEC_CH, 1) + x * signs


def turn_second(re, im, first, real, imag):
    new_re = jnp.where(first, re, re * real - im * imag)
    new_im = jnp.where(first, im, re * imag + im * real)
    return new_re, new_im


EIGHTHS = ((1.0, 0.0), (ROOT, -ROOT), (0.0, -1.0), (-ROOT, -ROOT))


def spectrum_rows(prod, twiddle, rows, signs, first):
    re, im = [], []
    for m in range(4):
        lanes = slice(m * PAIR, (m + 1) * PAIR)
        a = prod[pl.ds(rows, RB), lanes]
        b = prod[pl.ds(GROUPS + rows, RB), lanes]
        c = twiddle[0, pl.ds(rows, RB), lanes]
        s = twiddle[1, pl.ds(rows, RB), lanes]
        re.append(a * c + b * s)
        im.append(b * c - a * s)
    s0r, s0i, d0r, d0i = re[0] + re[2], im[0] + im[2], re[0] - re[2], im[0] - im[2]
    s1r, s1i, d1r, d1i = re[1] + re[3], im[1] + im[3], re[1] - re[3], im[1] - im[3]
    four = (
        (s0r + s1r, s0i + s1i),
        (d0r + d1i, d0i - d1r),
        (s0r - s1r, s0i - s1i),
        (d0r - d1i, d0i + d1r),
    )
    out = []
    for q in range(4):
        zr, zi = four[q]
        if q:
            zr, zi = turn_second(zr, zi, first, *EIGHTHS[q])
        out.append((lane_butterfly(zr, signs), lane_butterfly(zi, signs)))
    return out


def inverse_rows(parts, twiddle, rows, signs, first):
    z = []
    for q in range(4):
        zr, zi = (lane_butterfly(x, signs) for x in parts[q])
        if q:
            zr, zi = turn_second(zr, zi, first, EIGHTHS[q][0], -EIGHTHS[q][1])
        z.append((zr, zi))
    s0r, s0i = z[0][0] + z[2][0], z[0][1] + z[2][1]
    d0r, d0i = z[0][0] - z[2][0], z[0][1] - z[2][1]
    s1r, s1i = z[1][0] + z[3][0], z[1][1] + z[3][1]
    d1r, d1i = z[1][0] - z[3][0], z[1][1] - z[3][1]
    four = (
        (s0r + s1r, s0i + s1i),
        (d0r - d1i, d0i + d1r),
        (s0r - s1r, s0i - s1i),
        (d0r + d1i, d0i - d1r),
    )
    out = []
    for m in range(4):
        lanes = slice(m * PAIR, (m + 1) * PAIR)
        c = twiddle[0, pl.ds(rows, RB), lanes]
        s = twiddle[1, pl.ds(rows, RB), lanes]
        a, b = four[m]
        out.append((a * c - b * s, b * c + a * s))
    return out


def fill_mix(mix_w, wide):
    total = jnp.zeros((256, 256), F32)
    for t in range(2):
        row, col = iota((256, 128), 0), iota((256, 128), 1)
        at = (row // PAIR) * SPEC_CH + row % SPEC_CH
        hit = (at == col) & (row // SPEC_CH % 2 == t)
        pick = jnp.where(hit, 1.0, 0.0).astype(BF16)
        left = dot(pick, mix_w[...]).astype(BF16)
        total = total + lax.dot_general(
            left, pick, (((1,), (1,)), ((), ())), preferred_element_type=F32
        )
    wide[...] = total.astype(BF16)


def sigmoid(x):
    return 0.5 * jnp.tanh(0.5 * x) + 0.5


def gather_parts(stage, kk):
    lanes = []
    for m in range(4):
        re = stage[m, pl.ds(kk, GROUPS, stride=ROWS), :]
        im = stage[m, pl.ds(PER_GROUP + kk, GROUPS, stride=ROWS), :]
        lanes.append(jnp.concatenate([re, im], axis=0).astype(BF16))
    return jnp.concatenate(lanes, axis=1)


def fill_stage(block, stage):
    for m in range(4):
        stage[m] = block[:, m * PAIR : (m + 1) * PAIR].astype(F32)


def columns_kernel(
    block, forward_in, backward_in, twiddle_in, mix_in, above, below, spec_out, back_out,
    land, forward, backward, twiddle, wide, spec, stage, back, prod, pre, inv, sems, out_sems,
):
    del above, below
    mix_load = pltpu.make_async_copy(mix_in, wide, sems.at[4])
    forward_load = pltpu.make_async_copy(forward_in, forward, sems.at[5])
    twiddle_load = pltpu.make_async_copy(twiddle_in, twiddle, sems.at[6])
    backward_load = pltpu.make_async_copy(backward_in, backward, sems.at[7])
    for copy in (mix_load, forward_load, twiddle_load, backward_load):
        copy.start()
    for m in range(4):
        stage[m] = block[:, m * PAIR : (m + 1) * PAIR].astype(F32)
    mix_load.wait()
    forward_load.wait()
    twiddle_load.wait()
    backward_load.wait()
    stores = []
    signs = lane_signs((RB, PAIR))
    first = iota((RB, PAIR), 1) < SPEC_CH
    def transform(kk):
        prod[kk % 2] = dot(forward[...], gather_parts(stage, kk))

    def spectrum(kk):
        @pl.loop(0, GROUPS, step=RB, unroll=True)
        def _(rows):
            rows = pl.multiple_of(rows, RB)
            parts = spectrum_rows(prod.at[kk % 2], twiddle, rows, signs, first)
            for q in range(4):
                spec[kk * 4 + q, pl.ds(rows, RB), 0:PAIR] = parts[q][0].astype(BF16)
                spec[kk * 4 + q, pl.ds(rows, RB), PAIR:] = parts[q][1].astype(BF16)

        part = pl.ds(kk * 4, 4)
        stores.append(pltpu.make_async_copy(spec.at[part], spec_out.at[part], out_sems.at[kk]))
        stores[-1].start()

    def mix(kk):
        pre[kk % 2] = dot(spec[kk * 4 : kk * 4 + 4].reshape(512, 256), wide[...])

    def activate(kk):
        @pl.loop(0, GROUPS, step=RB, unroll=True)
        def _(rows):
            rows = pl.multiple_of(rows, RB)
            parts = []
            for q in range(4):
                v = pre[kk % 2, pl.ds(q * GROUPS + rows, RB), :]
                v = v * sigmoid(v)
                parts.append((v[:, 0:PAIR], v[:, PAIR:]))
            pairs = inverse_rows(parts, twiddle, rows, signs, first)
            for m in range(4):
                lanes = slice(m * PAIR, (m + 1) * PAIR)
                inv[kk % 2, pl.ds(rows, RB), lanes] = pairs[m][0].astype(BF16)
                inv[kk % 2, pl.ds(GROUPS + rows, RB), lanes] = pairs[m][1].astype(BF16)

    def transform_back(kk):
        result = dot(backward[...], inv[kk % 2])
        for m in range(4):
            lanes = slice(m * PAIR, (m + 1) * PAIR)
            back[m, pl.ds(kk, GROUPS, stride=ROWS), :] = result[0:GROUPS, lanes]
            back[m, pl.ds(PER_GROUP + kk, GROUPS, stride=ROWS), :] = result[GROUPS:, lanes]

    transform(0)
    for kk in range(PER_GROUP + 2):
        if kk + 1 < PER_GROUP:
            transform(kk + 1)
        if kk < PER_GROUP:
            spectrum(kk)
        if 0 <= kk - 1 < PER_GROUP:
            activate(kk - 1)
        if kk < PER_GROUP:
            mix(kk)
        if 0 <= kk - 1 < PER_GROUP:
            transform_back(kk - 1)
    for m in range(4):
        land[:, m * PAIR : (m + 1) * PAIR] = back[m].astype(BF16)
        lanes = pl.ds(m * PAIR, PAIR)
        copy = pltpu.make_async_copy(land.at[:, lanes], back_out.at[:, lanes], out_sems.at[4 + m])
        copy.start()
        stores.append(copy)
    for copy in stores:
        copy.wait()


def whole_spec(shape):
    return pl.BlockSpec(shape, lambda *_: (0,) * len(shape))


def columns(block, forward, backward, twiddle, wide, above, below):
    return pl.pallas_call(
        columns_kernel,
        in_specs=[VMEM] + [ANY] * 6,
        out_specs=[ANY, ANY],
        out_shape=[
            pltpu.HBM((16, GROUPS, 256), BF16),
            pltpu.HBM((1024, 512), BF16),
        ],
        scratch_shapes=[
            pltpu.VMEM((1024, 512), BF16),
            pltpu.VMEM((256, 256), BF16),
            pltpu.VMEM((256, 256), BF16),
            pltpu.VMEM((2, GROUPS, 512), F32),
            pltpu.VMEM((256, 256), BF16),
            pltpu.VMEM((16, GROUPS, 256), BF16),
            pltpu.VMEM((4, 1024, PAIR), F32),
            pltpu.VMEM((4, 1024, PAIR), F32),
            pltpu.VMEM((2, 256, 512), F32),
            pltpu.VMEM((2, 512, 256), F32),
            pltpu.VMEM((2, 256, 512), BF16),
            pltpu.SemaphoreType.DMA((8,)),
            pltpu.SemaphoreType.DMA((8,)),
        ],
        compiler_params=params(SMALL),
        cost_estimate=cost(8 * 10**9, 5 * 2**20),
    )(block, forward, backward, twiddle, in_hbm(wide), above, below)


def mix_kernel(block, spec, forward, twiddle, wide, grad, stage, prod, pre, slope, acc):
    fill_stage(block, stage)
    signs = lane_signs((RB, PAIR))
    first = iota((RB, PAIR), 1) < SPEC_CH
    acc[...] = jnp.zeros_like(acc)
    for kk in range(PER_GROUP):
        prod[...] = dot(forward[...], gather_parts(stage, kk))
        pre[...] = dot(spec[kk * 4 : kk * 4 + 4].reshape(512, 256), wide[...])

        @pl.loop(0, GROUPS, step=RB, unroll=True)
        def _(rows):
            rows = pl.multiple_of(rows, RB)
            parts = spectrum_rows(prod, twiddle, rows, signs, first)
            for q in range(4):
                for part in range(2):
                    lanes = slice(part * PAIR, (part + 1) * PAIR)
                    v = pre[pl.ds(q * GROUPS + rows, RB), lanes]
                    s = sigmoid(v)
                    v = parts[q][part] * (s * (1.0 + v * (1.0 - s)))
                    slope[pl.ds(q * GROUPS + rows, RB), lanes] = v.astype(BF16)

        acc[...] += dot_t(slope[...], spec[kk * 4 : kk * 4 + 4].reshape(512, 256))
    lane = iota((SPEC_CH, PAIR), 1) < SPEC_CH
    for part in range(2):
        even = acc[part * PAIR : part * PAIR + SPEC_CH, :]
        odd = acc[part * PAIR + SPEC_CH : (part + 1) * PAIR, :]
        real = even[:, 0:PAIR] + pltpu.roll(odd[:, 0:PAIR], SPEC_CH, 1)
        imag = pltpu.roll(even[:, PAIR:], SPEC_CH, 1) + odd[:, PAIR:]
        grad[part * SPEC_CH : (part + 1) * SPEC_CH, :] = jnp.where(lane, real, imag)


def mix_terms(block, spec, forward, twiddle, wide):
    return pl.pallas_call(
        mix_kernel,
        grid=(1,),
        in_specs=[
            pl.BlockSpec((1024, 512), lambda i: (0, 1)),
            whole_spec((16, GROUPS, 256)),
            whole_spec((256, 256)),
            whole_spec((2, GROUPS, 512)),
            whole_spec((256, 256)),
        ],
        out_specs=whole_spec((128, 128)),
        out_shape=jax.ShapeDtypeStruct((128, 128), F32),
        scratch_shapes=[
            pltpu.VMEM((4, 1024, PAIR), F32),
            pltpu.VMEM((256, 512), F32),
            pltpu.VMEM((512, 256), F32),
            pltpu.VMEM((512, 256), BF16),
            pltpu.VMEM((256, 256), F32),
        ],
        compiler_params=params(),
        cost_estimate=cost(6 * 10**9, 5 * 2**20),
    )(block, spec, forward, twiddle, wide)


def back_kernel(
    table, block, inner, cot, mix_part, ready, summed_out, terms_out,
    held, inners, cots, mix, summed, terms, packed, parts, sems, out_sems,
):
    del ready

    def load(source, target, sem):
        copy = pltpu.make_async_copy(source, target, sems.at[sem])
        copy.start()
        return copy

    first = load(table, held, 0)
    second = load(inner, inners, 1)
    pairs = [load(cot.at[0, pl.ds(2 * p, 2)], cots.at[p], 2 + p) for p in range(4)]
    last = load(mix_part, mix, 6)
    first.wait()
    for b in range(4):
        parts[b] = dot(held[b], block[b * 256 : (b + 1) * 256, :])
    second.wait()
    acc = jnp.zeros((PAIR, 256), F32)
    for p in range(4):
        lanes = slice(p * PAIR, (p + 1) * PAIR)

        @pl.loop(0, 128, step=RB, unroll=True)
        def _(rows):
            rows = pl.multiple_of(rows, RB)
            u = [
                [parts[b, pl.ds(128 * i + rows, RB), lanes] for i in range(2)] for b in range(4)
            ]
            for r, x in enumerate(eight_back(u)):
                at = pl.ds(128 * r + rows, RB)
                summed[at, lanes] = (x + inners[at, lanes].astype(F32)).astype(BF16)

        pairs[p].wait()
        pair = jnp.concatenate([cots[p, 0], cots[p, 1]], axis=1)
        acc = acc + dot_t(summed[:, lanes], pair)
    store = pltpu.make_async_copy(summed, summed_out, out_sems.at[0])
    store.start()
    last.wait()
    out_part = acc[0:SPEC_CH, 0:128] + acc[SPEC_CH:, 128:]
    high = out_part.astype(BF16).astype(F32)
    out_both = jnp.concatenate([high, out_part - high], axis=0).T
    for img in range(2):
        terms[pl.ds(2 * img, 128, stride=4), :] = mix[...]
        terms[pl.ds(2 * img + 1, 128, stride=4), :] = out_both
    packed[...] = terms[...].astype(BF16)
    copy = pltpu.make_async_copy(packed, terms_out, out_sems.at[1])
    copy.start()
    store.wait()
    copy.wait()


def back_rows(table, rows, inner, cot, mix_part, ready):
    return pl.pallas_call(
        back_kernel,
        in_specs=[ANY, VMEM, ANY, ANY, ANY, ANY],
        out_specs=[ANY, ANY],
        out_shape=[
            pltpu.HBM((WIDTH, 512), BF16),
            pltpu.HBM((512, 128), BF16),
        ],
        scratch_shapes=[
            pltpu.VMEM((4, 256, 256), BF16),
            pltpu.VMEM((WIDTH, 512), BF16),
            pltpu.VMEM((4, 2, WIDTH, 128), BF16),
            pltpu.VMEM((128, 128), F32),
            pltpu.VMEM((WIDTH, 512), BF16),
            pltpu.VMEM((512, 128), F32),
            pltpu.VMEM((512, 128), BF16),
            pltpu.VMEM((4, 256, 512), F32),
            pltpu.SemaphoreType.DMA((7,)),
            pltpu.SemaphoreType.DMA((2,)),
        ],
        compiler_params=params(SMALL),
        cost_estimate=cost(2 * 10**9, 8 * 2**20),
    )(in_hbm(table), rows, in_hbm(inner), in_hbm(cot), in_hbm(mix_part), in_hbm(ready))


def out_kernel(summed, out_w, out, held, wide, result, sems, out_sems):
    loads = []
    for p in range(4):
        lanes = pl.ds(p * PAIR, PAIR)
        loads.append(pltpu.make_async_copy(summed.at[:, lanes], held.at[p], sems.at[p]))
        loads[p].start()
    zero = jnp.zeros((SPEC_CH, 128), BF16)
    wide[0:SPEC_CH, :] = jnp.concatenate([out_w[...], zero], axis=1)
    wide[SPEC_CH:, :] = jnp.concatenate([zero, out_w[...]], axis=1)
    stores = []
    for p in range(4):
        loads[p].wait()
        prod = dot(held[p], wide[...])
        result[2 * p] = prod[:, 0:128].astype(BF16)
        result[2 * p + 1] = prod[:, 128:].astype(BF16)
        rows = pl.ds(2 * p, 2)
        stores.append(pltpu.make_async_copy(result.at[rows], out.at[0, rows], out_sems.at[p]))
        stores[p].start()
    for copy in stores:
        copy.wait()


def project_out(summed, out_w):
    return pl.pallas_call(
        out_kernel,
        grid=(1,),
        in_specs=[ANY, whole_spec((SPEC_CH, 128))],
        out_specs=ANY,
        out_shape=pltpu.HBM((1, ROWS, WIDTH, 128), BF16),
        scratch_shapes=[
            pltpu.VMEM((4, WIDTH, PAIR), BF16),
            pltpu.VMEM((128, 256), BF16),
            pltpu.VMEM((ROWS, WIDTH, 128), BF16),
            pltpu.SemaphoreType.DMA((4,)),
            pltpu.SemaphoreType.DMA((4,)),
        ],
        compiler_params=params(),
        cost_estimate=cost(5 * 10**8, 3 * 2**20),
    )(summed, out_w)


def fill_wide(weight, wide, sums):
    for a in range(3):
        for b in range(3):
            wide[a * 128 : (a + 1) * 128, b * 128 : (b + 1) * 128] = weight[a, b]
    sums[0, 0:8] = jnp.zeros((8, 128), F32)
    sums[2, WIDTH + 8 :] = jnp.zeros((8, 128), F32)


def conv_sums(top, mid, bottom, sums, wide):
    prod = dot(jnp.concatenate([top, mid, bottom], axis=1), wide[...])
    for b in range(3):
        sums[b, 8 : WIDTH + 8] = prod[:, b * 128 : (b + 1) * 128]
    total = sums[0, 7 : WIDTH + 7] + sums[1, 8 : WIDTH + 8] + sums[2, 9 : WIDTH + 9]
    return total.astype(BF16)


def conv_row(top, mid, bottom, weight, out, sums, wide):
    @pl.when(pl.program_id(0) == 0)
    def _():
        fill_wide(weight, wide, sums)

    out[0, 0] = conv_sums(top, mid, bottom, sums, wide)


def inner_kernel(above, mid, below, weight, mix_w, ready, out, mix, sums, wide):
    del ready
    conv_row(above[0, 0], mid[0, 0], below[0, 0], weight, out, sums, wide)

    @pl.when(pl.program_id(0) == 0)
    def _():
        fill_mix(mix_w, mix)


def edge_kernel(
    mid, beside, edge_above, edge_below, weight, done, ready, out, token, sums, wide
):
    del done, ready
    token[...] = jnp.zeros((8, 128), F32)
    first = pl.program_id(0) == 0
    top = jnp.where(first, edge_above[0, 0], beside[0, 0])
    bottom = jnp.where(first, beside[0, 0], edge_below[0, 0])
    conv_row(top, mid[0, 0], bottom, weight, out, sums, wide)


def sum_kernel(terms, mix, out):
    total = jnp.sum(terms[...].astype(F32).reshape(64, 8, 128), axis=0)
    even = iota((8, 128), 0) % 2 == 0
    mix[...] = jnp.sum(jnp.where(even, total, 0.0), axis=0, keepdims=True)
    odd = jnp.sum(jnp.where(even, 0.0, total), axis=0, keepdims=True)
    out[...] = odd[:, 0:SPEC_CH] + odd[:, SPEC_CH:]


def sum_terms(terms):
    return pl.pallas_call(
        sum_kernel,
        in_specs=[VMEM],
        out_specs=[VMEM, VMEM],
        out_shape=[
            jax.ShapeDtypeStruct((1, 128), F32),
            jax.ShapeDtypeStruct((1, SPEC_CH), F32),
        ],
        compiler_params=params(SMALL),
        cost_estimate=cost(10**6, 2**17),
    )(terms)


def row_spec(index):
    return pl.BlockSpec((1, 1, WIDTH, 128), lambda i: (0, index(i), 0, 0))


def conv_call(kernel, rows, in_specs, out_index, second, aliases, args):
    return pl.pallas_call(
        kernel,
        grid=(rows,),
        in_specs=in_specs,
        out_specs=[row_spec(out_index), whole_spec(second.shape)],
        out_shape=[
            pltpu.HBM((1, ROWS, WIDTH, 128), BF16),
            second,
        ],
        scratch_shapes=[pltpu.VMEM((3, WIDTH + 16, 128), F32), pltpu.VMEM((384, 384), BF16)],
        input_output_aliases=aliases,
        compiler_params=params(),
        cost_estimate=cost(rows * 10**9, rows * 2**20),
    )(*args)


def inner_rows(cells, weight, mix_w, ready):
    specs = [
        row_spec(lambda i: i),
        row_spec(lambda i: i + 1),
        row_spec(lambda i: i + 2),
        whole_spec((3, 3, 128, 128)),
        whole_spec((128, 128)),
        pl.BlockSpec(memory_space=pl.ANY),
    ]
    args = (cells, cells, cells, weight, mix_w, ready)
    second = jax.ShapeDtypeStruct((256, 256), BF16)
    return conv_call(inner_kernel, ROWS - 2, specs, lambda i: i + 1, second, {}, args)


BLOCK = 8


def neighbour_rows(cells):
    head, tail = cells[:, 0:1], cells[:, ROWS - 1 :]
    near = [i for i in range(GROUPS - 1) if i % BLOCK != BLOCK - 1]
    above = lax.ppermute(tail, "rows", [(i, i + 1) for i in near])
    below = lax.ppermute(head, "rows", [(i + 1, i) for i in near])
    return above, below


def far_row(cells):
    last = lax.axis_index("rows") % BLOCK == BLOCK - 1
    row = lax.dynamic_slice_in_dim(cells, jnp.where(last, ROWS - 1, 0), 1, axis=1)
    far = range(BLOCK - 1, GROUPS - 1, BLOCK)
    return lax.ppermute(row, "rows", [(i, i + 1) for i in far] + [(i + 1, i) for i in far])


def edge_rows(cells, above, below, weight, done, ready):
    specs = [
        row_spec(lambda i: i * (ROWS - 1)),
        row_spec(lambda i: 1 + i * (ROWS - 3)),
        whole_spec((1, 1, WIDTH, 128)),
        whole_spec((1, 1, WIDTH, 128)),
        whole_spec((3, 3, 128, 128)),
        pl.BlockSpec(memory_space=pl.ANY),
        pl.BlockSpec(memory_space=pl.ANY),
    ]
    args = (cells, cells, above, below, weight, done, ready)
    second = jax.ShapeDtypeStruct((8, 128), F32)
    return conv_call(edge_kernel, 2, specs, lambda i: i * (ROWS - 1), second, {5: 0}, args)


def far_kernel(cells, above, far, weight_in, done, ready, out, lines, weight, row_out, sums, wide, sems):
    del done, ready
    at = lax.axis_index("rows") % BLOCK
    last = at == BLOCK - 1
    row = jnp.where(last, ROWS - 1, 0)
    beside = jnp.where(last, ROWS - 2, 1)
    outer = jnp.where(last, 2, 0)
    weights = pltpu.make_async_copy(weight_in, weight, sems.at[0])
    weights.start()
    own = pltpu.make_async_copy(cells.at[0, row], lines.at[1], sems.at[1])
    own.start()
    inside = pltpu.make_async_copy(cells.at[0, beside], lines.at[2 - outer], sems.at[2])
    inside.start()

    @pl.when((at == 0) | last)
    def _():
        pltpu.make_async_copy(far.at[0, 0], lines.at[outer], sems.at[3]).start()

    @pl.when((at > 0) & (at < BLOCK - 1))
    def _():
        pltpu.make_async_copy(above.at[0, 0], lines.at[outer], sems.at[3]).start()

    weights.wait()
    fill_wide(weight, wide, sums)
    own.wait()
    inside.wait()
    pltpu.make_async_copy(above.at[0, 0], lines.at[outer], sems.at[3]).wait()
    row_out[...] = conv_sums(lines[0], lines[1], lines[2], sums, wide)
    copy = pltpu.make_async_copy(row_out, out.at[0, row], sems.at[4])
    copy.start()
    copy.wait()


def far_edge(cells, above, far, weight, done, ready):
    return pl.pallas_call(
        far_kernel,
        in_specs=[ANY] * 6,
        out_specs=ANY,
        out_shape=pltpu.HBM((1, ROWS, WIDTH, 128), BF16),
        scratch_shapes=[
            pltpu.VMEM((3, WIDTH, 128), BF16),
            pltpu.VMEM((3, 3, 128, 128), BF16),
            pltpu.VMEM((WIDTH, 128), BF16),
            pltpu.VMEM((3, WIDTH + 16, 128), F32),
            pltpu.VMEM((384, 384), BF16),
            pltpu.SemaphoreType.DMA((5,)),
        ],
        input_output_aliases={4: 0},
        compiler_params=params(SMALL),
        cost_estimate=cost(10**9, 2**20),
    )(in_hbm(cells), in_hbm(above), far, in_hbm(weight), in_hbm(done), in_hbm(ready))


def exchange(block):
    lanes = block.shape[1]
    moved = lax.all_to_all(
        block.reshape(GROUPS, ROWS, lanes), "rows", split_axis=0, concat_axis=0, tiled=True
    )
    return moved.reshape(GROUPS * ROWS, lanes)


def shards(local_maps, global_maps, conv_weight, in_weight, mix_weight, out_weight, out_cotangent):
    row_fwd, row_inv = row_tables()
    forward, backward, twiddle = column_tables()
    spec_rows, inner = rows_forward(global_maps, out_cotangent, in_weight.T, out_weight, row_fwd)
    spec_cols = exchange(spec_rows)
    local_inner, wide = inner_rows(local_maps, conv_weight, mix_weight, spec_rows)
    above, below = neighbour_rows(local_maps)
    spectrum, back_cols = columns(
        spec_cols, forward, backward, twiddle, wide, above, below
    )
    back = exchange(back_cols)
    mix_part = mix_terms(spec_cols, spectrum, forward, twiddle, wide)
    local_out, token = edge_rows(local_maps, above, below, conv_weight, local_inner, back_cols)
    summed, terms = back_rows(row_inv, back, inner, out_cotangent, mix_part, token)
    local_out = far_edge(
        local_maps, above, far_row(local_maps), conv_weight, local_out, in_hbm(terms)
    )
    terms = terms.reshape(256, 2, 128)
    terms = lax.all_to_all(terms, ("rows", "img"), split_axis=0, concat_axis=0, tiled=True)
    global_out = project_out(summed, out_weight)
    mix_grad, out_grad = sum_terms(terms.reshape(512, 128))
    mix_grad, out_grad = mix_grad.reshape(128, 1), out_grad.reshape(SPEC_CH, 1)
    return (local_out, global_out, mix_grad, out_grad)


def solution(mesh):
    maps = P("img", "rows", None, None)
    in_specs = (maps, maps, P(), P(), P(), P(), maps)
    out_specs = (maps, maps, P(None, "rows"), P(None, "rows"))
    return jax.shard_map(shards, mesh=mesh, in_specs=in_specs, out_specs=out_specs, check_vma=False)
```

```python
import math

import jax
import jax.numpy as jnp
import ml_dtypes
import numpy as np
from jax import lax
from jax.experimental import pallas as pl
from jax.experimental.pallas import tpu as pltpu
from jax.sharding import PartitionSpec as P

HEIGHT = 1024
WIDTH = 1024
SPEC_CH = 64
FREQS = 512
ROWS = 8
GROUPS = 128
PER_GROUP = 4
PAIR = 128
BF16 = jnp.bfloat16
F32 = jnp.float32

LIMIT = 60 * 2**20
SMALL = 40 * 2**20


def params(limit=LIMIT):
    return pltpu.CompilerParams(vmem_limit_bytes=limit)


def in_hbm(x):
    return pltpu.with_memory_space_constraint(x, pltpu.HBM)


VMEM = pl.BlockSpec(memory_space=pltpu.VMEM)


ANY = pl.BlockSpec(memory_space=pl.ANY)


def cost(flops, nbytes):
    return pl.CostEstimate(flops=flops, bytes_accessed=nbytes, transcendentals=0)


FIRSTS = ((0, 4), (1, 7), (2, 6), (3, 5))


def row_tables():
    s = np.arange(128)
    forward = np.zeros((4, 2, 16, 2, PER_GROUP, 2, 128))
    inverse = np.zeros((4, 2, 128, 2, 16, 2, PER_GROUP))
    for b, firsts in enumerate(FIRSTS):
        for half, k0 in enumerate(firsts):
            k = k0 + 8 * np.arange(64).reshape(16, PER_GROUP, 1)
            phase = (k * s % WIDTH) * (2.0 * math.pi / WIDTH)
            cosine, sine = np.cos(phase) / 32.0, np.sin(phase) / 32.0
            factor = np.where(k == 0, 1.0, 2.0)
            sign = 1.0 if half else -1.0
            if b == 0:
                forward[b, half, :, 0, :, half] = cosine
                forward[b, half, :, 1, :, half] = -sine
                inverse[b, half, :, half, :, 0] = (cosine * factor).transpose(2, 0, 1)
                inverse[b, half, :, half, :, 1] = (-sine * factor).transpose(2, 0, 1)
                continue
            forward[b, half, :, 0, :, 0] = cosine
            forward[b, half, :, 0, :, 1] = sign * sine
            forward[b, half, :, 1, :, 0] = -sine
            forward[b, half, :, 1, :, 1] = sign * cosine
            inverse[b, 0, :, half, :, 0] = (cosine * factor).transpose(2, 0, 1)
            inverse[b, 0, :, half, :, 1] = (-sine * factor).transpose(2, 0, 1)
            inverse[b, 1, :, half, :, 0] = (-sign * sine * factor).transpose(2, 0, 1)
            inverse[b, 1, :, half, :, 1] = (-sign * cosine * factor).transpose(2, 0, 1)
    forward = forward.reshape(4, 256, 256).astype(ml_dtypes.bfloat16)
    return forward, inverse.reshape(4, 256, 256).astype(ml_dtypes.bfloat16)


def column_tables():
    idx = np.arange(GROUPS)
    phase = ((idx[:, None] * idx[None, :]) % GROUPS) * (2.0 * math.pi / GROUPS)
    cosine, sine = np.cos(phase) / math.sqrt(HEIGHT), np.sin(phase) / math.sqrt(HEIGHT)
    forward = np.block([[cosine, sine], [-sine, cosine]])
    backward = np.block([[cosine, -sine], [sine, cosine]])
    turn = (idx[:, None] * np.arange(ROWS)[None, :]) * (2.0 * math.pi / HEIGHT)
    twiddle = np.repeat(np.stack([np.cos(turn), np.sin(turn)]), SPEC_CH, axis=2)
    return (
        forward.astype(ml_dtypes.bfloat16),
        backward.astype(ml_dtypes.bfloat16),
        twiddle.astype(np.float32),
    )


def dot(a, b):
    return jnp.dot(a, b, preferred_element_type=F32)


def dot_t(a, b):
    return lax.dot_general(a, b, (((0,), (0,)), ((), ())), preferred_element_type=F32)


def iota(shape, dim):
    return lax.broadcasted_iota(jnp.int32, shape, dim)


def first_half():
    return jnp.where(iota((SPEC_CH, PAIR), 0) == iota((SPEC_CH, PAIR), 1), 1.0, 0.0).astype(BF16)


def second_half():
    hit = iota((SPEC_CH, PAIR), 0) + SPEC_CH == iota((SPEC_CH, PAIR), 1)
    return jnp.where(hit, 1.0, 0.0).astype(BF16)


ROOT = math.sqrt(0.5)
RB = 16


def eight_points(x):
    a = [x[r] + x[r + 4] for r in range(4)]
    b = [x[r] - x[r + 4] for r in range(4)]
    even, odd = a[0] + a[2], a[1] + a[3]
    c, d = (b[1] - b[3]) * ROOT, (b[1] + b[3]) * ROOT
    return (
        (even + odd, even - odd),
        (b[0] + c, d + b[2]),
        (a[0] - a[2], a[1] - a[3]),
        (b[0] - c, d - b[2]),
    )


def eight_back(u):
    (u0, u4), (p1, q1), (p2, q2), (p3, q3) = u
    total, rest = u0 + u4, u0 - u4
    even = (total + p2, rest - q2, total - p2, rest + q2)
    c, d = (p1 - p3) * ROOT, (q1 + q3) * ROOT
    odd = (p1 + p3, c - d, q3 - q1, -c - d)
    return [even[r] + odd[r] for r in range(4)] + [even[r] - odd[r] for r in range(4)]


def rows_kernel(
    maps, cot, in_w, out_w, table, spec_out, inner_out,
    pairs, held, part, inner, eights, result, in_pair, out_pair, sems, table_sem, out_sems,
):
    half = ROWS * SPEC_CH
    loads = []
    for p in range(4):
        for n, source in enumerate((maps, cot)):
            rows = source.at[0, pl.ds(2 * p, 2)]
            loads.append(pltpu.make_async_copy(rows, pairs.at[p, n], sems.at[p, n]))
    table_load = pltpu.make_async_copy(table, held, table_sem)
    def start(i):
        p, n = (i % 4, i // 4)
        loads[2 * p + n].start()

    for i in range(8):
        start(i)
    table_load.start()
    a, b = first_half(), second_half()
    in_pair[0:PAIR, :] = dot_t(in_w[...], a).astype(BF16)
    in_pair[PAIR:, :] = dot_t(in_w[...], b).astype(BF16)
    out_pair[0:PAIR, :] = (2.0 * dot_t(out_w[...], a)).astype(BF16)
    out_pair[PAIR:, :] = (2.0 * dot_t(out_w[...], b)).astype(BF16)
    def project(i):
        p, n = (i % 4, i // 4)
        pair = jnp.concatenate([pairs[p, n, 0], pairs[p, n, 1]], axis=1)
        part[i % 2] = dot(pair, out_pair[...] if n else in_pair[...])

    for copy in loads[0::2]:
        copy.wait()
    project(0)
    for i in range(8):
        p, n = (i % 4, i // 4)
        if i == 3:
            for copy in loads[1::2] + [table_load]:
                copy.wait()
        if i < 7:
            project(i + 1)
        lanes = slice(n * half + p * PAIR, n * half + (p + 1) * PAIR)

        @pl.loop(0, 128, step=RB, unroll=True)
        def _(rows):
            rows = pl.multiple_of(rows, RB)
            x = [part[i % 2, pl.ds(128 * r + rows, RB), :] for r in range(8)]
            if n == 0:
                x = [jnp.maximum(v, 0.0) for v in x]
                for r in range(8):
                    inner[pl.ds(128 * r + rows, RB), lanes] = x[r].astype(BF16)
            for block, both in enumerate(eight_points(x)):
                for k in range(2):
                    eights[block, pl.ds(128 * k + rows, RB), lanes] = both[k].astype(BF16)

    stores = [pltpu.make_async_copy(inner, inner_out, out_sems.at[4])]
    stores[0].start()
    for b in range(4):
        rows = pl.ds(b * 256, 256)
        prod = dot(held[b], eights[b])
        result[rows, 0:half] = prod[:, 0:half].astype(BF16)
        if b == 0:
            row = iota((256, half), 0)
            factor = jnp.where((row == 0) | (row == PER_GROUP), 0.5, 1.0)
            result[rows, half:] = (prod[:, half:] * factor).astype(BF16)
        else:
            result[rows, half:] = prod[:, half:].astype(BF16)
        stores.append(pltpu.make_async_copy(result.at[rows], spec_out.at[rows], out_sems.at[b]))
        stores[-1].start()
    for copy in stores:
        copy.wait()


def rows_forward(maps, cot, in_w, out_w, table):
    return pl.pallas_call(
        rows_kernel,
        grid=(1,),
        in_specs=[ANY, ANY, whole_spec((SPEC_CH, 128)), whole_spec((SPEC_CH, 128)), ANY],
        out_specs=[ANY, ANY],
        out_shape=[
            pltpu.HBM((1024, 1024), BF16),
            pltpu.HBM((WIDTH, 512), BF16),
        ],
        scratch_shapes=[
            pltpu.VMEM((4, 2, 2, WIDTH, 128), BF16),
            pltpu.VMEM((4, 256, 256), BF16),
            pltpu.VMEM((2, WIDTH, PAIR), F32),
            pltpu.VMEM((WIDTH, 512), BF16),
            pltpu.VMEM((4, 256, 1024), BF16),
            pltpu.VMEM((1024, 1024), BF16),
            pltpu.VMEM((256, PAIR), BF16),
            pltpu.VMEM((256, PAIR), BF16),
            pltpu.SemaphoreType.DMA((4, 2)),
            pltpu.SemaphoreType.DMA,
            pltpu.SemaphoreType.DMA((5,)),
        ],
        compiler_params=params(),
        cost_estimate=cost(5 * 10**9, 11 * 2**20),
    )(maps, cot, in_w, out_w, table)


def lane_signs(shape):
    return jnp.where(iota(shape, 1) % PAIR < SPEC_CH, 1.0, -1.0).astype(F32)


def lane_butterfly(x, signs):
    return pltpu.roll(x, SPEC_CH, 1) + x * signs


def turn_second(re, im, first, real, imag):
    new_re = jnp.where(first, re, re * real - im * imag)
    new_im = jnp.where(first, im, re * imag + im * real)
    return new_re, new_im


EIGHTHS = ((1.0, 0.0), (ROOT, -ROOT), (0.0, -1.0), (-ROOT, -ROOT))


def spectrum_rows(prod, twiddle, rows, signs, first):
    re, im = [], []
    for m in range(4):
        lanes = slice(m * PAIR, (m + 1) * PAIR)
        a = prod[pl.ds(rows, RB), lanes]
        b = prod[pl.ds(GROUPS + rows, RB), lanes]
        c = twiddle[0, pl.ds(rows, RB), lanes]
        s = twiddle[1, pl.ds(rows, RB), lanes]
        re.append(a * c + b * s)
        im.append(b * c - a * s)
    s0r, s0i, d0r, d0i = re[0] + re[2], im[0] + im[2], re[0] - re[2], im[0] - im[2]
    s1r, s1i, d1r, d1i = re[1] + re[3], im[1] + im[3], re[1] - re[3], im[1] - im[3]
    four = (
        (s0r + s1r, s0i + s1i),
        (d0r + d1i, d0i - d1r),
        (s0r - s1r, s0i - s1i),
        (d0r - d1i, d0i + d1r),
    )
    out = []
    for q in range(4):
        zr, zi = four[q]
        if q:
            zr, zi = turn_second(zr, zi, first, *EIGHTHS[q])
        out.append((lane_butterfly(zr, signs), lane_butterfly(zi, signs)))
    return out


def inverse_rows(parts, twiddle, rows, signs, first):
    z = []
    for q in range(4):
        zr, zi = (lane_butterfly(x, signs) for x in parts[q])
        if q:
            zr, zi = turn_second(zr, zi, first, EIGHTHS[q][0], -EIGHTHS[q][1])
        z.append((zr, zi))
    s0r, s0i = z[0][0] + z[2][0], z[0][1] + z[2][1]
    d0r, d0i = z[0][0] - z[2][0], z[0][1] - z[2][1]
    s1r, s1i = z[1][0] + z[3][0], z[1][1] + z[3][1]
    d1r, d1i = z[1][0] - z[3][0], z[1][1] - z[3][1]
    four = (
        (s0r + s1r, s0i + s1i),
        (d0r - d1i, d0i + d1r),
        (s0r - s1r, s0i - s1i),
        (d0r + d1i, d0i - d1r),
    )
    out = []
    for m in range(4):
        lanes = slice(m * PAIR, (m + 1) * PAIR)
        c = twiddle[0, pl.ds(rows, RB), lanes]
        s = twiddle[1, pl.ds(rows, RB), lanes]
        a, b = four[m]
        out.append((a * c - b * s, b * c + a * s))
    return out


def fill_mix(mix_w, wide):
    total = jnp.zeros((256, 256), F32)
    for t in range(2):
        row, col = iota((256, 128), 0), iota((256, 128), 1)
        at = (row // PAIR) * SPEC_CH + row % SPEC_CH
        hit = (at == col) & (row // SPEC_CH % 2 == t)
        pick = jnp.where(hit, 1.0, 0.0).astype(BF16)
        left = dot(pick, mix_w[...]).astype(BF16)
        total = total + lax.dot_general(
            left, pick, (((1,), (1,)), ((), ())), preferred_element_type=F32
        )
    wide[...] = total.astype(BF16)


def sigmoid(x):
    return 0.5 * jnp.tanh(0.5 * x) + 0.5


def gather_parts(stage, kk):
    lanes = []
    for m in range(4):
        re = stage[m, pl.ds(kk, GROUPS, stride=ROWS), :]
        im = stage[m, pl.ds(PER_GROUP + kk, GROUPS, stride=ROWS), :]
        lanes.append(jnp.concatenate([re, im], axis=0).astype(BF16))
    return jnp.concatenate(lanes, axis=1)


def fill_stage(block, stage):
    for m in range(4):
        stage[m] = block[:, m * PAIR : (m + 1) * PAIR].astype(F32)


def columns_kernel(
    block, forward_in, backward_in, twiddle_in, mix_in, above, below, spec_out, back_out,
    land, forward, backward, twiddle, wide, spec, stage, back, prod, pre, inv, sems, out_sems,
):
    del above, below
    mix_load = pltpu.make_async_copy(mix_in, wide, sems.at[4])
    forward_load = pltpu.make_async_copy(forward_in, forward, sems.at[5])
    twiddle_load = pltpu.make_async_copy(twiddle_in, twiddle, sems.at[6])
    backward_load = pltpu.make_async_copy(backward_in, backward, sems.at[7])
    for copy in (mix_load, forward_load, twiddle_load, backward_load):
        copy.start()
    for m in range(4):
        stage[m] = block[:, m * PAIR : (m + 1) * PAIR].astype(F32)
    forward_load.wait()
    twiddle_load.wait()
    backward_load.wait()
    stores = []
    signs = lane_signs((RB, PAIR))
    first = iota((RB, PAIR), 1) < SPEC_CH
    def transform(kk):
        prod[kk % 2] = dot(forward[...], gather_parts(stage, kk))

    def spectrum(kk):
        @pl.loop(0, GROUPS, step=RB, unroll=True)
        def _(rows):
            rows = pl.multiple_of(rows, RB)
            parts = spectrum_rows(prod.at[kk % 2], twiddle, rows, signs, first)
            for q in range(4):
                spec[kk * 4 + q, pl.ds(rows, RB), 0:PAIR] = parts[q][0].astype(BF16)
                spec[kk * 4 + q, pl.ds(rows, RB), PAIR:] = parts[q][1].astype(BF16)

        part = pl.ds(kk * 4, 4)
        stores.append(pltpu.make_async_copy(spec.at[part], spec_out.at[part], out_sems.at[kk]))
        stores[-1].start()

    def mix(kk):
        pre[kk % 2] = dot(spec[kk * 4 : kk * 4 + 4].reshape(512, 256), wide[...])

    def activate(kk):
        @pl.loop(0, GROUPS, step=RB, unroll=True)
        def _(rows):
            rows = pl.multiple_of(rows, RB)
            parts = []
            for q in range(4):
                v = pre[kk % 2, pl.ds(q * GROUPS + rows, RB), :]
                v = v * sigmoid(v)
                parts.append((v[:, 0:PAIR], v[:, PAIR:]))
            pairs = inverse_rows(parts, twiddle, rows, signs, first)
            for m in range(4):
                lanes = slice(m * PAIR, (m + 1) * PAIR)
                inv[kk % 2, pl.ds(rows, RB), lanes] = pairs[m][0].astype(BF16)
                inv[kk % 2, pl.ds(GROUPS + rows, RB), lanes] = pairs[m][1].astype(BF16)

    def transform_back(kk):
        result = dot(backward[...], inv[kk % 2])
        for m in range(4):
            lanes = slice(m * PAIR, (m + 1) * PAIR)
            back[m, pl.ds(kk, GROUPS, stride=ROWS), :] = result[0:GROUPS, lanes]
            back[m, pl.ds(PER_GROUP + kk, GROUPS, stride=ROWS), :] = result[GROUPS:, lanes]

    transform(0)
    for kk in range(PER_GROUP + 2):
        if kk + 1 < PER_GROUP:
            transform(kk + 1)
        if kk < PER_GROUP:
            spectrum(kk)
        if 0 <= kk - 1 < PER_GROUP:
            activate(kk - 1)
        if kk == 0:
            mix_load.wait()
        if kk < PER_GROUP:
            mix(kk)
        if 0 <= kk - 1 < PER_GROUP:
            transform_back(kk - 1)
    for m in range(4):
        land[:, m * PAIR : (m + 1) * PAIR] = back[m].astype(BF16)
        lanes = pl.ds(m * PAIR, PAIR)
        copy = pltpu.make_async_copy(land.at[:, lanes], back_out.at[:, lanes], out_sems.at[4 + m])
        copy.start()
        stores.append(copy)
    for copy in stores:
        copy.wait()


def whole_spec(shape):
    return pl.BlockSpec(shape, lambda *_: (0,) * len(shape))


def columns(block, forward, backward, twiddle, wide, above, below):
    return pl.pallas_call(
        columns_kernel,
        in_specs=[VMEM] + [ANY] * 6,
        out_specs=[ANY, ANY],
        out_shape=[
            pltpu.HBM((16, GROUPS, 256), BF16),
            pltpu.HBM((1024, 512), BF16),
        ],
        scratch_shapes=[
            pltpu.VMEM((1024, 512), BF16),
            pltpu.VMEM((256, 256), BF16),
            pltpu.VMEM((256, 256), BF16),
            pltpu.VMEM((2, GROUPS, 512), F32),
            pltpu.VMEM((256, 256), BF16),
            pltpu.VMEM((16, GROUPS, 256), BF16),
            pltpu.VMEM((4, 1024, PAIR), F32),
            pltpu.VMEM((4, 1024, PAIR), F32),
            pltpu.VMEM((2, 256, 512), F32),
            pltpu.VMEM((2, 512, 256), F32),
            pltpu.VMEM((2, 256, 512), BF16),
            pltpu.SemaphoreType.DMA((8,)),
            pltpu.SemaphoreType.DMA((8,)),
        ],
        compiler_params=params(SMALL),
        cost_estimate=cost(8 * 10**9, 5 * 2**20),
    )(block, forward, backward, twiddle, in_hbm(wide), above, below)


def mix_kernel(block, spec, forward, twiddle, wide, grad, stage, prod, pre, slope, acc):
    fill_stage(block, stage)
    signs = lane_signs((RB, PAIR))
    first = iota((RB, PAIR), 1) < SPEC_CH
    acc[...] = jnp.zeros_like(acc)
    for kk in range(PER_GROUP):
        prod[...] = dot(forward[...], gather_parts(stage, kk))
        pre[...] = dot(spec[kk * 4 : kk * 4 + 4].reshape(512, 256), wide[...])

        @pl.loop(0, GROUPS, step=RB, unroll=True)
        def _(rows):
            rows = pl.multiple_of(rows, RB)
            parts = spectrum_rows(prod, twiddle, rows, signs, first)
            for q in range(4):
                for part in range(2):
                    lanes = slice(part * PAIR, (part + 1) * PAIR)
                    v = pre[pl.ds(q * GROUPS + rows, RB), lanes]
                    s = sigmoid(v)
                    v = parts[q][part] * (s * (1.0 + v * (1.0 - s)))
                    slope[pl.ds(q * GROUPS + rows, RB), lanes] = v.astype(BF16)

        acc[...] += dot_t(slope[...], spec[kk * 4 : kk * 4 + 4].reshape(512, 256))
    lane = iota((SPEC_CH, PAIR), 1) < SPEC_CH
    for part in range(2):
        even = acc[part * PAIR : part * PAIR + SPEC_CH, :]
        odd = acc[part * PAIR + SPEC_CH : (part + 1) * PAIR, :]
        real = even[:, 0:PAIR] + pltpu.roll(odd[:, 0:PAIR], SPEC_CH, 1)
        imag = pltpu.roll(even[:, PAIR:], SPEC_CH, 1) + odd[:, PAIR:]
        grad[part * SPEC_CH : (part + 1) * SPEC_CH, :] = jnp.where(lane, real, imag)


def mix_terms(block, spec, forward, twiddle, wide):
    return pl.pallas_call(
        mix_kernel,
        grid=(1,),
        in_specs=[
            pl.BlockSpec((1024, 512), lambda i: (0, 1)),
            whole_spec((16, GROUPS, 256)),
            whole_spec((256, 256)),
            whole_spec((2, GROUPS, 512)),
            whole_spec((256, 256)),
        ],
        out_specs=whole_spec((128, 128)),
        out_shape=jax.ShapeDtypeStruct((128, 128), F32),
        scratch_shapes=[
            pltpu.VMEM((4, 1024, PAIR), F32),
            pltpu.VMEM((256, 512), F32),
            pltpu.VMEM((512, 256), F32),
            pltpu.VMEM((512, 256), BF16),
            pltpu.VMEM((256, 256), F32),
        ],
        compiler_params=params(),
        cost_estimate=cost(6 * 10**9, 5 * 2**20),
    )(block, spec, forward, twiddle, wide)


def back_kernel(
    table, block, inner, cot, mix_part, ready, summed_out, terms_out,
    held, inners, cots, mix, summed, terms, packed, parts, sems, out_sems,
):
    del ready

    def load(source, target, sem):
        copy = pltpu.make_async_copy(source, target, sems.at[sem])
        copy.start()
        return copy

    first = load(table, held, 0)
    second = load(inner, inners, 1)
    pairs = [load(cot.at[0, pl.ds(2 * p, 2)], cots.at[p], 2 + p) for p in range(4)]
    last = load(mix_part, mix, 6)
    first.wait()
    for b in range(4):
        parts[b] = dot(held[b], block[b * 256 : (b + 1) * 256, :])
    second.wait()
    acc = jnp.zeros((PAIR, 256), F32)
    for p in range(4):
        lanes = slice(p * PAIR, (p + 1) * PAIR)

        @pl.loop(0, 128, step=RB, unroll=True)
        def _(rows):
            rows = pl.multiple_of(rows, RB)
            u = [
                [parts[b, pl.ds(128 * i + rows, RB), lanes] for i in range(2)] for b in range(4)
            ]
            for r, x in enumerate(eight_back(u)):
                at = pl.ds(128 * r + rows, RB)
                summed[at, lanes] = (x + inners[at, lanes].astype(F32)).astype(BF16)

        pairs[p].wait()
        pair = jnp.concatenate([cots[p, 0], cots[p, 1]], axis=1)
        acc = acc + dot_t(summed[:, lanes], pair)
    store = pltpu.make_async_copy(summed, summed_out, out_sems.at[0])
    store.start()
    last.wait()
    out_part = acc[0:SPEC_CH, 0:128] + acc[SPEC_CH:, 128:]
    high = out_part.astype(BF16).astype(F32)
    out_both = jnp.concatenate([high, out_part - high], axis=0).T
    for img in range(2):
        terms[pl.ds(2 * img, 128, stride=4), :] = mix[...]
        terms[pl.ds(2 * img + 1, 128, stride=4), :] = out_both
    packed[...] = terms[...].astype(BF16)
    copy = pltpu.make_async_copy(packed, terms_out, out_sems.at[1])
    copy.start()
    store.wait()
    copy.wait()


def back_rows(table, rows, inner, cot, mix_part, ready):
    return pl.pallas_call(
        back_kernel,
        in_specs=[ANY, VMEM, ANY, ANY, ANY, ANY],
        out_specs=[ANY, ANY],
        out_shape=[
            pltpu.HBM((WIDTH, 512), BF16),
            pltpu.HBM((512, 128), BF16),
        ],
        scratch_shapes=[
            pltpu.VMEM((4, 256, 256), BF16),
            pltpu.VMEM((WIDTH, 512), BF16),
            pltpu.VMEM((4, 2, WIDTH, 128), BF16),
            pltpu.VMEM((128, 128), F32),
            pltpu.VMEM((WIDTH, 512), BF16),
            pltpu.VMEM((512, 128), F32),
            pltpu.VMEM((512, 128), BF16),
            pltpu.VMEM((4, 256, 512), F32),
            pltpu.SemaphoreType.DMA((7,)),
            pltpu.SemaphoreType.DMA((2,)),
        ],
        compiler_params=params(SMALL),
        cost_estimate=cost(2 * 10**9, 8 * 2**20),
    )(in_hbm(table), rows, in_hbm(inner), in_hbm(cot), in_hbm(mix_part), in_hbm(ready))


def out_kernel(summed, out_w, out, held, wide, result, sems, out_sems):
    loads = []
    for p in range(4):
        lanes = pl.ds(p * PAIR, PAIR)
        loads.append(pltpu.make_async_copy(summed.at[:, lanes], held.at[p], sems.at[p]))
        loads[p].start()
    zero = jnp.zeros((SPEC_CH, 128), BF16)
    wide[0:SPEC_CH, :] = jnp.concatenate([out_w[...], zero], axis=1)
    wide[SPEC_CH:, :] = jnp.concatenate([zero, out_w[...]], axis=1)
    stores = []
    for copy in loads:
        copy.wait()
    for p in range(4):
        prod = dot(held[p], wide[...])
        result[2 * p] = prod[:, 0:128].astype(BF16)
        result[2 * p + 1] = prod[:, 128:].astype(BF16)
        rows = pl.ds(2 * p, 2)
        stores.append(pltpu.make_async_copy(result.at[rows], out.at[0, rows], out_sems.at[p]))
        stores[p].start()
    for copy in stores:
        copy.wait()


def project_out(summed, out_w):
    return pl.pallas_call(
        out_kernel,
        grid=(1,),
        in_specs=[ANY, whole_spec((SPEC_CH, 128))],
        out_specs=ANY,
        out_shape=pltpu.HBM((1, ROWS, WIDTH, 128), BF16),
        scratch_shapes=[
            pltpu.VMEM((4, WIDTH, PAIR), BF16),
            pltpu.VMEM((128, 256), BF16),
            pltpu.VMEM((ROWS, WIDTH, 128), BF16),
            pltpu.SemaphoreType.DMA((4,)),
            pltpu.SemaphoreType.DMA((4,)),
        ],
        compiler_params=params(),
        cost_estimate=cost(5 * 10**8, 3 * 2**20),
    )(summed, out_w)


def fill_wide(weight, wide, sums):
    for a in range(3):
        for b in range(3):
            wide[a * 128 : (a + 1) * 128, b * 128 : (b + 1) * 128] = weight[a, b]
    sums[0, 0:8] = jnp.zeros((8, 128), F32)
    sums[2, WIDTH + 8 :] = jnp.zeros((8, 128), F32)


def conv_sums(top, mid, bottom, sums, wide):
    prod = dot(jnp.concatenate([top, mid, bottom], axis=1), wide[...])
    for b in range(3):
        sums[b, 8 : WIDTH + 8] = prod[:, b * 128 : (b + 1) * 128]
    total = sums[0, 7 : WIDTH + 7] + sums[1, 8 : WIDTH + 8] + sums[2, 9 : WIDTH + 9]
    return total.astype(BF16)


def conv_row(top, mid, bottom, weight, out, sums, wide):
    @pl.when(pl.program_id(0) == 0)
    def _():
        fill_wide(weight, wide, sums)

    out[0, 0] = conv_sums(top, mid, bottom, sums, wide)


def inner_kernel(above, mid, below, weight, mix_w, ready, out, mix, sums, wide):
    del ready
    conv_row(above[0, 0], mid[0, 0], below[0, 0], weight, out, sums, wide)

    @pl.when(pl.program_id(0) == 0)
    def _():
        fill_mix(mix_w, mix)


def edge_kernel(
    mid, beside, edge_above, edge_below, weight, done, ready, out, token, sums, wide
):
    del done, ready
    token[...] = jnp.zeros((8, 128), F32)
    first = pl.program_id(0) == 0
    top = jnp.where(first, edge_above[0, 0], beside[0, 0])
    bottom = jnp.where(first, beside[0, 0], edge_below[0, 0])
    conv_row(top, mid[0, 0], bottom, weight, out, sums, wide)


def sum_kernel(terms, mix, out):
    total = jnp.sum(terms[...].astype(F32).reshape(64, 8, 128), axis=0)
    even = iota((8, 128), 0) % 2 == 0
    mix[...] = jnp.sum(jnp.where(even, total, 0.0), axis=0, keepdims=True)
    odd = jnp.sum(jnp.where(even, 0.0, total), axis=0, keepdims=True)
    out[...] = odd[:, 0:SPEC_CH] + odd[:, SPEC_CH:]


def sum_terms(terms):
    return pl.pallas_call(
        sum_kernel,
        in_specs=[VMEM],
        out_specs=[VMEM, VMEM],
        out_shape=[
            jax.ShapeDtypeStruct((1, 128), F32),
            jax.ShapeDtypeStruct((1, SPEC_CH), F32),
        ],
        compiler_params=params(SMALL),
        cost_estimate=cost(10**6, 2**17),
    )(terms)


def row_spec(index):
    return pl.BlockSpec((1, 1, WIDTH, 128), lambda i: (0, index(i), 0, 0))


def conv_call(kernel, rows, in_specs, out_index, second, aliases, args):
    return pl.pallas_call(
        kernel,
        grid=(rows,),
        in_specs=in_specs,
        out_specs=[row_spec(out_index), whole_spec(second.shape)],
        out_shape=[
            pltpu.HBM((1, ROWS, WIDTH, 128), BF16),
            second,
        ],
        scratch_shapes=[pltpu.VMEM((3, WIDTH + 16, 128), F32), pltpu.VMEM((384, 384), BF16)],
        input_output_aliases=aliases,
        compiler_params=params(),
        cost_estimate=cost(rows * 10**9, rows * 2**20),
    )(*args)


def inner_rows(cells, weight, mix_w, ready):
    specs = [
        row_spec(lambda i: i),
        row_spec(lambda i: i + 1),
        row_spec(lambda i: i + 2),
        whole_spec((3, 3, 128, 128)),
        whole_spec((128, 128)),
        pl.BlockSpec(memory_space=pl.ANY),
    ]
    args = (cells, cells, cells, weight, mix_w, ready)
    second = jax.ShapeDtypeStruct((256, 256), BF16)
    return conv_call(inner_kernel, ROWS - 2, specs, lambda i: i + 1, second, {}, args)


BLOCK = 8


def neighbour_rows(cells):
    head, tail = cells[:, 0:1], cells[:, ROWS - 1 :]
    near = [i for i in range(GROUPS - 1) if i % BLOCK != BLOCK - 1]
    above = lax.ppermute(tail, "rows", [(i, i + 1) for i in near])
    below = lax.ppermute(head, "rows", [(i + 1, i) for i in near])
    return above, below


def far_row(cells):
    last = lax.axis_index("rows") % BLOCK == BLOCK - 1
    row = lax.dynamic_slice_in_dim(cells, jnp.where(last, ROWS - 1, 0), 1, axis=1)
    far = range(BLOCK - 1, GROUPS - 1, BLOCK)
    return lax.ppermute(row, "rows", [(i, i + 1) for i in far] + [(i + 1, i) for i in far])


def edge_rows(cells, above, below, weight, done, ready):
    specs = [
        row_spec(lambda i: i * (ROWS - 1)),
        row_spec(lambda i: 1 + i * (ROWS - 3)),
        whole_spec((1, 1, WIDTH, 128)),
        whole_spec((1, 1, WIDTH, 128)),
        whole_spec((3, 3, 128, 128)),
        pl.BlockSpec(memory_space=pl.ANY),
        pl.BlockSpec(memory_space=pl.ANY),
    ]
    args = (cells, cells, above, below, weight, done, ready)
    second = jax.ShapeDtypeStruct((8, 128), F32)
    return conv_call(edge_kernel, 2, specs, lambda i: i * (ROWS - 1), second, {5: 0}, args)


def far_kernel(cells, above, far, weight_in, done, ready, out, lines, weight, row_out, sums, wide, sems):
    del done, ready
    at = lax.axis_index("rows") % BLOCK
    last = at == BLOCK - 1
    row = jnp.where(last, ROWS - 1, 0)
    beside = jnp.where(last, ROWS - 2, 1)
    outer = jnp.where(last, 2, 0)
    weights = pltpu.make_async_copy(weight_in, weight, sems.at[0])
    weights.start()
    own = pltpu.make_async_copy(cells.at[0, row], lines.at[1], sems.at[1])
    own.start()
    inside = pltpu.make_async_copy(cells.at[0, beside], lines.at[2 - outer], sems.at[2])
    inside.start()

    @pl.when((at == 0) | last)
    def _():
        pltpu.make_async_copy(far.at[0, 0], lines.at[outer], sems.at[3]).start()

    @pl.when((at > 0) & (at < BLOCK - 1))
    def _():
        pltpu.make_async_copy(above.at[0, 0], lines.at[outer], sems.at[3]).start()

    weights.wait()
    fill_wide(weight, wide, sums)
    own.wait()
    inside.wait()
    pltpu.make_async_copy(above.at[0, 0], lines.at[outer], sems.at[3]).wait()
    row_out[...] = conv_sums(lines[0], lines[1], lines[2], sums, wide)
    copy = pltpu.make_async_copy(row_out, out.at[0, row], sems.at[4])
    copy.start()
    copy.wait()


def far_edge(cells, above, far, weight, done, ready):
    return pl.pallas_call(
        far_kernel,
        in_specs=[ANY] * 6,
        out_specs=ANY,
        out_shape=pltpu.HBM((1, ROWS, WIDTH, 128), BF16),
        scratch_shapes=[
            pltpu.VMEM((3, WIDTH, 128), BF16),
            pltpu.VMEM((3, 3, 128, 128), BF16),
            pltpu.VMEM((WIDTH, 128), BF16),
            pltpu.VMEM((3, WIDTH + 16, 128), F32),
            pltpu.VMEM((384, 384), BF16),
            pltpu.SemaphoreType.DMA((5,)),
        ],
        input_output_aliases={4: 0},
        compiler_params=params(SMALL),
        cost_estimate=cost(10**9, 2**20),
    )(in_hbm(cells), in_hbm(above), far, in_hbm(weight), in_hbm(done), in_hbm(ready))


def exchange(block):
    lanes = block.shape[1]
    moved = lax.all_to_all(
        block.reshape(GROUPS, ROWS, lanes), "rows", split_axis=0, concat_axis=0, tiled=True
    )
    return moved.reshape(GROUPS * ROWS, lanes)


def shards(local_maps, global_maps, conv_weight, in_weight, mix_weight, out_weight, out_cotangent):
    row_fwd, row_inv = row_tables()
    forward, backward, twiddle = column_tables()
    spec_rows, inner = rows_forward(global_maps, out_cotangent, in_weight.T, out_weight, row_fwd)
    spec_cols = exchange(spec_rows)
    local_inner, wide = inner_rows(local_maps, conv_weight, mix_weight, spec_rows)
    above, below = neighbour_rows(local_maps)
    spectrum, back_cols = columns(
        spec_cols, forward, backward, twiddle, wide, above, below
    )
    back = exchange(back_cols)
    mix_part = mix_terms(spec_cols, spectrum, forward, twiddle, wide)
    local_out, token = edge_rows(local_maps, above, below, conv_weight, local_inner, back_cols)
    summed, terms = back_rows(row_inv, back, inner, out_cotangent, mix_part, token)
    local_out = far_edge(
        local_maps, above, far_row(local_maps), conv_weight, local_out, in_hbm(terms)
    )
    terms = terms.reshape(256, 2, 128)
    terms = lax.all_to_all(terms, ("rows", "img"), split_axis=0, concat_axis=0, tiled=True)
    global_out = project_out(summed, out_weight)
    mix_grad, out_grad = sum_terms(terms.reshape(512, 128))
    mix_grad, out_grad = mix_grad.reshape(128, 1), out_grad.reshape(SPEC_CH, 1)
    return (local_out, global_out, mix_grad, out_grad)


def solution(mesh):
    maps = P("img", "rows", None, None)
    in_specs = (maps, maps, P(), P(), P(), P(), maps)
    out_specs = (maps, maps, P(None, "rows"), P(None, "rows"))
    return jax.shard_map(shards, mesh=mesh, in_specs=in_specs, out_specs=out_specs, check_vma=False)
```
